32 devices in a mesh: wide: 8 (over y, x, core), narrow: 4 (over z).
Axes of the slice: x: 2, y: 2, z: 4, core: 2. Of those that a mesh axis runs over, the one named last changes fastest.
Arguments:
- images: bfloat16 [3, 1024000], P(None, ('wide', 'narrow')), may hold values from -6 to 6
- large_flag: int32 [640], P(('wide', 'narrow')), may hold values from 0 to 1
- labels: int32 [640], P(('wide', 'narrow')), may hold values from 0 to 9
- example_weights: int32 [640], P(('wide', 'narrow')), may hold values from 1 to 6
- cycle_noise: int32 [8, 7, 28056], P('wide'), may hold values from 0 to 65535
- stem_weight: float32 [64, 27], P('wide'), may hold values from -1.25 to 1.25
- conv_weight: float32 [6, 64, 576], P(None, 'wide'), may hold values from -0.25 to 0.25
- norm_params: float32 [2, 7, 64], P(None, None, 'wide'), as said below
- head_weight: float32 [10, 64], P(None, 'wide'), may hold values from -3 to 3
- head_bias: float32 [10], replicated, may hold values from -3 to 3
- stem_first: float32 [64, 27], P('wide'), may hold values from -6.67572e-06 to 6.67572e-06
- stem_second: float32 [64, 27], P('wide'), may hold values from 1.7820706e-14 to 7.1282823e-14
- conv_first: float32 [6, 64, 576], P(None, 'wide'), may hold values from -6.67572e-06 to 6.67572e-06
- conv_second: float32 [6, 64, 576], P(None, 'wide'), may hold values from 1.7820706e-14 to 7.1282823e-14
- norm_first: float32 [2, 7, 64], P(None, None, 'wide'), may hold values from -6.67572e-06 to 6.67572e-06
- norm_second: float32 [2, 7, 64], P(None, None, 'wide'), may hold values from 1.7820706e-14 to 7.1282823e-14
- head_first: float32 [10, 64], P(None, 'wide'), may hold values from -6.67572e-06 to 6.67572e-06
- head_second: float32 [10, 64], P(None, 'wide'), may hold values from 1.7820706e-14 to 7.1282823e-14
- bias_first: float32 [10], replicated, may hold values from -6.67572e-06 to 6.67572e-06
- bias_second: float32 [10], replicated, may hold values from 1.7820706e-14 to 7.1282823e-14
Outputs:
- stem_new: float32 [64, 27], P('wide')
- stem_first_new: float32 [64, 27], P('wide')
- stem_second_new: float32 [64, 27], P('wide')
- conv_new: float32 [6, 64, 576], P(None, 'wide')
- conv_first_new: float32 [6, 64, 576], P(None, 'wide')
- conv_second_new: float32 [6, 64, 576], P(None, 'wide')
- norm_new: float32 [2, 7, 64], P(None, None, 'wide')
- norm_first_new: float32 [2, 7, 64], P(None, None, 'wide')
- norm_second_new: float32 [2, 7, 64], P(None, None, 'wide')
- head_new: float32 [10, 64], P(None, 'wide')
- head_first_new: float32 [10, 64], P(None, 'wide')
- head_second_new: float32 [10, 64], P(None, 'wide')
- bias_new: float32 [10], replicated
- bias_first_new: float32 [10], replicated
- bias_second_new: float32 [10], replicated
- grad_norm: float32 [], replicated
- loss_sum: float32 [], replicated
- weight_total: float32 [], replicated
The draws below stay inside these ranges and needn't reach their ends.
Inputs may be any that keep to these rules, and one draw needn't show every extreme that they name: `norm_params`: gains of the batch norms in row 0 are positive.
All inputs are finite; a program needn't handle non-finite values. Where the reference program divides by a largest or mean magnitude, that divisor is 1e-20 or more.
Results may differ from the reference program's by a relative error of at most 0.025.
Values may be sent and summed in bfloat16 or wider, within the bound.
No kernel may reach another device: no remote copies, remote signals or barrier semaphores. Data moves between devices by JAX's collectives and lax.ppermute only.
A program may use at most 960 MiB of HBM per device.

```python
import math
import jax
import jax.numpy as jnp
import numpy as np
from jax import lax

C = 64
CLASSES = 10
SIDE = 40
SHORT = 32
STEP = 10
IMAGES = 640
PARAMS = 224458
SHARE = 28056
N_WIDE = 8


def draw_large_flag(key, part):
    key = jax.random.fold_in(key, 11)
    index = jnp.arange(IMAGES, dtype=jnp.int32)
    level = jax.random.randint(key, (IMAGES,), 0, 4, dtype=jnp.int32)
    flags = (level < 1 + 2 * index // IMAGES).astype(jnp.int32)
    return flags.at[0].set(0).at[IMAGES - 1].set(1)


def draw_example_weights(key, part):
    key = jax.random.fold_in(key, 12)
    index = jnp.arange(IMAGES, dtype=jnp.int32)
    upper = 2 + 6 * index // IMAGES
    values = jax.random.randint(key, (IMAGES,), 1, upper, dtype=jnp.int32)
    return values.at[0].set(1).at[IMAGES - 1].set(6)


def draw_norm_params(key, part):
    key = jax.random.fold_in(key, 13)
    gain_key, shift_key = jax.random.split(key)
    gains = jax.random.uniform(gain_key, (7, C), jnp.float32, 0.5, 1.5)
    shifts = 0.3 * jax.random.normal(shift_key, (7, C), jnp.float32)
    return jnp.stack([gains, shifts], 0)


def place_ends(entries, key, smallest, high):
    longest = entries.shape.index(max(entries.shape))
    spots = []
    for shift in (0, 1):
        where = [jax.random.randint(jax.random.fold_in(key, axis), (), 0, length) for axis, length in enumerate(entries.shape)]
        where[longest] = (where[longest] + shift) % entries.shape[longest]
        spots.append(tuple(where))
    return entries.at[spots[0]].set(smallest).at[spots[1]].set(high)


def shard_levels(key, extent, shards, least, high):
    level, own = 1.0, jax.random.fold_in(key, 6)
    for axis_at, shards_of in shards:
        draws = jnp.exp(jax.random.uniform(jax.random.fold_in(own, axis_at), (shards_of,), jnp.float32, least / len(shards), high / len(shards)))
        level = level * jnp.repeat(draws, extent[axis_at] // shards_of).reshape([-1 if axis == axis_at else 1 for axis in range(len(extent))])
    return level


def rank_table(amount, skew):
    weights = [(1 << 20) // math.isqrt(grade ** skew) + 1 for grade in range(1, amount + 1)]
    deviation = 1 + sum(weights) // (1 << 30)
    return np.cumsum(np.array([max(1, weight // deviation) for weight in weights]))


def ranked_ids(key, extent, number_of, skew):
    listing = rank_table(number_of, skew)
    lot = jax.random.randint(jax.random.fold_in(key, 1), extent, 0, int(listing[number_of - 1]))
    grade = jnp.searchsorted(jnp.asarray(listing, jnp.int32), lot, side="right")
    return jax.random.permutation(jax.random.fold_in(key, 2), number_of)[grade].astype(jnp.int32)


def gaussian(rng, dims, scale, most, cuts=(), held_as=jnp.bfloat16):
    array = scale * jax.random.normal(rng, dims, jnp.float32)
    if cuts:
        array = array * shard_levels(rng, dims, cuts, -0.22, 0.18)
    return jnp.clip(array, -most, most).astype(held_as)


def setup_inputs(seed: int = 0) -> dict:
    splits = jax.random.split(jax.random.key(seed), 21)
    return {
        "images": gaussian(splits[0], (3, IMAGES * SIDE * SIDE), 1.0, 6.0, ((1, 32),)),
        "large_flag": draw_large_flag(jax.random.fold_in(splits[20], 71), 0),
        "labels": place_ends(ranked_ids(splits[2], (IMAGES,), CLASSES, 2), jax.random.fold_in(splits[2], 3), 0, CLASSES - 1).astype(jnp.int32),
        "example_weights": draw_example_weights(jax.random.fold_in(splits[20], 71), 0),
        "cycle_noise": place_ends(jax.random.randint(splits[4], (N_WIDE, N_WIDE - 1, SHARE), 0, 65536), jax.random.fold_in(splits[4], 1), 0, 65535).astype(jnp.int32),
        "stem_weight": gaussian(splits[5], (C, 27), 27 ** -0.5, 1.25, ((0, 8),), jnp.float32),
        "conv_weight": gaussian(splits[6], (6, C, 9 * C), (9 * C) ** -0.5, 0.25, ((1, 8),), jnp.float32),
        "norm_params": draw_norm_params(jax.random.fold_in(splits[20], 71), 0),
        "head_weight": gaussian(splits[8], (CLASSES, C), (C // 16) ** -0.5, 3.0, ((1, 8),), jnp.float32),
        "head_bias": gaussian(splits[9], (CLASSES,), 0.5, 3.0, (), jnp.float32),
        "stem_first": gaussian(splits[10], (C, 27), (0.00022 * PARAMS ** -0.5), 6.67572021484375e-06, ((0, 8),), jnp.float32),
        "stem_second": jnp.clip(jnp.exp(math.log(7.128282339396996e-14) - 1.3862944 * jax.random.uniform(splits[11], (C, 27), jnp.float32) ** shard_levels(splits[11], (C, 27), ((0, 8),), -0.2, 0.2)), 1.782070584849249e-14, 7.128282339396996e-14),
        "conv_first": gaussian(splits[12], (6, C, 9 * C), (0.00022 * PARAMS ** -0.5), 6.67572021484375e-06, ((1, 8),), jnp.float32),
        "conv_second": jnp.clip(jnp.exp(math.log(7.128282339396996e-14) - 1.3862944 * jax.random.uniform(splits[13], (6, C, 9 * C), jnp.float32) ** shard_levels(splits[13], (6, C, 9 * C), ((1, 8),), -0.2, 0.2)), 1.782070584849249e-14, 7.128282339396996e-14),
        "norm_first": gaussian(splits[14], (2, 7, C), (0.00022 * PARAMS ** -0.5), 6.67572021484375e-06, ((2, 8),), jnp.float32),
        "norm_second": jnp.clip(jnp.exp(math.log(7.128282339396996e-14) - 1.3862944 * jax.random.uniform(splits[15], (2, 7, C), jnp.float32) ** shard_levels(splits[15], (2, 7, C), ((2, 8),), -0.2, 0.2)), 1.782070584849249e-14, 7.128282339396996e-14),
        "head_first": gaussian(splits[16], (CLASSES, C), (0.00022 * PARAMS ** -0.5), 6.67572021484375e-06, ((1, 8),), jnp.float32),
        "head_second": jnp.clip(jnp.exp(math.log(7.128282339396996e-14) - 1.3862944 * jax.random.uniform(splits[17], (CLASSES, C), jnp.float32) ** shard_levels(splits[17], (CLASSES, C), ((1, 8),), -0.2, 0.2)), 1.782070584849249e-14, 7.128282339396996e-14),
        "bias_first": gaussian(splits[18], (CLASSES,), (0.00022 * PARAMS ** -0.5), 6.67572021484375e-06, (), jnp.float32),
        "bias_second": jnp.clip(jnp.exp(jax.random.uniform(splits[19], (CLASSES,), jnp.float32, math.log(1.782070584849249e-14), math.log(7.128282339396996e-14))), 1.782070584849249e-14, 7.128282339396996e-14),
    }


@jax.custom_vjp
def low(v):
    return lax.optimization_barrier(v.astype(jnp.bfloat16)).astype(jnp.float32)

@jax.custom_vjp
def low_back(v):
    return v

def low_keep(v):
    return (low(v), None)

def low_pass(kept, grad):
    return (grad,)

def back_keep(v):
    return (v, None)

def back_low(kept, grad):
    return (low(grad),)
low.defvjp(low_keep, low_pass)
low_back.defvjp(back_keep, back_low)
norm_epsilon = 1e-05
clip_limit = 0.002
learn_rate = 0.4
first_decay = 0.9
second_decay = 0.999
adam_epsilon = 1e-08
weight_decay = 0.0005
decoupled = 0.01
levels = 15.0
highest = lax.Precision.HIGHEST

def convolve(field, matrix, inputs):
    outputs = matrix.shape[0]
    kernel = matrix.reshape(outputs, 3, 3, inputs).transpose(0, 3, 1, 2)
    return lax.conv_general_dilated(field, kernel, (1, 1), ((1, 1), (1, 1)), dimension_numbers=('NCHW', 'OIHW', 'NCHW'), precision=highest)
group_conv = jax.vmap(convolve, in_axes=(0, 0, None))

def batch_norm(conv_out, gain, shift, pixel_mask, pixel_total):
    masked = conv_out * pixel_mask
    mean = lax.optimization_barrier(jnp.sum(masked, axis=(0, 1, 3, 4))) / pixel_total
    square = lax.optimization_barrier(jnp.sum(masked * conv_out, axis=(0, 1, 3, 4))) / pixel_total
    scale = lax.rsqrt(square - mean * mean + norm_epsilon)
    normed = (conv_out - mean[None, None, :, None, None]) * scale[None, None, :, None, None]
    return normed * gain[:, None, :, None, None] + shift[:, None, :, None, None]

def block(stream, first_matrix, second_matrix, gains, shifts, pixel_mask, pixel_total):
    channels = stream.shape[2]
    first = low_back(group_conv(low(stream), low(first_matrix), channels))
    hidden = jax.nn.silu(batch_norm(first, gains[:, 0], shifts[:, 0], pixel_mask, pixel_total)) * pixel_mask
    second = low_back(group_conv(low(hidden), low(second_matrix), channels))
    return jax.nn.silu(batch_norm(second, gains[:, 1], shifts[:, 1], pixel_mask, pixel_total) + stream) * pixel_mask

def forward(params, images_f, pixel_mask, pixel_total, pixel_counts, onehot, weights_f, weight_total):
    stem_weight, conv_weight, norm_params, head_weight, head_bias = params
    stem = low_back(group_conv(images_f, low(stem_weight), 3))
    stream = jax.nn.silu(batch_norm(stem, norm_params[:, 0, 0], norm_params[:, 1, 0], pixel_mask, pixel_total)) * pixel_mask
    for index in range(3):
        stream = jax.checkpoint(block)(stream, conv_weight[:, 2 * index], conv_weight[:, 2 * index + 1], norm_params[:, 0, 1 + 2 * index:3 + 2 * index], norm_params[:, 1, 1 + 2 * index:3 + 2 * index], pixel_mask, pixel_total)
    pooled = lax.optimization_barrier(jnp.sum(stream, axis=(3, 4))) / pixel_counts[:, :, None]
    logits = low_back(jnp.einsum('gbc,gkc->gbk', low(pooled), low(head_weight), precision=highest) + head_bias[None, None, :])
    log_probs = jax.nn.log_softmax(logits, axis=2)
    losses = -lax.optimization_barrier(jnp.sum(onehot * log_probs, axis=2))
    loss_sum = jnp.sum(weights_f * losses)
    return (loss_sum / weight_total, loss_sum)

def flatten(stem, conv, norm, head):
    pieces = N_WIDE
    width = stem.shape[0] // pieces
    return jnp.concatenate([stem.reshape(pieces, -1), conv.reshape(6, pieces, width, -1).transpose(1, 0, 2, 3).reshape(pieces, -1), norm.reshape(2, 7, pieces, width).transpose(2, 0, 1, 3).reshape(pieces, -1), head.reshape(head.shape[0], pieces, width).transpose(1, 0, 2).reshape(pieces, -1)], 1)

def unflatten_all(shares):
    pieces = N_WIDE
    width = C // pieces
    first = width * 27
    second = first + 6 * width * 9 * C
    third = second + 14 * width
    stem = shares[:, :first].reshape(C, 27)
    conv = shares[:, first:second].reshape(pieces, 6, width, 9 * C).transpose(1, 0, 2, 3).reshape(6, C, 9 * C)
    norm = shares[:, second:third].reshape(pieces, 2, 7, width).transpose(1, 2, 0, 3).reshape(2, 7, C)
    head = shares[:, third:].reshape(pieces, CLASSES, width).transpose(1, 0, 2).reshape(CLASSES, C)
    return (stem, conv, norm, head)

def quantize(block_value, noise):
    scale = lax.optimization_barrier(jnp.max(jnp.abs(block_value), axis=-1, keepdims=True)) + 1e-06
    dither = (noise.astype(jnp.float32) + 0.5) / 65536.0 - 0.5
    return (block_value / scale * levels + dither, scale)

def adam_update(gradient, first, second, master, factor):
    clipped = gradient * factor
    new_first = first_decay * first + (1.0 - first_decay) * clipped
    new_second = second_decay * second + (1.0 - second_decay) * clipped * clipped
    corrected = new_first / (1.0 - first_decay ** STEP) / (jnp.sqrt(new_second / (1.0 - second_decay ** STEP)) + adam_epsilon)
    return (master - learn_rate * (corrected + decoupled * master), new_first, new_second)

def reference(images, large_flag, labels, example_weights, cycle_noise, stem_weight, conv_weight, norm_params, head_weight, head_bias, stem_first, stem_second, conv_first, conv_second, norm_first, norm_second, head_first, head_second, bias_first, bias_second):
    groups = N_WIDE
    per = IMAGES // groups
    sides = jnp.where(large_flag == 1, SIDE, SHORT).astype(jnp.int32)
    rows = jnp.arange(SIDE, dtype=jnp.int32)
    valid = (rows[None, :, None] < sides[:, None, None]) & (rows[None, None, :] < sides[:, None, None])
    pixel_mask = valid.astype(jnp.float32).reshape(groups, per, 1, SIDE, SIDE)
    pixel_total = jnp.sum(pixel_mask)
    pixel_counts = (sides * sides).astype(jnp.float32).reshape(groups, per)
    weights_f = example_weights.astype(jnp.float32).reshape(groups, per)
    weight_total = jnp.sum(weights_f)
    onehot = (labels[:, None] == jnp.arange(CLASSES, dtype=jnp.int32)[None, :]).astype(jnp.float32).reshape(groups, per, CLASSES)
    canvas = images.reshape(3, groups, per, SIDE, SIDE).transpose(1, 2, 0, 3, 4)
    images_f = canvas.astype(jnp.float32) * pixel_mask

    def objective(params):
        return forward(params, images_f, pixel_mask, pixel_total, pixel_counts, onehot, weights_f, weight_total)
    copies = tuple((jnp.broadcast_to(w[None], (groups,) + w.shape) for w in (stem_weight, conv_weight, norm_params, head_weight)))
    params = copies + (head_bias,)
    value, pullback, loss_sum = jax.vjp(objective, params, has_aux=True)
    grads = pullback(jnp.ones((), jnp.float32))[0]
    partials = jax.vmap(flatten)(grads[0], grads[1], grads[2], grads[3])
    span = jnp.arange(groups, dtype=jnp.int32)
    acc = partials[(span + 1) % groups, span]
    for hop in range(1, groups):
        level, scale = quantize(acc, cycle_noise[(span + hop) % groups, hop - 1])
        acc = low(level) * scale / levels + partials[(span + hop + 1) % groups, span]
    stem_g, conv_g, norm_g, head_g = unflatten_all(acc)
    stem_g = stem_g + weight_decay * stem_weight
    conv_g = conv_g + weight_decay * conv_weight
    head_g = head_g + weight_decay * head_weight
    full = (stem_g, conv_g, norm_g, head_g, grads[4])
    squares = sum((jnp.sum(grad * grad) for grad in full))
    grad_norm = jnp.sqrt(squares)
    factor = clip_limit / jnp.maximum(grad_norm, clip_limit)
    masters = (stem_weight, conv_weight, norm_params, head_weight, head_bias)
    firsts = (stem_first, conv_first, norm_first, head_first, bias_first)
    seconds = (stem_second, conv_second, norm_second, head_second, bias_second)
    results = [adam_update(full[index], firsts[index], seconds[index], masters[index], factor) for index in range(5)]
    return (results[0][0], results[0][1], results[0][2], results[1][0], results[1][1], results[1][2], results[2][0], results[2][1], results[2][2], results[3][0], results[3][1], results[3][2], results[4][0], results[4][1], results[4][2], grad_norm, loss_sum, weight_total)
```

```python
import functools

import jax
import jax.numpy as jnp
import numpy as np
from jax import lax
from jax.experimental import pallas as pl
from jax.experimental.pallas import tpu as pltpu
from jax.sharding import PartitionSpec as P

SIDE = 40
SHORT = 32
STEP = 10

norm_epsilon = 1e-05
clip_limit = 0.002
learn_rate = 0.4
first_decay = 0.9
second_decay = 0.999
adam_epsilon = 1e-08
weight_decay = 0.0005
decoupled = 0.01
levels = 15.0

QUARTERS = 4
PATCHES = SIDE // 2
NI = PATCHES // QUARTERS
NJ = PATCHES
SHORT_J = SHORT // 2
LANES = 256
UNROLL = 4
LAG = 2
VMEM_LIMIT = 52 * 2**20

f32 = jnp.float32
bf16 = jnp.bfloat16
BOTH = ("wide", "narrow")


def window_place(slot):
    group, sy, sx = slot // 4, (slot // 2) % 2, slot % 2
    wx = 1 + sx if group in (0, 2) else (3 if sx == 0 else 0)
    wy = 1 + sy if group in (0, 1) else (3 if sy == 0 else 0)
    return wy, wx


def tap_of(slot, out):
    wy, wx = window_place(slot)
    ky, kx = wy - out // 2, wx - out % 2
    if 0 <= ky < 3 and 0 <= kx < 3:
        return ky * 3 + kx
    return None


def whole():
    return pl.BlockSpec(memory_space=pltpu.VMEM)


def call(kernel, outs, scratch, args, name, cost=None):
    return pl.pallas_call(
        kernel,
        out_shape=outs,
        in_specs=[whole()] * len(args),
        out_specs=jax.tree.map(lambda _: whole(), outs),
        scratch_shapes=scratch,
        compiler_params=pltpu.CompilerParams(vmem_limit_bytes=VMEM_LIMIT),
        name=name,
        cost_estimate=cost,
    )(*args)


def field(rows):
    return jax.ShapeDtypeStruct((NI, NJ, rows, LANES), bf16)


def wide_pair(row):
    turned = pltpu.roll(row, 64, 1)
    lower = lax.broadcasted_iota(jnp.int32, row.shape, 1) < 64
    first = jnp.where(lower, row, turned)
    second = jnp.where(lower, turned, row)
    return jnp.concatenate([first, first], 1), jnp.concatenate([second, second], 1)


def folded(row):
    half = row[:, :128] + row[:, 128:]
    return half + pltpu.roll(half, 64, 1)


def message(first, second):
    lower = lax.broadcasted_iota(jnp.int32, (1, 128), 1) < 64
    return jnp.where(lower, folded(first), folded(second))


def totals(gathered):
    return wide_pair(jnp.sum(gathered[:, :128], 0, keepdims=True))


def norm_constants(gathered, counted, norm4, index):
    sums, squares = totals(gathered)
    mean = sums / counted
    scale = lax.rsqrt(squares / counted - mean * mean + norm_epsilon)
    gain = norm4[index : index + 1]
    slope = gain * scale
    return mean, scale, slope, norm4[7 + index : 8 + index] - mean * slope


def pixels_of(gathered_first):
    return jnp.sum(gathered_first[:, 128:129], 0, keepdims=True)


def twice(tile):
    return jnp.concatenate([tile, tile], 1)


def mask_row(J):
    return jnp.where(J < SHORT_J, 0, jnp.where(J < NJ, 1, 2))


def put_column(ring, slot, s, value, low, q_ref):
    rows = value.shape[0]
    ring[slot, s + 1] = low
    if s == 0:
        ring[slot, NI + 1, :, :128] = (pltpu.roll(value[:, :128], rows - 1, 0) * q_ref[0]).astype(
            bf16
        )
    if s == NI - 1:
        ring[slot, 0, :, 128:] = (pltpu.roll(value[:, 128:], 1, 0) * q_ref[1]).astype(bf16)


def side_columns(ring, side, u, lanes):
    for s in range(NI + 2):
        if s == 0:
            side[u, s, :, 128:] = jnp.where(
                lanes[:, 128:], ring[u + 2, s, :, 128:], ring[u, s, :, 128:]
            )
        elif s == NI + 1:
            side[u, s, :, :128] = jnp.where(
                lanes[:, :128], ring[u + 2, s, :, :128], ring[u, s, :, :128]
            )
        else:
            side[u, s] = jnp.where(lanes, ring[u + 2, s], ring[u, s])


def operands(ring, side, u):
    rows = ring.shape[2]
    whole_rows = NI * rows
    last = NI + 2
    own = ring[u + 1, 1 : NI + 1].reshape(whole_rows, LANES)
    beside = side[u, 1 : NI + 1].reshape(whole_rows, LANES)
    above = jnp.concatenate(
        [ring[u + 1, 2:last, :, :128], ring[u + 1, 0:NI, :, 128:]], -1
    ).reshape(whole_rows, LANES)
    corner = jnp.concatenate([side[u, 2:last, :, :128], side[u, 0:NI, :, 128:]], -1).reshape(
        whole_rows, LANES
    )
    return own, beside, above, corner


def product(parts, w_ref):
    total = jnp.dot(parts[0], w_ref[0:LANES], preferred_element_type=f32)
    for k in range(1, 4):
        total += jnp.dot(
            parts[k], w_ref[k * LANES : (k + 1) * LANES], preferred_element_type=f32
        )
    return total


def by_eight(value):
    return jnp.sum(value.reshape(value.shape[0] // 8, 8, value.shape[1]), 0)


def half_lanes(rows):
    return lax.broadcasted_iota(jnp.int32, (rows, LANES), 1) % 128 < 64


def weights_kernel(conv_ref, forward_ref, backward_ref):
    for layer in range(6):
        matrix = conv_ref[layer].astype(f32)
        turned = matrix.T
        empty = jnp.zeros((64, 64), f32)
        for slot in range(16):
            ahead, back = [], []
            for out in range(4):
                tap = tap_of(slot, out)
                if tap is None:
                    ahead.append(empty)
                    back.append(empty)
                else:
                    other = 8 - tap
                    ahead.append(turned[tap * 64 : (tap + 1) * 64])
                    back.append(matrix[:, other * 64 : (other + 1) * 64])
            at = slice(slot * 64, (slot + 1) * 64)
            forward_ref[layer, at] = jnp.concatenate(ahead, 1).astype(bf16)
            backward_ref[layer, at] = jnp.concatenate(back, 1).astype(bf16)


def stem_kernel(planes_ref, w_ref, mask_ref, info_ref, out_ref, z_ref, stat_ref, zf, *, devices):
    rows = planes_ref.shape[1]
    zf[...] = jnp.zeros_like(zf)
    span = 2 * NI
    blocks = SIDE // span
    deep = (span + 2) * 4
    for i in range(3):
        turned = planes_ref[i].astype(f32).T
        for block in range(blocks):
            first = max(block * span - 1, 0)
            last = min(block * span + span + 1, SIDE)
            skip = first - (block * span - 1)
            for y in range(span):
                base = (block * (span + 2) + y + 1) * deep + skip * 4 + i
                zf[pl.ds(base, last - first, stride=4), :rows] = turned[
                    y * SIDE + first : y * SIDE + last
                ]
    lane = lax.broadcasted_iota(jnp.int32, (deep, 128), 1)
    for block in range(blocks):
        at = block * (span + 2) * deep
        low = zf[at + span * deep : at + (span + 1) * deep]
        zf[at : at + deep] = jnp.where(lane % 4 == 0, 0.0, pltpu.roll(low, 1, 1))
        high = zf[at + deep : at + 2 * deep]
        zf[at + (span + 1) * deep : at + (span + 2) * deep] = jnp.where(
            lane % 4 == 3, 0.0, pltpu.roll(high, 127, 1)
        )
    z_ref[...] = zf[...].astype(bf16)
    first_sum = jnp.zeros((8, LANES), f32)
    second_sum = jnp.zeros((8, LANES), f32)
    for block in range(blocks):
        for s in range(NI):
            at = (block * (span + 2) + 2 * s) * deep
            result = lax.dot_general(
                z_ref[at : at + 4 * deep],
                w_ref[...],
                (((0,), (0,)), ((), ())),
                preferred_element_type=f32,
            )
            for j in range(NI):
                J = block * NI + j
                mask = mask_ref[0 if J < SHORT_J else 1, 0 if s == 0 else 1]
                tile = result[:rows, j * LANES : (j + 1) * LANES] * twice(mask)
                out_ref[s, J] = tile.astype(bf16)
                first_sum += by_eight(tile)
                second_sum += by_eight(tile * tile)
    row = message(
        jnp.sum(first_sum, 0, keepdims=True), jnp.sum(second_sum, 0, keepdims=True)
    )
    counts = jnp.sum(info_ref[...], 0, keepdims=True) * (1.0 / QUARTERS)
    stat_ref[...] = jnp.broadcast_to(jnp.concatenate([row, counts], 1), (devices, LANES))


def forward_kernel(*refs, index, keep, residual, devices):
    refs = list(refs)
    c_ref = refs.pop(0)
    res_ref = refs.pop(0) if residual else None
    gath_ref, first_ref, norm_ref, mask_ref, q_ref, w_ref, out_ref = refs[:7]
    refs = refs[7:]
    keep_ref = refs.pop(0) if keep else None
    stat_ref, ring, side, sums = refs
    rows = c_ref.shape[2]
    counted = pixels_of(first_ref)
    _, _, slope, start = norm_constants(gath_ref, counted, norm_ref, index)
    half_slope, half_start = slope * 0.5, start * 0.5
    lanes = half_lanes(rows)
    sums[...] = jnp.zeros_like(sums)

    def activate(J, slot):
        Jc = jnp.minimum(J, NJ - 1)
        jm = mask_row(J)
        for s in range(NI):
            half = c_ref[s, Jc].astype(f32) * half_slope + half_start
            if residual:
                half = half + 0.5 * res_ref[s, Jc].astype(f32)
            mask = mask_ref[jm, 0 if s == 0 else 1]
            value = (half + half * jnp.tanh(half)) * twice(mask)
            low = value.astype(bf16)
            put_column(ring, slot, s, value, low, q_ref)
            if keep:
                @pl.when(J < NJ)
                def _():
                    keep_ref[s, Jc] = low

    def convolve(J, u):
        side_columns(ring, side, u, lanes)
        total = product(operands(ring, side, u), w_ref)
        jm = mask_row(J)
        first_sum, second_sum = sums[0], sums[1]
        for s in range(NI):
            tile = total[s * rows : (s + 1) * rows] * twice(mask_ref[jm, 0 if s == 0 else 1])
            out_ref[s, J] = tile.astype(bf16)
            first_sum += by_eight(tile)
            second_sum += by_eight(tile * tile)
        sums[0], sums[1] = first_sum, second_sum

    ring[UNROLL] = jnp.zeros(ring.shape[1:], bf16)
    for k in range(LAG):
        activate(k, UNROLL + 1 + k)

    def step(i, carry):
        for k in range(LAG + 1):
            ring[k] = ring[UNROLL + k]
        for u in range(UNROLL):
            activate(i * UNROLL + u + LAG, u + LAG + 1)
            convolve(i * UNROLL + u, u)
        return carry

    lax.fori_loop(0, NJ // UNROLL, step, 0)
    row = message(jnp.sum(sums[0], 0, keepdims=True), jnp.sum(sums[1], 0, keepdims=True))
    stat_ref[...] = jnp.broadcast_to(row, (devices, 128))


def head_kernel(
    c_ref, res_ref, gath_ref, first_ref, norm_ref, mask_ref, hot_ref, info_ref, into_ref, back_ref,
    bias_ref, dy_ref, stat_ref, head_ref, small_ref, grads, pool, *, classes, devices
):
    rows = c_ref.shape[2]
    counted = pixels_of(first_ref)
    weight_total = jnp.sum(first_ref[:, 129:130], 0, keepdims=True)
    mean, scale, slope, start = norm_constants(gath_ref, counted, norm_ref, 6)
    half_slope, half_start = slope * 0.5, start * 0.5
    pool[...] = jnp.zeros_like(pool)

    def gather(J, carry):
        jm = mask_row(J)
        total = pool[...]
        for s in range(NI):
            half = c_ref[s, J].astype(f32) * half_slope + half_start
            half = half + 0.5 * res_ref[s, J].astype(f32)
            mask = twice(mask_ref[jm, 0 if s == 0 else 1])
            t = jnp.tanh(half)
            total += (half + half * t) * mask
            grads[s, J] = (0.5 + 0.5 * t) * (1.0 + half * (1.0 - t)) * mask
        pool[...] = total
        return carry

    lax.fori_loop(0, NJ, gather, 0)
    pooled = pool[...]
    row_index = lax.broadcasted_iota(jnp.int32, (rows, LANES), 0)
    pooled = pooled + jnp.where(
        row_index % 2 == 0, pltpu.roll(pooled, rows - 1, 0), pltpu.roll(pooled, 1, 0)
    )
    pooled = pooled + jnp.where(
        row_index % 4 < 2, pltpu.roll(pooled, rows - 2, 0), pltpu.roll(pooled, 2, 0)
    )
    half_pool = pooled[:, :128] + pooled[:, 128:]
    half_pool = half_pool + pltpu.roll(half_pool, 64, 1)
    count = info_ref[:, 0:1]
    weight = info_ref[:, 1:2]
    pooled_low = (half_pool / count).astype(bf16)
    logits = jnp.dot(pooled_low, into_ref[...], preferred_element_type=f32) + bias_ref[...]
    lane = lax.broadcasted_iota(jnp.int32, logits.shape, 1)
    inside = lane < classes
    top = jnp.max(jnp.where(inside, logits, -jnp.inf), 1, keepdims=True)
    shifted = jnp.where(inside, logits - top, 0.0)
    powers = jnp.where(inside, jnp.exp(shifted), 0.0)
    sum_powers = jnp.sum(powers, 1, keepdims=True)
    hot = hot_ref[...]
    losses = jnp.log(sum_powers) - jnp.sum(hot * shifted, 1, keepdims=True)
    single = (lax.broadcasted_iota(jnp.int32, (rows, 1), 0) % QUARTERS == 0).astype(f32)
    loss = jnp.sum(losses * weight * single, 0, keepdims=True)
    grad_low = ((weight / weight_total) * (powers / sum_powers - hot)).astype(bf16)
    grad_once = grad_low * single.astype(bf16)
    bias_grad = jnp.sum(grad_once.astype(f32), 0, keepdims=True)
    head_ref[...] = lax.dot_general(
        grad_once, pooled_low, (((0,), (0,)), ((), ())), preferred_element_type=f32
    )
    small_ref[...] = jnp.concatenate([bias_grad, jnp.broadcast_to(loss, (1, 128))], 0)
    spread = jnp.dot(grad_low, back_ref[...], preferred_element_type=f32) / count

    def scatter(J, carry):
        first_sum, second_sum = carry
        for s in range(NI):
            dy = spread * grads[s, J]
            dy_ref[s, J] = dy.astype(bf16)
            first_sum += by_eight(dy)
            second_sum += by_eight(dy * c_ref[s, J].astype(f32))
        return first_sum, second_sum

    zero = jnp.zeros((8, LANES), f32)
    first_sum, second_sum = lax.fori_loop(0, NJ, scatter, (zero, zero))
    first_sum = jnp.sum(first_sum, 0, keepdims=True)
    second_sum = (jnp.sum(second_sum, 0, keepdims=True) - mean * first_sum) * scale
    stat_ref[...] = jnp.broadcast_to(message(first_sum, second_sum), (devices, 128))


def grad_constants(sums_ref, gath_ref, counted, norm4, index):
    first_total, second_total = totals(sums_ref)
    mean, scale, slope, _ = norm_constants(gath_ref, counted, norm4, index)
    along = -slope * scale * second_total / counted
    return slope, along, -slope * first_total / counted - along * mean


def backward_kernel(*refs, index, residual, adding, devices):
    refs = list(refs)
    dy_ref, c_ref, prev_ref = refs[:3]
    refs = refs[3:]
    res_ref = refs.pop(0) if residual else None
    add_ref = refs.pop(0) if adding else None
    (
        sums_ref, gath_ref, gath_prev_ref, first_ref, norm_ref, mask_ref, q_ref, w_ref,
        out_ref, grad_ref, stat_ref, ring, side, vring, vside, slopes, sums, acc,
    ) = refs
    rows = c_ref.shape[2]
    counted = pixels_of(first_ref)
    grad_slope, grad_along, grad_start = grad_constants(
        sums_ref, gath_ref, counted, norm_ref, index
    )
    mean, scale, slope, start = norm_constants(gath_prev_ref, counted, norm_ref, index - 1)
    half_slope, half_start = slope * 0.5, start * 0.5
    lanes = half_lanes(rows)
    sums[...] = jnp.zeros_like(sums)
    acc[...] = jnp.zeros_like(acc)

    def activate(J, slot):
        Jc = jnp.minimum(J, NJ - 1)
        jm = mask_row(J)
        for s in range(NI):
            mask = twice(mask_ref[jm, 0 if s == 0 else 1])
            grad = (
                dy_ref[s, Jc].astype(f32) * grad_slope
                + c_ref[s, Jc].astype(f32) * grad_along
                + grad_start
            ) * mask
            put_column(ring, slot, s, grad, grad.astype(bf16), q_ref)
            half = prev_ref[s, Jc].astype(f32) * half_slope + half_start
            if residual:
                half = half + 0.5 * res_ref[s, Jc].astype(f32)
            t = jnp.tanh(half)
            value = (half + half * t) * mask
            put_column(vring, slot, s, value, value.astype(bf16), q_ref)
            slopes[slot, s] = (0.5 + 0.5 * t) * (1.0 + half * (1.0 - t)) * mask

    def convolve(J, u):
        side_columns(ring, side, u, lanes)
        side_columns(vring, vside, u, lanes)
        total = product(operands(ring, side, u), w_ref)
        first_sum, second_sum = sums[0], sums[1]
        for s in range(NI):
            tile = total[s * rows : (s + 1) * rows]
            if adding:
                tile = tile + add_ref[s, J].astype(f32)
            tile = tile * slopes[u + 1, s]
            out_ref[s, J] = tile.astype(bf16)
            first_sum += by_eight(tile)
            second_sum += by_eight(tile * prev_ref[s, J].astype(f32))
        sums[0], sums[1] = first_sum, second_sum

    ring[UNROLL] = jnp.zeros(ring.shape[1:], bf16)
    vring[UNROLL] = jnp.zeros(ring.shape[1:], bf16)
    for k in range(LAG):
        activate(k, UNROLL + 1 + k)

    def step(i, carry):
        for k in range(LAG + 1):
            ring[k] = ring[UNROLL + k]
            vring[k] = vring[UNROLL + k]
            slopes[k] = slopes[UNROLL + k]
        for u in range(UNROLL):
            activate(i * UNROLL + u + LAG, u + LAG + 1)
            convolve(i * UNROLL + u, u)
        grad = ring[1 : UNROLL + 1, 1 : NI + 1].reshape(UNROLL * NI * rows, LANES)
        parts = [operands(vring, vside, u) for u in range(UNROLL)]
        for k in range(4):
            value = jnp.concatenate([parts[u][k] for u in range(UNROLL)], 0)
            acc[:, k * LANES : (k + 1) * LANES] += lax.dot_general(
                grad, value, (((0,), (0,)), ((), ())), preferred_element_type=f32
            )
        return carry

    lax.fori_loop(0, NJ // UNROLL, step, 0)
    taps = [None] * 9
    for slot in range(16):
        for out in range(4):
            tap = tap_of(slot, out)
            if tap is not None:
                piece = acc[out * 64 : (out + 1) * 64, slot * 64 : (slot + 1) * 64]
                taps[tap] = piece if taps[tap] is None else taps[tap] + piece
    grad_ref[...] = jnp.concatenate(taps, 1)
    first_sum = jnp.sum(sums[0], 0, keepdims=True)
    second_sum = (jnp.sum(sums[1], 0, keepdims=True) - mean * first_sum) * scale
    stat_ref[...] = jnp.broadcast_to(message(first_sum, second_sum), (devices, 128))


def stem_back_kernel(
    dy_ref, c_ref, z_ref, sums_ref, gath_ref, norm_ref, mask_ref, grad_ref
):
    rows = c_ref.shape[2]
    counted = pixels_of(gath_ref)
    slope, along, start = grad_constants(sums_ref, gath_ref, counted, norm_ref, 0)
    span = 2 * NI
    deep = (span + 2) * 4
    total = jnp.zeros((4 * deep, NI * LANES), f32)
    for block in range(SIDE // span):
        for s in range(NI):
            at = (block * (span + 2) + 2 * s) * deep
            pieces = []
            for j in range(NI):
                J = block * NI + j
                mask = twice(mask_ref[0 if J < SHORT_J else 1, 0 if s == 0 else 1])
                pieces.append(
                    (
                        (
                            dy_ref[s, J].astype(f32) * slope
                            + c_ref[s, J].astype(f32) * along
                            + start
                        )
                        * mask
                    ).astype(bf16)
                )
            total += jnp.dot(
                z_ref[at : at + 4 * deep][:, :rows],
                jnp.concatenate(pieces, 1),
                preferred_element_type=f32,
            )
    grad_ref[...] = total


def stem_table():
    span = 2 * NI + 2
    table = np.zeros((NI * 4, 4, span, 4, 27), np.float32)
    for j in range(NI):
        for out in range(4):
            for ky in range(3):
                for kx in range(3):
                    for i in range(3):
                        table[
                            j * 4 + out, out // 2 + ky, 2 * j + out % 2 + kx, i,
                            (ky * 3 + kx) * 3 + i,
                        ] = 1.0
    return table.reshape(NI * 4, 4 * span * 4, 27)


def passed_along(value, axis, by):
    count = lax.axis_size(axis)
    return lax.ppermute(value, axis, [(i, (i + by) % count) for i in range(count)])


def flatten(stem, conv, norm, head, pieces):
    width = stem.shape[0] // pieces
    return jnp.concatenate(
        [
            stem.reshape(pieces, -1),
            conv.reshape(6, pieces, width, -1).transpose(1, 0, 2, 3).reshape(pieces, -1),
            norm.reshape(2, 7, pieces, width).transpose(2, 0, 1, 3).reshape(pieces, -1),
            head.reshape(head.shape[0], pieces, width).transpose(1, 0, 2).reshape(pieces, -1),
        ],
        1,
    )


def unflatten_one(share, width, channels, classes):
    first = width * 27
    second = first + 6 * width * 9 * channels
    third = second + 14 * width
    return (
        share[:first].reshape(width, 27),
        share[first:second].reshape(6, width, 9 * channels),
        share[second:third].reshape(2, 7, width),
        share[third:].reshape(classes, width),
    )


def quantize(block_value, noise):
    scale = jnp.max(jnp.abs(block_value), axis=-1, keepdims=True) + 1e-06
    dither = (noise.astype(jnp.float32) + 0.5) / 65536.0 - 0.5
    return (block_value / scale * levels + dither, scale)


def adam_update(gradient, first, second, master, factor):
    clipped = gradient * factor
    new_first = first_decay * first + (1.0 - first_decay) * clipped
    new_second = second_decay * second + (1.0 - second_decay) * clipped * clipped
    corrected = (
        new_first
        / (1.0 - first_decay**STEP)
        / (jnp.sqrt(new_second / (1.0 - second_decay**STEP)) + adam_epsilon)
    )
    return (master - learn_rate * (corrected + decoupled * master), new_first, new_second)


def shared(rows):
    return lax.all_to_all(rows, BOTH, 0, 0, tiled=True)


def body(
    images,
    large_flag,
    labels,
    example_weights,
    cycle_noise,
    stem_weight,
    conv_weight,
    norm_params,
    head_weight,
    head_bias,
    stem_first,
    stem_second,
    conv_first,
    conv_second,
    norm_first,
    norm_second,
    head_first,
    head_second,
    bias_first,
    bias_second,
):
    wide_count = lax.axis_size("wide")
    devices = wide_count * lax.axis_size("narrow")
    count = large_flag.shape[0]
    rows = QUARTERS * count
    width = stem_weight.shape[0]
    channels = width * wide_count
    classes = head_weight.shape[0]
    assert channels == 64 and rows % 16 == 0 and rows <= 128

    conv_full = lax.all_gather(conv_weight.astype(bf16), "wide", axis=1, tiled=True)
    small = jnp.concatenate(
        [stem_weight, norm_params.reshape(14, width).T, head_weight.T], 1
    )
    small = lax.all_gather(small, "wide", axis=0, tiled=True)
    stem_low = small[:, :27].astype(bf16)
    norm4 = jnp.tile(small[:, 27:41].T, (1, 4))
    norm4 = jnp.pad(norm4, ((0, 2), (0, 0)))
    head_low = small[:, 41:].astype(bf16)
    into_head = jnp.pad(head_low, ((0, 64), (0, 128 - classes)))
    from_head = jnp.pad(jnp.tile(head_low.T, (1, 4)), ((0, 128 - classes), (0, 0)))
    bias_row = jnp.pad(head_bias[None, :], ((0, 0), (0, 128 - classes)))
    stem_wide = jnp.einsum(
        "krt,ot->rko", jnp.asarray(stem_table(), bf16), stem_low, preferred_element_type=f32
    ).astype(bf16).reshape(-1, NI * LANES)

    large = large_flag == 1
    row_large = jnp.repeat(large, QUARTERS)
    quarter = jnp.arange(rows, dtype=jnp.int32) % QUARTERS
    upper = row_large | (quarter < SHORT_J // NI)
    ones = jnp.ones((rows,), bool)
    none = jnp.zeros((rows,), bool)
    mask_table = jnp.stack(
        [jnp.stack([ones, upper]), jnp.stack([row_large, row_large]), jnp.stack([none, none])]
    )
    mask_table = jnp.broadcast_to(mask_table[..., None], (3, 2, rows, 128)).astype(f32)
    q_table = jnp.broadcast_to(
        jnp.stack([quarter != QUARTERS - 1, quarter != 0])[..., None], (2, rows, 128)
    ).astype(f32)
    sides = jnp.where(large, SIDE, SHORT).astype(jnp.int32)
    weights_f = example_weights.astype(f32)
    lane = jnp.arange(128, dtype=jnp.int32)[None, :]
    info = jnp.where(
        lane == 0,
        jnp.repeat((sides * sides).astype(f32), QUARTERS)[:, None],
        jnp.where(lane == 1, jnp.repeat(weights_f, QUARTERS)[:, None], 0.0),
    )
    hot = (jnp.repeat(labels, QUARTERS)[:, None] == lane).astype(f32)

    span = 2 * NI
    position = jnp.arange(span * SIDE, dtype=jnp.int32)
    inside = row_large[:, None] | (
        (quarter[:, None] * span + (position // SIDE)[None, :] < SHORT)
        & ((position % SIDE)[None, :] < SHORT)
    )
    planes = images.reshape(3, rows, span * SIDE) * inside.astype(bf16)[None]

    big = jax.ShapeDtypeStruct((6, 1024, LANES), bf16)
    ahead, back = call(weights_kernel, (big, big), [], (conv_full,), "weights")

    z_rows = (SIDE // span) * (span + 2) * (span + 2) * 4
    ring_shape = (UNROLL + 1 + LAG, NI + 2, rows, LANES)
    side_shape = (UNROLL, NI + 2, rows, LANES)
    stat = jax.ShapeDtypeStruct((devices, 128), f32)

    c0, z, stat0 = call(
        functools.partial(stem_kernel, devices=devices),
        (
            field(rows),
            jax.ShapeDtypeStruct((z_rows, 128), bf16),
            jax.ShapeDtypeStruct((devices, LANES), f32),
        ),
        [pltpu.VMEM((z_rows, 128), f32)],
        (planes, stem_wide, mask_table, info),
        "stem",
    )
    fields = [c0]
    gathered = [shared(stat0)]
    streams = []
    for layer in range(1, 7):
        keep = layer % 2 == 1
        residual = keep and layer > 1
        args = (fields[layer - 1],) + ((streams[-1],) if residual else ())
        args += (gathered[layer - 1], gathered[0], norm4, mask_table, q_table, ahead[layer - 1])
        outs = call(
            functools.partial(
                forward_kernel, index=layer - 1, keep=keep, residual=residual, devices=devices
            ),
            (field(rows),) + ((field(rows),) if keep else ()) + (stat,),
            [
                pltpu.VMEM(ring_shape, bf16),
                pltpu.VMEM(side_shape, bf16),
                pltpu.VMEM((2, 8, LANES), f32),
            ],
            args,
            "forward",
        )
        fields.append(outs[0])
        if keep:
            streams.append(outs[1])
        gathered.append(shared(outs[-1]))

    dys = [None] * 7
    stats = [None] * 7
    dys[6], stats[6], head_grad, small_grads = call(
        functools.partial(head_kernel, classes=classes, devices=devices),
        (
            field(rows),
            stat,
            jax.ShapeDtypeStruct((128, 128), f32),
            jax.ShapeDtypeStruct((2, 128), f32),
        ),
        [pltpu.VMEM((NI, NJ, rows, LANES), f32), pltpu.VMEM((rows, LANES), f32)],
        (
            fields[6], streams[2], gathered[6], gathered[0], norm4, mask_table, hot, info,
            into_head, from_head, bias_row,
        ),
        "head",
    )
    conv_grads = [None] * 6
    for layer in range(6, 0, -1):
        residual = layer in (5, 3)
        adding = layer % 2 == 1
        sums = shared(stats[layer])
        args = (dys[layer], fields[layer], fields[layer - 1])
        args += (streams[layer // 2 - 1],) if residual else ()
        args += (dys[layer + 1],) if adding else ()
        args += (
            sums, gathered[layer], gathered[layer - 1], gathered[0], norm4, mask_table, q_table,
            back[layer - 1],
        )
        dys[layer - 1], conv_grads[layer - 1], stats[layer - 1] = call(
            functools.partial(
                backward_kernel, index=layer, residual=residual, adding=adding, devices=devices
            ),
            (field(rows), jax.ShapeDtypeStruct((64, 576), f32), stat),
            [
                pltpu.VMEM(ring_shape, bf16),
                pltpu.VMEM(side_shape, bf16),
                pltpu.VMEM(ring_shape, bf16),
                pltpu.VMEM(side_shape, bf16),
                pltpu.VMEM((UNROLL + 1 + LAG, NI, rows, LANES), f32),
                pltpu.VMEM((2, 8, LANES), f32),
                pltpu.VMEM((LANES, 1024), f32),
            ],
            args,
            "backward",
        )
    stem_raw = call(
        stem_back_kernel,
        jax.ShapeDtypeStruct((4 * (span + 2) * 4, NI * LANES), f32),
        [],
        (dys[0], fields[0], z, shared(stats[0]), gathered[0], norm4, mask_table),
        "stem_back",
    )
    stem_grad = jnp.einsum(
        "krt,rko->ot",
        jnp.asarray(stem_table(), f32),
        stem_raw.reshape(-1, NI * 4, 64),
        precision=lax.Precision.HIGHEST,
    )
    local = jnp.stack([s[0] for s in stats])
    norm_grad = jnp.stack([local[:, 64:], local[:, :64]])
    conv_grad = jnp.stack(conv_grads, 0)
    head_grad = head_grad[:classes, :64]
    bias_grad = small_grads[0, :classes]
    loss_part = small_grads[1, 0]
    weight_total = jnp.sum(gathered[0][:, 129])

    member = lax.axis_index("wide")
    flat = flatten(stem_grad, conv_grad, norm_grad, head_grad, wide_count)
    flat, bias_sum, loss_narrow = (
        lax.psum(flat.astype(jnp.bfloat16), "narrow").astype(jnp.float32),
        lax.psum(bias_grad.astype(jnp.bfloat16), "narrow").astype(jnp.float32),
        lax.psum(loss_part.astype(jnp.bfloat16), "narrow").astype(jnp.float32),
    )

    def own_row(row):
        piece = lax.dynamic_index_in_dim(flat, (row + 2 * wide_count) % wide_count, 0, False)
        return piece

    def one_hop(hop, carried):
        noise = lax.dynamic_index_in_dim(cycle_noise[0], hop - 1, 0, False)
        level, scale = quantize(carried, noise)
        level_in = passed_along(level.astype(jnp.bfloat16), "wide", 1)
        scale_in = passed_along(scale, "wide", 1)
        return level_in.astype(jnp.float32) * scale_in / levels + own_row(member - 1 - hop)

    reduced = lax.fori_loop(1, wide_count, one_hop, own_row(member - 1))
    stem_share, conv_share, norm_share, head_share = unflatten_one(
        reduced, stem_weight.shape[0], channels, classes
    )
    stem_share = stem_share + weight_decay * stem_weight
    conv_share = conv_share + weight_decay * conv_weight
    head_share = head_share + weight_decay * head_weight
    squares = (
        jnp.sum(stem_share * stem_share)
        + jnp.sum(conv_share * conv_share)
        + jnp.sum(norm_share * norm_share)
        + jnp.sum(head_share * head_share)
    )
    square_total, bias_total, loss_total = lax.psum((squares, bias_sum, loss_narrow), "wide")
    grad_norm = jnp.sqrt(square_total + jnp.sum(bias_total * bias_total))
    factor = clip_limit / jnp.maximum(grad_norm, clip_limit)
    results = []
    for gradient, first, second, master in (
        (stem_share, stem_first, stem_second, stem_weight),
        (conv_share, conv_first, conv_second, conv_weight),
        (norm_share, norm_first, norm_second, norm_params),
        (head_share, head_first, head_second, head_weight),
        (bias_total, bias_first, bias_second, head_bias),
    ):
        results.extend(adam_update(gradient, first, second, master, factor))
    return (*results, grad_norm, loss_total, weight_total)


def solution(mesh):
    split = P(BOTH)
    ins = (
        P(None, BOTH), split, split, split, P("wide", None, None),
        P("wide", None), P(None, "wide", None), P(None, None, "wide"), P(None, "wide"), P(),
        P("wide", None), P("wide", None), P(None, "wide", None), P(None, "wide", None),
        P(None, None, "wide"), P(None, None, "wide"), P(None, "wide"), P(None, "wide"), P(), P(),
    )
    outs = (
        (P("wide", None),) * 3
        + (P(None, "wide", None),) * 3
        + (P(None, None, "wide"),) * 3
        + (P(None, "wide"),) * 3
        + (P(),) * 6
    )
    return jax.shard_map(body, mesh=mesh, in_specs=ins, out_specs=outs, check_vma=False)
```

```python
import functools

import jax
import jax.numpy as jnp
import numpy as np
from jax import lax
from jax.experimental import pallas as pl
from jax.experimental.pallas import tpu as pltpu
from jax.sharding import PartitionSpec as P

SIDE = 40
SHORT = 32
STEP = 10

norm_epsilon = 1e-05
clip_limit = 0.002
learn_rate = 0.4
first_decay = 0.9
second_decay = 0.999
adam_epsilon = 1e-08
weight_decay = 0.0005
decoupled = 0.01
levels = 15.0

QUARTERS = 4
PATCHES = SIDE // 2
NI = PATCHES // QUARTERS
NJ = PATCHES
SHORT_J = SHORT // 2
LANES = 256
UNROLL = 4
LAG = 2

f32 = jnp.float32
bf16 = jnp.bfloat16
BOTH = ("wide", "narrow")


def window_place(slot):
    group, sy, sx = slot // 4, (slot // 2) % 2, slot % 2
    wx = 1 + sx if group in (0, 2) else (3 if sx == 0 else 0)
    wy = 1 + sy if group in (0, 1) else (3 if sy == 0 else 0)
    return wy, wx


def tap_of(slot, out):
    wy, wx = window_place(slot)
    ky, kx = wy - out // 2, wx - out % 2
    if 0 <= ky < 3 and 0 <= kx < 3:
        return ky * 3 + kx
    return None


def whole():
    return pl.BlockSpec(memory_space=pltpu.VMEM)


def call(kernel, outs, scratch, args, name, cost=None, limit=24, stored=(), aliases=None):
    def place(out):
        return pl.BlockSpec(memory_space=pltpu.HBM) if type(out) is Stored else whole()

    def shape(out):
        kind = pltpu.HBM if isinstance(out, (Stored, Result)) else jax.ShapeDtypeStruct
        return kind(out.shape, out.dtype)

    args = [
        pltpu.with_memory_space_constraint(arg, pltpu.HBM) if k in stored else arg
        for k, arg in enumerate(args)
    ]

    return pl.pallas_call(
        kernel,
        out_shape=tuple(shape(out) for out in outs),
        in_specs=[
            pl.BlockSpec(memory_space=pltpu.HBM) if k in stored else whole()
            for k in range(len(args))
        ],
        out_specs=tuple(place(out) for out in outs),
        scratch_shapes=scratch,
        compiler_params=pltpu.CompilerParams(vmem_limit_bytes=limit * 2**20),
        name=name,
        input_output_aliases=aliases or {},
        cost_estimate=pl.CostEstimate(flops=cost, bytes_accessed=2**20, transcendentals=0)
        if cost
        else None,
    )(*args)


class Stored:
    def __init__(self, shape, dtype=bf16):
        self.shape, self.dtype = shape, dtype


class Result(Stored):
    pass


def stored_field(rows):
    return Stored((NI, NJ, rows, LANES))


class Streams:
    def __init__(self, outside, inside, sems, base):
        self.outside, self.inside = tuple(outside), tuple(inside)
        self.sems, self.base = sems, base

    def pairs(self, i):
        for k, (far, near) in enumerate(zip(self.outside, self.inside)):
            yield chunk(far, i), chunk(near, i), self.sems.at[self.base + k, i]

    def start_load(self, i):
        for far, near, sem in self.pairs(i):
            pltpu.make_async_copy(far, near, sem).start()

    def wait_load(self, i):
        for far, near, sem in self.pairs(i):
            pltpu.make_async_copy(far, near, sem).wait()

    def start_save(self, i):
        for far, near, sem in self.pairs(i):
            pltpu.make_async_copy(near, far, sem).start()

    def wait_save(self, i):
        for far, near, sem in self.pairs(i):
            pltpu.make_async_copy(near, far, sem).wait()


def chunk(ref, i):
    return ref.at[:, pl.ds(i * UNROLL, UNROLL)]


CHUNKS = NJ // UNROLL


def field(rows):
    return jax.ShapeDtypeStruct((NI, NJ, rows, LANES), bf16)


def wide_pair(row):
    turned = pltpu.roll(row, 64, 1)
    lower = lax.broadcasted_iota(jnp.int32, row.shape, 1) < 64
    first = jnp.where(lower, row, turned)
    second = jnp.where(lower, turned, row)
    return jnp.concatenate([first, first], 1), jnp.concatenate([second, second], 1)


def folded(row):
    half = row[:, :128] + row[:, 128:]
    return half + pltpu.roll(half, 64, 1)


def message(first, second):
    lower = lax.broadcasted_iota(jnp.int32, (1, 128), 1) < 64
    return jnp.where(lower, folded(first), folded(second))


def totals(gathered):
    rows = gathered[:, 0, :] if len(gathered.shape) == 3 else gathered[...]
    return wide_pair(jnp.sum(rows, 0, keepdims=True))


def send(ref, first, second=None):
    if second is None:
        ref[...] = jnp.broadcast_to(first, ref.shape)
    else:
        both = jnp.concatenate([first, second], 0)[None]
        ref[...] = jnp.broadcast_to(both, ref.shape)


def norm_constants(gathered, counted, norm4, index):
    sums, squares = totals(gathered)
    mean = sums / counted
    scale = lax.rsqrt(squares / counted - mean * mean + norm_epsilon)
    gain = norm4[index : index + 1]
    slope = gain * scale
    return mean, scale, slope, norm4[7 + index : 8 + index] - mean * slope


def pixels_of(gathered_first):
    return jnp.sum(gathered_first[:, 1, 0:1], 0, keepdims=True)


def twice(tile):
    return jnp.concatenate([tile, tile], 1)


def mask_row(J):
    return jnp.where(J < SHORT_J, 0, jnp.where(J < NJ, 1, 2))


def put_column(ring, slot, s, value, low, q_ref):
    rows = value.shape[0]
    ring[slot, s + 1] = low
    if s == 0:
        ring[slot, NI + 1, :, :128] = (pltpu.roll(value[:, :128], rows - 1, 0) * q_ref[0]).astype(
            bf16
        )
    if s == NI - 1:
        ring[slot, 0, :, 128:] = (pltpu.roll(value[:, 128:], 1, 0) * q_ref[1]).astype(bf16)


def side_columns(ring, side, u, lanes):
    for s in range(NI + 2):
        if s == 0:
            side[u, s, :, 128:] = jnp.where(
                lanes[:, 128:], ring[u + 2, s, :, 128:], ring[u, s, :, 128:]
            )
        elif s == NI + 1:
            side[u, s, :, :128] = jnp.where(
                lanes[:, :128], ring[u + 2, s, :, :128], ring[u, s, :, :128]
            )
        else:
            side[u, s] = jnp.where(lanes, ring[u + 2, s], ring[u, s])


def operands(ring, side, u):
    rows = ring.shape[2]
    whole_rows = NI * rows
    last = NI + 2
    own = ring[u + 1, 1 : NI + 1].reshape(whole_rows, LANES)
    beside = side[u, 1 : NI + 1].reshape(whole_rows, LANES)
    above = jnp.concatenate(
        [ring[u + 1, 2:last, :, :128], ring[u + 1, 0:NI, :, 128:]], -1
    ).reshape(whole_rows, LANES)
    corner = jnp.concatenate([side[u, 2:last, :, :128], side[u, 0:NI, :, 128:]], -1).reshape(
        whole_rows, LANES
    )
    return own, beside, above, corner


def product(parts, w_ref):
    total = jnp.dot(parts[0], w_ref[0:LANES], preferred_element_type=f32)
    for k in range(1, 4):
        total += jnp.dot(
            parts[k], w_ref[k * LANES : (k + 1) * LANES], preferred_element_type=f32
        )
    return total


def by_eight(value):
    return jnp.sum(value.reshape(value.shape[0] // 8, 8, value.shape[1]), 0)


def half_lanes(rows):
    return lax.broadcasted_iota(jnp.int32, (rows, LANES), 1) % 128 < 64


def pack_kernel(stem_ref, conv_ref, norm_ref, head_ref, out_ref):
    width = stem_ref.shape[0]
    gains = [norm_ref[:, k, :].T for k in range(2)]
    head = head_ref[...]
    used = 27 + 14 + head.shape[1]
    small = jnp.concatenate(
        [stem_ref[...], *gains, head, jnp.zeros((width, 128 - used), f32)], 1
    )
    high = small.astype(bf16)
    rest = small - high.astype(f32)
    middle = rest.astype(bf16)
    low = (rest - middle.astype(f32)).astype(bf16)
    tail = jnp.concatenate([high, middle, low, jnp.zeros((width, 192), bf16)], 1)
    for w in range(out_ref.shape[0]):
        for layer in range(6):
            out_ref[w, layer] = conv_ref[layer].astype(bf16)
        out_ref[w, 6] = tail


def weights_kernel(packed_ref, *refs):
    outs, (held, sems) = refs[:12], refs[12:]
    copies = []
    for layer in range(6):
        matrix = jnp.concatenate(
            [packed_ref[w, layer].astype(f32) for w in range(packed_ref.shape[0])], 0
        )
        turned = matrix.T
        empty = jnp.zeros((64, 64), f32)
        for slot in range(16):
            ahead, back = [], []
            for out in range(4):
                tap = tap_of(slot, out)
                if tap is None:
                    ahead.append(empty)
                    back.append(empty)
                else:
                    other = 8 - tap
                    ahead.append(turned[tap * 64 : (tap + 1) * 64])
                    back.append(matrix[:, other * 64 : (other + 1) * 64])
            at = slice(slot * 64, (slot + 1) * 64)
            held[layer, at] = jnp.concatenate(ahead, 1).astype(bf16)
            held[6 + layer, at] = jnp.concatenate(back, 1).astype(bf16)
        for k in (layer, 6 + layer):
            copies.append(pltpu.make_async_copy(held.at[k], outs[k], sems.at[k]))
            copies[-1].start()
    for copy in copies:
        copy.wait()


def small_kernel(packed_ref, table_ref, norm_ref, into_ref, back_ref, stem_ref):
    count, _, width, _ = packed_ref.shape
    parts = [
        jnp.concatenate(
            [packed_ref[w, 6, :, k * 128 : (k + 1) * 128].astype(f32) for w in range(count)], 0
        )
        for k in range(3)
    ]
    turned = ((parts[0] + parts[1]) + parts[2]).T
    norms = turned[27:43]
    norm_ref[...] = jnp.concatenate([norms] * 4, 1)
    head = jnp.concatenate([turned[41:], jnp.zeros((41, 64), f32)], 0)
    back_ref[...] = jnp.concatenate([head] * 4, 1).astype(bf16)
    into_ref[...] = jnp.concatenate([head.T, jnp.zeros((64, 128), f32)], 0).astype(bf16)
    stem = turned[:32].astype(bf16)
    for k in range(table_ref.shape[0] // 2):
        pair = [
            jnp.dot(table_ref[2 * k + e], stem, preferred_element_type=f32) for e in range(2)
        ]
        stem_ref[:, k * 128 : (k + 1) * 128] = jnp.concatenate(pair, 1).astype(bf16)


def stem_kernel(
    planes_ref, w_ref, mask_ref, info_ref, out_ref, save_ref, z_ref, stat_ref, zf, sem, *, devices
):
    rows = planes_ref.shape[1]
    zf[...] = jnp.zeros_like(zf)
    span = 2 * NI
    blocks = SIDE // span
    deep = (span + 2) * 4
    for i in range(3):
        turned = planes_ref[i].astype(f32).T
        for block in range(blocks):
            first = max(block * span - 1, 0)
            last = min(block * span + span + 1, SIDE)
            skip = first - (block * span - 1)
            for y in range(span):
                base = (block * (span + 2) + y + 1) * deep + skip * 4 + i
                zf[pl.ds(base, last - first, stride=4), :rows] = turned[
                    y * SIDE + first : y * SIDE + last
                ]
    lane = lax.broadcasted_iota(jnp.int32, (deep, 128), 1)
    for block in range(blocks):
        at = block * (span + 2) * deep
        low = zf[at + span * deep : at + (span + 1) * deep]
        zf[at : at + deep] = jnp.where(lane % 4 == 0, 0.0, pltpu.roll(low, 1, 1))
        high = zf[at + deep : at + 2 * deep]
        zf[at + (span + 1) * deep : at + (span + 2) * deep] = jnp.where(
            lane % 4 == 3, 0.0, pltpu.roll(high, 127, 1)
        )
    z_ref[...] = zf[...].astype(bf16)
    first_sum = jnp.zeros((8, LANES), f32)
    second_sum = jnp.zeros((8, LANES), f32)
    for block in range(blocks):
        for s in range(NI):
            at = (block * (span + 2) + 2 * s) * deep
            result = lax.dot_general(
                z_ref[at : at + 4 * deep],
                w_ref[...],
                (((0,), (0,)), ((), ())),
                preferred_element_type=f32,
            )
            for j in range(NI):
                J = block * NI + j
                mask = mask_ref[0 if J < SHORT_J else 1, 0 if s == 0 else 1]
                tile = result[:rows, j * LANES : (j + 1) * LANES] * twice(mask)
                out_ref[s, J] = tile.astype(bf16)
                first_sum += by_eight(tile)
                second_sum += by_eight(tile * tile)
    row = message(
        jnp.sum(first_sum, 0, keepdims=True), jnp.sum(second_sum, 0, keepdims=True)
    )
    counts = jnp.sum(info_ref[...], 0, keepdims=True) * (1.0 / QUARTERS)
    copy = pltpu.make_async_copy(out_ref, save_ref, sem)
    copy.start()
    send(stat_ref, row, counts)
    copy.wait()


def forward_kernel(*refs, index, keep, residual, devices):
    refs = list(refs)
    c_ref = refs.pop(0)
    res_ref = refs.pop(0) if residual else None
    gath_ref, first_ref, norm_ref, mask_ref, q_ref, w_ref, out_ref, save_ref = refs[:8]
    refs = refs[8:]
    keep_ref = refs.pop(0) if keep else None
    keep_save_ref = refs.pop(0) if keep else None
    stat_ref, ring, side, sums, sems, matrix, matrix_sem = refs
    fetch = pltpu.make_async_copy(w_ref, matrix, matrix_sem)
    fetch.start()
    rows = c_ref.shape[2]
    counted = pixels_of(first_ref)
    _, _, slope, start = norm_constants(gath_ref, counted, norm_ref, index)
    half_slope, half_start = slope * 0.5, start * 0.5
    lanes = half_lanes(rows)
    sums[...] = jnp.zeros_like(sums)

    def activate(J, slot):
        Jc = jnp.minimum(J, NJ - 1)
        jm = mask_row(J)
        for s in range(NI):
            half = c_ref[s, Jc].astype(f32) * half_slope + half_start
            if residual:
                half = half + 0.5 * res_ref[s, Jc].astype(f32)
            mask = mask_ref[jm, 0 if s == 0 else 1]
            value = (half + half * jnp.tanh(half)) * twice(mask)
            low = value.astype(bf16)
            put_column(ring, slot, s, value, low, q_ref)

    def convolve(J, u):
        side_columns(ring, side, u, lanes)
        total = product(operands(ring, side, u), matrix)
        jm = mask_row(J)
        first_sum, second_sum = sums[0], sums[1]
        for s in range(NI):
            tile = total[s * rows : (s + 1) * rows] * twice(mask_ref[jm, 0 if s == 0 else 1])
            out_ref[s, J] = tile.astype(bf16)
            if keep:
                keep_ref[s, J] = ring[u + 1, s + 1]
            first_sum += by_eight(tile)
            second_sum += by_eight(tile * tile)
        sums[0], sums[1] = first_sum, second_sum

    ring[UNROLL] = jnp.zeros(ring.shape[1:], bf16)
    for k in range(LAG):
        activate(k, UNROLL + 1 + k)
    fetch.wait()

    def step(i, carry):
        for k in range(LAG + 1):
            ring[k] = ring[UNROLL + k]
        for u in range(UNROLL):
            activate(i * UNROLL + u + LAG, u + LAG + 1)
            convolve(i * UNROLL + u, u)
        for copy in saves(i):
            copy.start()
        return carry

    def saves(i):
        copies = [pltpu.make_async_copy(chunk(out_ref, i), chunk(save_ref, i), sems.at[0, i])]
        if keep:
            copies.append(
                pltpu.make_async_copy(chunk(keep_ref, i), chunk(keep_save_ref, i), sems.at[1, i])
            )
        return copies

    lax.fori_loop(0, CHUNKS, step, 0)
    row = message(jnp.sum(sums[0], 0, keepdims=True), jnp.sum(sums[1], 0, keepdims=True))
    send(stat_ref, row)
    for i in range(CHUNKS):
        for copy in saves(i):
            copy.wait()


def head_kernel(
    c_ref, res_ref, gath_ref, first_ref, norm_ref, mask_ref, hot_ref, info_ref, into_ref, back_ref,
    bias_ref, dy_save_ref, stat_ref, head_ref, grads, pool, dy_ref, sems, *, classes, devices
):
    rows = c_ref.shape[2]
    counted = pixels_of(first_ref)
    weight_total = jnp.sum(first_ref[:, 1, 1:2], 0, keepdims=True)
    mean, scale, slope, start = norm_constants(gath_ref, counted, norm_ref, 6)
    half_slope, half_start = slope * 0.5, start * 0.5
    pool[...] = jnp.zeros_like(pool)

    def gather(J, carry):
        jm = mask_row(J)
        total = pool[...]
        for s in range(NI):
            half = c_ref[s, J].astype(f32) * half_slope + half_start
            half = half + 0.5 * res_ref[s, J].astype(f32)
            mask = twice(mask_ref[jm, 0 if s == 0 else 1])
            t = jnp.tanh(half)
            total += (half + half * t) * mask
            grads[s, J] = (0.5 + 0.5 * t) * (1.0 + half * (1.0 - t)) * mask
        pool[...] = total
        return carry

    lax.fori_loop(0, NJ, gather, 0)
    pooled = pool[...]
    row_index = lax.broadcasted_iota(jnp.int32, (rows, LANES), 0)
    pooled = pooled + jnp.where(
        row_index % 2 == 0, pltpu.roll(pooled, rows - 1, 0), pltpu.roll(pooled, 1, 0)
    )
    pooled = pooled + jnp.where(
        row_index % 4 < 2, pltpu.roll(pooled, rows - 2, 0), pltpu.roll(pooled, 2, 0)
    )
    half_pool = pooled[:, :128] + pooled[:, 128:]
    half_pool = half_pool + pltpu.roll(half_pool, 64, 1)
    count = info_ref[:, 0:1]
    weight = info_ref[:, 1:2]
    pooled_low = (half_pool / count).astype(bf16)
    logits = jnp.dot(pooled_low, into_ref[...], preferred_element_type=f32) + bias_ref[...]
    lane = lax.broadcasted_iota(jnp.int32, logits.shape, 1)
    inside = lane < classes
    top = jnp.max(jnp.where(inside, logits, -jnp.inf), 1, keepdims=True)
    shifted = jnp.where(inside, logits - top, 0.0)
    powers = jnp.where(inside, jnp.exp(shifted), 0.0)
    sum_powers = jnp.sum(powers, 1, keepdims=True)
    hot = hot_ref[...]
    losses = jnp.log(sum_powers) - jnp.sum(hot * shifted, 1, keepdims=True)
    single = (lax.broadcasted_iota(jnp.int32, (rows, 1), 0) % QUARTERS == 0).astype(f32)
    loss = jnp.sum(losses * weight * single, 0, keepdims=True)
    grad_low = ((weight / weight_total) * (powers / sum_powers - hot)).astype(bf16)
    grad_once = grad_low * single.astype(bf16)
    bias_grad = jnp.sum(grad_once.astype(f32), 0, keepdims=True)
    head_ref[...] = lax.dot_general(
        grad_once, pooled_low, (((0,), (0,)), ((), ())), preferred_element_type=f32
    )
    extra = jnp.where(lax.broadcasted_iota(jnp.int32, (1, 128), 1) == 127, loss, bias_grad)
    spread = jnp.dot(grad_low, back_ref[...], preferred_element_type=f32) / count

    out = Streams([dy_save_ref], [dy_ref], sems, 0)

    def scatter(i, carry):
        first_sum, second_sum = carry
        for u in range(UNROLL):
            J = i * UNROLL + u
            for s in range(NI):
                dy = spread * grads[s, J]
                dy_ref[s, J] = dy.astype(bf16)
                first_sum += by_eight(dy)
                second_sum += by_eight(dy * c_ref[s, J].astype(f32))
        out.start_save(i)
        return first_sum, second_sum

    zero = jnp.zeros((8, LANES), f32)
    first_sum, second_sum = lax.fori_loop(0, CHUNKS, scatter, (zero, zero))
    first_sum = jnp.sum(first_sum, 0, keepdims=True)
    second_sum = (jnp.sum(second_sum, 0, keepdims=True) - mean * first_sum) * scale
    send(stat_ref, message(first_sum, second_sum), extra)
    for i in range(CHUNKS):
        out.wait_save(i)


def grad_constants(sums_ref, gath_ref, counted, norm4, index):
    first_total, second_total = totals(sums_ref)
    mean, scale, slope, _ = norm_constants(gath_ref, counted, norm4, index)
    along = -slope * scale * second_total / counted
    return slope, along, -slope * first_total / counted - along * mean


def backward_kernel(*refs, index, residual, adding, devices):
    inputs = 3 + residual + adding
    far_in, refs = refs[:inputs], refs[inputs:]
    (
        sums_ref, gath_ref, gath_prev_ref, first_ref, norm_ref, mask_ref, q_ref, w_ref,
        out_far, grad_far, value_far, stat_ref, ring, side, offsets, sums, sems, matrix,
        matrix_sem, out_ref, grad_ref, value_ref,
    ) = refs[:22]
    held = list(refs[22:])
    loads = Streams(far_in, held, sems, 0)
    saves = Streams([out_far, grad_far, value_far], [out_ref, grad_ref, value_ref], sems, inputs)
    loads.start_load(0)
    fetch = pltpu.make_async_copy(w_ref, matrix, matrix_sem)
    fetch.start()
    for i in range(1, CHUNKS):
        loads.start_load(i)
    dy_ref = held.pop(0)
    c_ref, prev_ref = held[:2]
    res_ref = held[2] if residual else None
    add_ref = held[-1] if adding else None
    rows = c_ref.shape[2]
    counted = pixels_of(first_ref)
    grad_slope, grad_along, grad_start = grad_constants(
        sums_ref, gath_ref, counted, norm_ref, index
    )
    mean, scale, slope, start = norm_constants(gath_prev_ref, counted, norm_ref, index - 1)
    half_slope, half_start = slope * 0.5, start * 0.5
    lanes = half_lanes(rows)
    sums[...] = jnp.zeros_like(sums)
    for a in range(3):
        for b in range(2):
            offsets[a, b] = grad_start * twice(mask_ref[a, b])

    def activate(J, slot):
        Jc = jnp.minimum(J, NJ - 1)
        jm = mask_row(J)
        slope_now, along_now = grad_slope, grad_along
        if slot > UNROLL:
            present = jnp.where(J < NJ, 1.0, 0.0)
            slope_now, along_now = grad_slope * present, grad_along * present
        for s in range(NI):
            grad = dy_ref[s, Jc].astype(f32) * slope_now + (
                c_ref[s, Jc].astype(f32) * along_now + offsets[jm, 0 if s == 0 else 1]
            )
            put_column(ring, slot, s, grad, grad.astype(bf16), q_ref)

    def convolve(J, u):
        side_columns(ring, side, u, lanes)
        total = product(operands(ring, side, u), matrix)
        first_sum, second_sum = sums[0], sums[1]
        jm = mask_row(J)
        for s in range(NI):
            grad_ref[s, J] = ring[u + 1, s + 1]
            prev = prev_ref[s, J].astype(f32)
            half = prev * half_slope + half_start
            if residual:
                half = half + 0.5 * res_ref[s, J].astype(f32)
            sigma = (0.5 + 0.5 * jnp.tanh(half)) * twice(mask_ref[jm, 0 if s == 0 else 1])
            value = (half + half) * sigma
            value_ref[s, J] = value.astype(bf16)
            tile = total[s * rows : (s + 1) * rows]
            if adding:
                tile = tile + add_ref[s, J].astype(f32)
            tile = tile * (sigma + value - value * sigma)
            out_ref[s, J] = tile.astype(bf16)
            first_sum += by_eight(tile)
            second_sum += by_eight(tile * prev)
        sums[0], sums[1] = first_sum, second_sum

    ring[UNROLL] = jnp.zeros(ring.shape[1:], bf16)
    loads.wait_load(0)
    for k in range(LAG):
        activate(k, UNROLL + 1 + k)
    fetch.wait()

    def step(i, carry):
        @pl.when(i + 1 < CHUNKS)
        def _():
            loads.wait_load(i + 1)

        for k in range(LAG + 1):
            ring[k] = ring[UNROLL + k]
        for u in range(UNROLL):
            activate(i * UNROLL + u + LAG, u + LAG + 1)
            convolve(i * UNROLL + u, u)
        saves.start_save(i)
        return carry

    lax.fori_loop(0, CHUNKS, step, 0)
    first_sum = jnp.sum(sums[0], 0, keepdims=True)
    second_sum = (jnp.sum(sums[1], 0, keepdims=True) - mean * first_sum) * scale
    send(stat_ref, message(first_sum, second_sum))
    for i in range(CHUNKS):
        saves.wait_save(i)


def weight_grad_kernel(*refs, slot_out):
    if slot_out is None:
        grad_far, value_far, q_ref, out_ref = refs[:4]
        refs = refs[4:]
    else:
        grad_far, value_far, q_ref, _, out_far = refs[:5]
        refs = refs[5:]
    ring, side, acc, grad_in_ref, value_ref, sems, piece_ref, piece_sem = refs
    loads = Streams([grad_far, value_far], [grad_in_ref, value_ref], sems, 0)
    for i in range(CHUNKS):
        loads.start_load(i)
    rows = value_ref.shape[2]
    lanes = half_lanes(rows)

    def load(J, slot):
        Jc = jnp.minimum(J, NJ - 1)
        some = jnp.where(J < NJ, 1.0, 0.0)
        for s in range(NI):
            low = value_ref[s, Jc]
            if slot == UNROLL + 1:
                low = low * some.astype(bf16)
            put_column(ring, slot, s, low.astype(f32), low, q_ref)

    ring[UNROLL] = jnp.zeros(ring.shape[1:], bf16)
    loads.wait_load(0)
    load(0, UNROLL + 1)

    def step(i, carry):
        @pl.when(i + 1 < CHUNKS)
        def _():
            loads.wait_load(i + 1)

        for k in range(2):
            ring[k] = ring[UNROLL + k]
        for u in range(UNROLL):
            load(i * UNROLL + u + 1, u + 2)
        for u in range(UNROLL):
            side_columns(ring, side, u, lanes)
        grad = jnp.concatenate(
            [grad_in_ref[:, i * UNROLL + u] for u in range(UNROLL)], 0
        ).reshape(UNROLL * NI * rows, LANES)
        parts = [operands(ring, side, u) for u in range(UNROLL)]
        for k in range(4):
            value = jnp.concatenate([parts[u][k] for u in range(UNROLL)], 0)
            piece = lax.dot_general(
                grad, value, (((0,), (0,)), ((), ())), preferred_element_type=f32
            )
            at = slice(k * LANES, (k + 1) * LANES)
            acc[:, at] = jnp.where(i == 0, piece, acc[:, at] + piece)
        return carry

    lax.fori_loop(0, CHUNKS, step, 0)
    taps = [None] * 9
    for slot in range(16):
        for out in range(4):
            tap = tap_of(slot, out)
            if tap is not None:
                piece = acc[out * 64 : (out + 1) * 64, slot * 64 : (slot + 1) * 64]
                taps[tap] = piece if taps[tap] is None else taps[tap] + piece
    result = jnp.concatenate(taps, 1)
    if slot_out is None:
        out_ref[...] = result.astype(bf16)
    else:
        width = piece_ref.shape[1]
        for j in range(piece_ref.shape[0]):
            piece_ref[j] = result[j * width : (j + 1) * width].astype(bf16)
        copy = pltpu.make_async_copy(piece_ref, out_far.at[:, slot_out], piece_sem)
        copy.start()
        copy.wait()


def stem_back_kernel(
    dy_ref, c_ref, z_ref, sums_ref, gath_ref, norm_ref, mask_ref, table_ref, conv_ref, head_ref,
    *refs
):
    stat_refs, (out_ref, held, raw, sems) = refs[:7], refs[7:]
    copies = [
        pltpu.make_async_copy(
            c_ref.at[:, pl.ds(k * NI, NI)], held.at[:, pl.ds(k * NI, NI)], sems.at[k]
        )
        for k in range(NJ // NI)
    ]
    for copy in copies:
        copy.start()
    rows = held.shape[2]
    counted = pixels_of(gath_ref)
    slope, along, start = grad_constants(sums_ref, gath_ref, counted, norm_ref, 0)
    span = 2 * NI
    deep = (span + 2) * 4
    total = None
    for block in range(NJ // NI):
        copies[block].wait()
        for s in range(NI):
            at = (block * (span + 2) + 2 * s) * deep
            pieces = []
            for j in range(NI):
                J = block * NI + j
                mask = twice(mask_ref[0 if J < SHORT_J else 1, 0 if s == 0 else 1])
                grad = dy_ref[s, J].astype(f32) * slope + held[s, J].astype(f32) * along
                pieces.append(((grad + start) * mask).astype(bf16))
            piece = jnp.dot(
                z_ref[at : at + 4 * deep][:, :rows],
                jnp.concatenate(pieces, 1),
                preferred_element_type=f32,
            )
            if block == 0 and s == 0:
                raw[...] = piece
            else:
                raw[...] += piece
    total = jnp.zeros((64, 32), f32)
    for k in range(NI * 4):
        part = raw[:, k * 64 : (k + 1) * 64]
        high = part.astype(bf16)
        rest = (part - high.astype(f32)).astype(bf16)
        for value in (high, rest):
            total += lax.dot_general(
                value, table_ref[k], (((0,), (0,)), ((), ())), preferred_element_type=f32
            )
    stats = jnp.concatenate([ref[0:1] if len(ref.shape) == 2 else ref[0, 0:1] for ref in stat_refs], 0)
    shifts, gains = stats[:, :64], stats[:, 64:]
    norms = jnp.concatenate([gains, shifts, jnp.zeros((2, 64), f32)], 0).T
    head = head_ref[:, :64].T
    extra = jnp.concatenate(
        [total[:, :27], norms[:, :14], head[:, :23]], 1
    )
    out_ref[...] = jnp.concatenate([conv_ref[...].astype(f32), extra], 1).astype(bf16)


def chain_kernel(
    early_ref, last_ref, noise_ref, conv_ref, stem_ref, head_ref, conv_out, extra_out,
    square_ref, *, devices
):
    count, width = early_ref.shape[0], early_ref.shape[2]
    narrow = devices // count
    member = lax.axis_index("wide")

    def partial(w):
        last = last_ref[w * narrow].astype(f32)
        for n in range(1, narrow):
            last = last + last_ref[w * narrow + n].astype(f32)
        return [last[:, :576]] + [early_ref[w, k].astype(f32) for k in range(5)], last[:, 576:]

    def place(k):
        return lax.rem(member + k, count)

    def hop(k, carried):
        conv, extra = carried
        top = jnp.max(jnp.abs(extra), keepdims=True)
        for piece in conv:
            top = jnp.maximum(top, jnp.max(jnp.abs(piece), keepdims=True))
        scale = top + 1e-06
        sender = place(k)
        more, more_extra = partial(place(k + 1))

        def passed(value, dither, added):
            level = (value / scale * levels + dither.astype(f32)).astype(bf16)
            return level.astype(f32) * scale / levels + added

        conv = [passed(conv[m], noise_ref[sender, m], more[m]) for m in range(6)]
        dither = noise_ref[sender, 6][:, :64]
        known = lax.broadcasted_iota(jnp.int32, extra.shape, 1) < 41 + head_ref.shape[1]
        return conv, jnp.where(known, passed(extra, dither, more_extra), 0.0)

    conv, extra = lax.fori_loop(1, count, hop, partial(place(1)))
    head = head_ref[...]
    masters = jnp.concatenate(
        [
            stem_ref[...], jnp.zeros((width, 14), f32), head,
            jnp.zeros((width, 64 - 41 - head.shape[1]), f32),
        ],
        1,
    )
    extra = extra + weight_decay * masters
    total = jnp.sum(extra * extra, keepdims=True)
    for m in range(6):
        value = conv[m] + weight_decay * conv_ref[m]
        conv_out[m] = value
        total = total + jnp.sum(value * value, keepdims=True)
    extra_out[...] = jnp.concatenate([extra, extra], 1)
    square_ref[...] = jnp.broadcast_to(total, square_ref.shape)


def adam_kernel(square_ref, heads_ref, first_ref, conv_ref, extra_ref, *refs, classes):
    news, olds = refs[15:], refs[:15]
    bias = jnp.sum(heads_ref[:, 1, :], 0, keepdims=True)
    loss = bias[:, 127:128]
    bias = bias[:, :classes]
    total = jnp.sum(square_ref[...][:, 0:1], 0, keepdims=True)
    total = total + jnp.sum(bias * bias, keepdims=True)
    norm = jnp.sqrt(total)
    factor = clip_limit / jnp.maximum(norm, clip_limit)
    extra = extra_ref[...]
    turned = extra.T
    parts = (
        (extra[:, :27],), tuple(conv_ref[m] for m in range(6)),
        (turned[27:34], turned[34:41]), (extra[:, 41 : 41 + classes],), (bias,),
    )
    for k, pieces in enumerate(parts):
        master, first, second = olds[3 * k : 3 * k + 3]
        for m, gradient in enumerate(pieces):
            at = {6: (m,), 2: (slice(None), m)}.get(len(pieces), ())
            results = adam_update(gradient, first[at], second[at], master[at], factor)
            for ref, value in zip(news[3 * k : 3 * k + 3], results):
                ref[at] = value
    news[15][...] = norm
    news[16][...] = loss
    news[17][...] = jnp.sum(first_ref[:, 1, 1:2], 0, keepdims=True)


def stem_table():
    span = 2 * NI + 2
    table = np.zeros((NI * 4, 4, span, 4, 27), np.float32)
    for j in range(NI):
        for out in range(4):
            for ky in range(3):
                for kx in range(3):
                    for i in range(3):
                        table[
                            j * 4 + out, out // 2 + ky, 2 * j + out % 2 + kx, i,
                            (ky * 3 + kx) * 3 + i,
                        ] = 1.0
    return np.pad(table.reshape(NI * 4, 4 * span * 4, 27), ((0, 0), (0, 0), (0, 5)))


def adam_update(gradient, first, second, master, factor):
    clipped = gradient * factor
    new_first = first_decay * first + (1.0 - first_decay) * clipped
    new_second = second_decay * second + (1.0 - second_decay) * clipped * clipped
    corrected = (
        new_first
        / (1.0 - first_decay**STEP)
        / (jnp.sqrt(new_second / (1.0 - second_decay**STEP)) + adam_epsilon)
    )
    return (master - learn_rate * (corrected + decoupled * master), new_first, new_second)


def shared(rows):
    return lax.all_to_all(rows, BOTH, 0, 0, tiled=True)


def body(
    images,
    large_flag,
    labels,
    example_weights,
    cycle_noise,
    stem_weight,
    conv_weight,
    norm_params,
    head_weight,
    head_bias,
    stem_first,
    stem_second,
    conv_first,
    conv_second,
    norm_first,
    norm_second,
    head_first,
    head_second,
    bias_first,
    bias_second,
):
    wide_count = lax.axis_size("wide")
    devices = wide_count * lax.axis_size("narrow")
    count = large_flag.shape[0]
    rows = QUARTERS * count
    width = stem_weight.shape[0]
    channels = width * wide_count
    classes = head_weight.shape[0]
    assert channels == 64 and rows % 16 == 0 and rows <= 128

    member = lax.axis_index("wide")

    def to_wide(value):
        return lax.all_to_all(value, "wide", 0, 0, tiled=True)

    packed = call(
        pack_kernel,
        (jax.ShapeDtypeStruct((wide_count, 7, width, 576), bf16),),
        [],
        (stem_weight, conv_weight, norm_params.transpose(1, 0, 2), head_weight.T),
        "pack",
    )[0]
    packed = to_wide(packed)
    bias_row = jnp.pad(head_bias[None, :], ((0, 0), (0, 128 - classes)))

    dither = ((cycle_noise[0].astype(f32) + 0.5) / 65536.0 - 0.5).astype(bf16)
    hop_row = (member - 1 - jnp.arange(wide_count, dtype=jnp.int32)) % wide_count
    dither = jnp.take(dither, jnp.minimum(hop_row, wide_count - 2), axis=0)
    one, two, three = width * 27, width * 27 + 6 * width * 576, width * 41 + 6 * width * 576
    extra = jnp.concatenate(
        [
            dither[:, :one].reshape(wide_count, width, 27),
            dither[:, two:three].reshape(wide_count, 14, width).transpose(0, 2, 1),
            dither[:, three:].reshape(wide_count, classes, width).transpose(0, 2, 1),
        ],
        2,
    )
    extra = jnp.pad(extra, ((0, 0), (0, 0), (0, 576 - extra.shape[2])))
    dither = jnp.concatenate(
        [dither[:, one:two].reshape(wide_count, 6, width, 576), extra[:, None]], 1
    )

    large = large_flag == 1
    row_large = jnp.repeat(large, QUARTERS)
    quarter = jnp.arange(rows, dtype=jnp.int32) % QUARTERS
    upper = row_large | (quarter < SHORT_J // NI)
    ones = jnp.ones((rows,), bool)
    none = jnp.zeros((rows,), bool)
    mask_table = jnp.stack(
        [jnp.stack([ones, upper]), jnp.stack([row_large, row_large]), jnp.stack([none, none])]
    )
    mask_table = jnp.broadcast_to(mask_table[..., None], (3, 2, rows, 128)).astype(f32)
    q_table = jnp.broadcast_to(
        jnp.stack([quarter != QUARTERS - 1, quarter != 0])[..., None], (2, rows, 128)
    ).astype(f32)
    sides = jnp.where(large, SIDE, SHORT).astype(jnp.int32)
    weights_f = example_weights.astype(f32)
    lane = jnp.arange(128, dtype=jnp.int32)[None, :]
    info = jnp.where(
        lane == 0,
        jnp.repeat((sides * sides).astype(f32), QUARTERS)[:, None],
        jnp.where(lane == 1, jnp.repeat(weights_f, QUARTERS)[:, None], 0.0),
    )
    hot = (jnp.repeat(labels, QUARTERS)[:, None] == lane).astype(f32)

    span = 2 * NI
    position = jnp.arange(span * SIDE, dtype=jnp.int32)
    inside = row_large[:, None] | (
        (quarter[:, None] * span + (position // SIDE)[None, :] < SHORT)
        & ((position % SIDE)[None, :] < SHORT)
    )
    planes = images.reshape(3, rows, span * SIDE) * inside.astype(bf16)[None]

    (planes, mask_table, info, hot, bias_row, dither, packed) = lax.optimization_barrier(
        (planes, mask_table, info, hot, bias_row, dither, packed)
    )
    table = jnp.asarray(stem_table(), bf16)
    norm4, into_head, from_head, stem_wide = call(
        small_kernel,
        (
            jax.ShapeDtypeStruct((16, LANES), f32),
            jax.ShapeDtypeStruct((128, 128), bf16),
            jax.ShapeDtypeStruct((128, LANES), bf16),
            jax.ShapeDtypeStruct((table.shape[1], NI * LANES), bf16),
        ),
        [],
        (packed, table),
        "small",
        limit=12,
    )
    matrices = call(
        weights_kernel,
        (Stored((1024, LANES)),) * 12,
        [pltpu.VMEM((12, 1024, LANES), bf16), pltpu.SemaphoreType.DMA((12,))],
        (packed,),
        "weights",
        limit=16,
    )
    ahead, back = matrices[:6], matrices[6:]

    z_rows = (SIDE // span) * (span + 2) * (span + 2) * 4
    ring_shape = (UNROLL + 1 + LAG, NI + 2, rows, LANES)
    side_shape = (UNROLL, NI + 2, rows, LANES)
    stat = jax.ShapeDtypeStruct((devices, 128), f32)

    c0, c0_saved, z, stat0 = call(
        functools.partial(stem_kernel, devices=devices),
        (
            field(rows),
            stored_field(rows),
            jax.ShapeDtypeStruct((z_rows, 128), bf16),
            jax.ShapeDtypeStruct((devices, 2, 128), f32),
        ),
        [pltpu.VMEM((z_rows, 128), f32), pltpu.SemaphoreType.DMA],
        (planes, stem_wide, mask_table, info),
        "stem",
    )
    current, saved = c0, [c0_saved]
    gathered = [shared(stat0)]
    stream, streams = None, []
    for layer in range(1, 7):
        keep = layer % 2 == 1
        residual = keep and layer > 1
        args = (current,) + ((stream,) if residual else ())
        args += (gathered[layer - 1], gathered[0], norm4, mask_table, q_table, ahead[layer - 1])
        outs = call(
            functools.partial(
                forward_kernel, index=layer - 1, keep=keep, residual=residual, devices=devices
            ),
            (field(rows), stored_field(rows)) * (2 if keep else 1) + (stat,),
            [
                pltpu.VMEM(ring_shape, bf16),
                pltpu.VMEM(side_shape, bf16),
                pltpu.VMEM((2, 8, LANES), f32),
                pltpu.SemaphoreType.DMA((2, CHUNKS)),
                pltpu.VMEM((1024, LANES), bf16),
                pltpu.SemaphoreType.DMA,
            ],
            args,
            "forward",
            cost=int(7e9),
            limit=24,
            stored=(len(args) - 1,),
        )
        current = outs[0]
        saved.append(outs[1])
        if keep:
            stream = outs[2]
            streams.append(outs[3])
        gathered.append(shared(outs[-1]))

    dither = to_wide(dither)
    dys = [None] * 7
    stats = [None] * 7
    dys[6], stats[6], head_grad = call(
        functools.partial(head_kernel, classes=classes, devices=devices),
        (
            stored_field(rows),
            jax.ShapeDtypeStruct((devices, 2, 128), f32),
            jax.ShapeDtypeStruct((128, 128), f32),
        ),
        [
            pltpu.VMEM((NI, NJ, rows, LANES), f32),
            pltpu.VMEM((rows, LANES), f32),
            pltpu.VMEM((NI, NJ, rows, LANES), bf16),
            pltpu.SemaphoreType.DMA((1, CHUNKS)),
        ],
        (
            current, stream, gathered[6], gathered[0], norm4, mask_table, hot, info,
            into_head, from_head, bias_row,
        ),
        "head",
        cost=int(8e9),
        limit=28,
    )
    early = jnp.zeros((wide_count, 5, width, 576), bf16)
    full = pltpu.VMEM((NI, NJ, rows, LANES), bf16)
    for layer in range(6, 0, -1):
        residual = layer in (5, 3)
        adding = layer % 2 == 1
        sums = shared(stats[layer])
        if layer == 6:
            heads = sums
        args = (dys[layer], saved[layer], saved[layer - 1])
        args += (streams[layer // 2 - 1],) if residual else ()
        args += (dys[layer + 1],) if adding else ()
        inputs = len(args)
        args += (
            sums, gathered[layer], gathered[layer - 1], gathered[0], norm4, mask_table, q_table,
            back[layer - 1],
        )
        dys[layer - 1], grad, value, stats[layer - 1] = call(
            functools.partial(
                backward_kernel, index=layer, residual=residual, adding=adding, devices=devices
            ),
            (stored_field(rows),) * 3 + (stat,),
            [
                pltpu.VMEM(ring_shape, bf16),
                pltpu.VMEM(side_shape, bf16),
                pltpu.VMEM((3, 2, rows, LANES), f32),
                pltpu.VMEM((2, 8, LANES), f32),
                pltpu.SemaphoreType.DMA((8, CHUNKS)),
                pltpu.VMEM((1024, LANES), bf16),
                pltpu.SemaphoreType.DMA,
            ]
            + [full] * (3 + inputs),
            args,
            "backward",
            cost=int(8e9),
            limit=46,
            stored=tuple(range(inputs)) + (len(args) - 1,),
        )
        args = (grad, value, q_table) + ((early,) if layer > 1 else ())
        result = call(
            functools.partial(weight_grad_kernel, slot_out=layer - 2 if layer > 1 else None),
            (Stored(early.shape) if layer > 1 else jax.ShapeDtypeStruct((64, 576), bf16),),
            [
                pltpu.VMEM((UNROLL + 2, NI + 2, rows, LANES), bf16),
                pltpu.VMEM(side_shape, bf16),
                pltpu.VMEM((LANES, 1024), f32),
                full,
                full,
                pltpu.SemaphoreType.DMA((2, CHUNKS)),
                pltpu.VMEM((wide_count, width, 576), bf16),
                pltpu.SemaphoreType.DMA,
            ],
            args,
            "weight_grad",
            cost=int(7e9),
            limit=24,
            stored=(0, 1) + ((3,) if layer > 1 else ()),
            aliases={3: 0} if layer > 1 else None,
        )[0]
        if layer > 1:
            early = result
    early = lax.psum(early, "narrow")
    last = call(
        stem_back_kernel,
        (jax.ShapeDtypeStruct((64, 640), bf16),),
        [
            pltpu.VMEM((NI, NJ, rows, LANES), bf16),
            pltpu.VMEM((4 * (span + 2) * 4, NI * LANES), f32),
            pltpu.SemaphoreType.DMA((NJ // NI,)),
        ],
        (
            dys[0], saved[0], z, shared(stats[0]), gathered[0], norm4, mask_table, table,
            result, head_grad, *stats,
        ),
        "stem_back",
        stored=(1,),
    )[0]
    narrow_count = devices // wide_count
    early = to_wide(early)
    last = jnp.broadcast_to(
        last.reshape(wide_count, 1, width, 640), (wide_count, narrow_count, width, 640)
    )
    last = shared(last.reshape(devices, width, 640))
    conv_total, extra_total, squares = call(
        functools.partial(chain_kernel, devices=devices),
        (
            jax.ShapeDtypeStruct((6, width, 576), f32),
            jax.ShapeDtypeStruct((width, 128), f32),
            jax.ShapeDtypeStruct((wide_count, 128), f32),
        ),
        [],
        (early, last, dither, conv_weight, stem_weight, head_weight.T),
        "chain",
    )
    olds = (
        stem_weight, stem_first, stem_second, conv_weight, conv_first, conv_second,
        *(value.transpose(1, 0, 2) for value in (norm_params, norm_first, norm_second)),
        head_weight.T, head_first.T, head_second.T,
        head_bias[None], bias_first[None], bias_second[None],
    )
    single = jax.ShapeDtypeStruct((1, 1), f32)
    news = call(
        functools.partial(adam_kernel, classes=classes),
        tuple(Result(old.shape, f32) for old in olds) + (single,) * 3,
        [],
        (to_wide(squares), heads, gathered[0], conv_total, extra_total, *olds),
        "adam",
    )
    return (
        *news[:6],
        *(new.transpose(1, 0, 2) for new in news[6:9]),
        *(new.T for new in news[9:12]),
        *(new[0] for new in news[12:15]),
        *(new[0, 0] for new in news[15:]),
    )


def solution(mesh):
    split = P(BOTH)
    ins = (
        P(None, BOTH), split, split, split, P("wide", None, None),
        P("wide", None), P(None, "wide", None), P(None, None, "wide"), P(None, "wide"), P(),
        P("wide", None), P("wide", None), P(None, "wide", None), P(None, "wide", None),
        P(None, None, "wide"), P(None, None, "wide"), P(None, "wide"), P(None, "wide"), P(), P(),
    )
    outs = (
        (P("wide", None),) * 3
        + (P(None, "wide", None),) * 3
        + (P(None, None, "wide"),) * 3
        + (P(None, "wide"),) * 3
        + (P(),) * 6
    )
    return jax.shard_map(body, mesh=mesh, in_specs=ins, out_specs=outs, check_vma=False)
```

```python
import functools

import jax
import jax.numpy as jnp
import numpy as np
from jax import lax
from jax.experimental import pallas as pl
from jax.experimental.pallas import tpu as pltpu
from jax.sharding import PartitionSpec as P

SIDE = 40
SHORT = 32
STEP = 10

norm_epsilon = 1e-05
clip_limit = 0.002
learn_rate = 0.4
first_decay = 0.9
second_decay = 0.999
adam_epsilon = 1e-08
weight_decay = 0.0005
decoupled = 0.01
levels = 15.0

QUARTERS = 4
PATCHES = SIDE // 2
NI = PATCHES // QUARTERS
NJ = PATCHES
SHORT_J = SHORT // 2
LANES = 256
UNROLL = 4
BLOCK = 2

f32 = jnp.float32
bf16 = jnp.bfloat16
BOTH = ("wide", "narrow")


def window_place(slot):
    group, sy, sx = slot // 4, (slot // 2) % 2, slot % 2
    wx = 1 + sx if group in (0, 2) else (3 if sx == 0 else 0)
    wy = 1 + sy if group in (0, 1) else (3 if sy == 0 else 0)
    return wy, wx


def tap_of(slot, out):
    wy, wx = window_place(slot)
    ky, kx = wy - out // 2, wx - out % 2
    if 0 <= ky < 3 and 0 <= kx < 3:
        return ky * 3 + kx
    return None


def whole():
    return pl.BlockSpec(memory_space=pltpu.VMEM)


def call(kernel, outs, scratch, args, name, cost=None, limit=24, stored=(), aliases=None):
    def place(out):
        return pl.BlockSpec(memory_space=pltpu.HBM) if type(out) is Stored else whole()

    def shape(out):
        kind = pltpu.HBM if isinstance(out, (Stored, Result)) else jax.ShapeDtypeStruct
        return kind(out.shape, out.dtype)

    args = [
        pltpu.with_memory_space_constraint(arg, pltpu.HBM) if k in stored else arg
        for k, arg in enumerate(args)
    ]

    return pl.pallas_call(
        kernel,
        out_shape=tuple(shape(out) for out in outs),
        in_specs=[
            pl.BlockSpec(memory_space=pltpu.HBM) if k in stored else whole()
            for k in range(len(args))
        ],
        out_specs=tuple(place(out) for out in outs),
        scratch_shapes=scratch,
        compiler_params=pltpu.CompilerParams(vmem_limit_bytes=limit * 2**20),
        name=name,
        input_output_aliases=aliases or {},
        cost_estimate=pl.CostEstimate(flops=cost, bytes_accessed=2**20, transcendentals=0)
        if cost
        else None,
    )(*args)


class Stored:
    def __init__(self, shape, dtype=bf16):
        self.shape, self.dtype = shape, dtype


class Result(Stored):
    pass


def stored_field(rows):
    return Stored((NI, NJ, rows, LANES))


class Streams:
    def __init__(self, outside, inside, sems, base, columns=None):
        self.outside, self.inside = tuple(outside), tuple(inside)
        self.sems, self.base, self.columns = sems, base, columns or BLOCK

    def pairs(self, i):
        for k, (far, near) in enumerate(zip(self.outside, self.inside)):
            at = pl.ds(i * self.columns, self.columns)
            yield far.at[:, at], near.at[:, at], self.sems.at[self.base + k, i]

    def when(self, condition, action, i):
        @pl.when(condition)
        def _():
            action(i)

    def start_load(self, i):
        for far, near, sem in self.pairs(i):
            pltpu.make_async_copy(far, near, sem).start()

    def wait_load(self, i):
        for far, near, sem in self.pairs(i):
            pltpu.make_async_copy(far, near, sem).wait()

    def wait_loads(self, i):
        self.wait_load(i)
        self.wait_load(i + 1)

    def start_save(self, i):
        for far, near, sem in self.pairs(i):
            pltpu.make_async_copy(near, far, sem).start()

    def wait_save(self, i):
        for far, near, sem in self.pairs(i):
            pltpu.make_async_copy(near, far, sem).wait()


CHUNKS = NJ // BLOCK
GROUPS = NJ // UNROLL


def field(rows):
    return jax.ShapeDtypeStruct((NI, NJ, rows, LANES), bf16)


def wide_pair(row):
    turned = pltpu.roll(row, 64, 1)
    lower = lax.broadcasted_iota(jnp.int32, row.shape, 1) < 64
    first = jnp.where(lower, row, turned)
    second = jnp.where(lower, turned, row)
    return jnp.concatenate([first, first], 1), jnp.concatenate([second, second], 1)


def folded(row):
    half = row[:, :128] + row[:, 128:]
    return half + pltpu.roll(half, 64, 1)


def message(first, second):
    lower = lax.broadcasted_iota(jnp.int32, (1, 128), 1) < 64
    return jnp.where(lower, folded(first), folded(second))


def totals(gathered):
    rows = gathered[:, 0, :] if len(gathered.shape) == 3 else gathered[...]
    return wide_pair(jnp.sum(rows, 0, keepdims=True))


def send(ref, first, second=None):
    if second is None:
        ref[...] = jnp.broadcast_to(first, ref.shape)
    else:
        both = jnp.concatenate([first, second], 0)[None]
        ref[...] = jnp.broadcast_to(both, ref.shape)


def norm_constants(gathered, counted, norm4, index):
    sums, squares = totals(gathered)
    mean = sums / counted
    scale = lax.rsqrt(squares / counted - mean * mean + norm_epsilon)
    gain = norm4[index : index + 1]
    slope = gain * scale
    return mean, scale, slope, norm4[7 + index : 8 + index] - mean * slope


def pixels_of(gathered_first):
    return jnp.sum(gathered_first[:, 1, 0:1], 0, keepdims=True)


def twice(tile):
    return jnp.concatenate([tile, tile], 1)


def mask_row(J):
    return jnp.where((J < 0) | (J >= NJ), 2, jnp.where(J < SHORT_J, 0, 1))


def put_column(ring, slot, s, value, low, q_ref):
    rows = value.shape[0]
    ring[slot, s + 1] = low
    if s == 0:
        ring[slot, NI + 1, :, :128] = (pltpu.roll(value[:, :128], rows - 1, 0) * q_ref[0]).astype(
            bf16
        )
    if s == NI - 1:
        ring[slot, 0, :, 128:] = (pltpu.roll(value[:, 128:], 1, 0) * q_ref[1]).astype(bf16)


def side_columns(ring, side, u, lanes):
    for s in range(NI + 2):
        if s == 0:
            side[u, s, :, 128:] = jnp.where(
                lanes[:, 128:], ring[u + 2, s, :, 128:], ring[u, s, :, 128:]
            )
        elif s == NI + 1:
            side[u, s, :, :128] = jnp.where(
                lanes[:, :128], ring[u + 2, s, :, :128], ring[u, s, :, :128]
            )
        else:
            side[u, s] = jnp.where(lanes, ring[u + 2, s], ring[u, s])


def operands(ring, side, u):
    rows = ring.shape[2]
    whole_rows = NI * rows
    last = NI + 2
    own = ring[u + 1, 1 : NI + 1].reshape(whole_rows, LANES)
    beside = side[u, 1 : NI + 1].reshape(whole_rows, LANES)
    above = jnp.concatenate(
        [ring[u + 1, 2:last, :, :128], ring[u + 1, 0:NI, :, 128:]], -1
    ).reshape(whole_rows, LANES)
    corner = jnp.concatenate([side[u, 2:last, :, :128], side[u, 0:NI, :, 128:]], -1).reshape(
        whole_rows, LANES
    )
    return own, beside, above, corner


def product(parts, w_ref):
    total = jnp.dot(parts[0], w_ref[0:LANES], preferred_element_type=f32)
    for k in range(1, 4):
        total += jnp.dot(
            parts[k], w_ref[k * LANES : (k + 1) * LANES], preferred_element_type=f32
        )
    return total


def tree(values):
    values = list(values)
    while len(values) > 1:
        paired = [a + b for a, b in zip(values[::2], values[1::2])]
        values = paired + values[len(values) - len(values) % 2 :]
    return values[0]


def by_eight(value):
    return tree(value[k : k + 8] for k in range(0, value.shape[0], 8))


def summed(tiles):
    low = tree(tiles)
    low = tree(low[k : k + 16] for k in range(0, low.shape[0], 16))
    return by_eight(low.astype(f32))


def total_of(sums, which):
    return jnp.sum(tree(sums[which, u] for u in range(sums.shape[1])), 0, keepdims=True)


def pipeline(sets, activate, finish, matrix, lanes, before, after):
    def ready(block, own, other):
        ring, side, _ = own
        if other is None:
            ring[0] = jnp.zeros(ring.shape[1:], bf16)
            activate(0, ring, 1)
        else:
            ring[0] = other[0][BLOCK]
            ring[1] = other[0][BLOCK + 1]
        for u in range(BLOCK):
            activate(block * BLOCK + u + 1, ring, u + 2)
        for u in range(BLOCK):
            side_columns(ring, side, u, lanes)

    def multiply(own):
        ring, side, result = own
        parts = [operands(ring, side, u) for u in range(BLOCK)]
        result[...] = product(
            [jnp.concatenate([part[k] for part in parts], 0) for k in range(4)], matrix
        )

    def step(j, carry):
        for half in range(2):
            own, other = sets[half], sets[1 - half]
            block = 2 * j + half
            if half == 0:
                before(block)
            multiply(own)
            for u in range(BLOCK):
                finish((block - 1) * BLOCK + u, other, u)
            ready(block + 1, other, own)
            after(block)
        return carry

    sets[1][2][...] = jnp.zeros(sets[1][2].shape, f32)
    ready(0, sets[0], None)

    def tail():
        for u in range(BLOCK):
            finish(NJ - BLOCK + u, sets[1], u)

    return step, tail


def half_lanes(rows):
    return lax.broadcasted_iota(jnp.int32, (rows, LANES), 1) % 128 < 64


def pack_kernel(*refs):
    out_ref, held, sems = refs[4], refs[5:9], refs[9]
    copies = [pltpu.make_async_copy(refs[k], held[k], sems.at[k]) for k in range(4)]
    for copy in copies:
        copy.start()
    for copy in copies:
        copy.wait()
    stem_ref, conv_ref, norm_ref, head_ref = held
    width = stem_ref.shape[0]
    gains = [norm_ref[:, k, :].T for k in range(2)]
    head = head_ref[...]
    used = 27 + 14 + head.shape[1]
    small = jnp.concatenate(
        [stem_ref[...], *gains, head, jnp.zeros((width, 128 - used), f32)], 1
    )
    high = small.astype(bf16)
    rest = small - high.astype(f32)
    middle = rest.astype(bf16)
    low = (rest - middle.astype(f32)).astype(bf16)
    tail = jnp.concatenate([high, middle, low, jnp.zeros((width, 192), bf16)], 1)
    for w in range(out_ref.shape[0]):
        for layer in range(6):
            out_ref[w, layer] = conv_ref[layer].astype(bf16)
        out_ref[w, 6] = tail


def weights_kernel(packed_ref, *refs):
    outs, (held, sems) = refs[:12], refs[12:]
    copies = []
    for layer in range(6):
        matrix = jnp.concatenate(
            [packed_ref[w, layer].astype(f32) for w in range(packed_ref.shape[0])], 0
        )
        turned = matrix.T
        empty = jnp.zeros((64, 64), f32)
        for slot in range(16):
            ahead, back = [], []
            for out in range(4):
                tap = tap_of(slot, out)
                if tap is None:
                    ahead.append(empty)
                    back.append(empty)
                else:
                    other = 8 - tap
                    ahead.append(turned[tap * 64 : (tap + 1) * 64])
                    back.append(matrix[:, other * 64 : (other + 1) * 64])
            at = slice(slot * 64, (slot + 1) * 64)
            held[layer, at] = jnp.concatenate(ahead, 1).astype(bf16)
            held[6 + layer, at] = jnp.concatenate(back, 1).astype(bf16)
        for k in (layer, 6 + layer):
            copies.append(pltpu.make_async_copy(held.at[k], outs[k], sems.at[k]))
            copies[-1].start()
    for copy in copies:
        copy.wait()


def small_kernel(packed_ref, table_ref, norm_ref, into_ref, back_ref, stem_ref):
    count, _, width, _ = packed_ref.shape
    parts = [
        jnp.concatenate(
            [packed_ref[w, 6, :, k * 128 : (k + 1) * 128].astype(f32) for w in range(count)], 0
        )
        for k in range(3)
    ]
    turned = ((parts[0] + parts[1]) + parts[2]).T
    norms = turned[27:43]
    norm_ref[...] = jnp.concatenate([norms] * 4, 1)
    head = jnp.concatenate([turned[41:], jnp.zeros((41, 64), f32)], 0)
    back_ref[...] = jnp.concatenate([head] * 4, 1).astype(bf16)
    into_ref[...] = jnp.concatenate([head.T, jnp.zeros((64, 128), f32)], 0).astype(bf16)
    stem = turned[:32].astype(bf16)
    for k in range(table_ref.shape[0] // 2):
        pair = [
            jnp.dot(table_ref[2 * k + e], stem, preferred_element_type=f32) for e in range(2)
        ]
        stem_ref[:, k * 128 : (k + 1) * 128] = jnp.concatenate(pair, 1).astype(bf16)


def stem_kernel(
    planes_ref, w_ref, mask_ref, info_ref, save_ref, z_ref, stat_ref, zf, out_ref, sems, *, devices
):
    rows = planes_ref.shape[1]
    zf[...] = jnp.zeros_like(zf)
    span = 2 * NI
    blocks = SIDE // span
    deep = (span + 2) * 4
    for i in range(3):
        turned = planes_ref[i].astype(f32).T
        for block in range(blocks):
            first = max(block * span - 1, 0)
            last = min(block * span + span + 1, SIDE)
            skip = first - (block * span - 1)
            for y in range(span):
                base = (block * (span + 2) + y + 1) * deep + skip * 4 + i
                zf[pl.ds(base, last - first, stride=4), :rows] = turned[
                    y * SIDE + first : y * SIDE + last
                ]
    lane = lax.broadcasted_iota(jnp.int32, (deep, 128), 1)
    for block in range(blocks):
        at = block * (span + 2) * deep
        low = zf[at + span * deep : at + (span + 1) * deep]
        zf[at : at + deep] = jnp.where(lane % 4 == 0, 0.0, pltpu.roll(low, 1, 1))
        high = zf[at + deep : at + 2 * deep]
        zf[at + (span + 1) * deep : at + (span + 2) * deep] = jnp.where(
            lane % 4 == 3, 0.0, pltpu.roll(high, 127, 1)
        )
    z_ref[...] = zf[...].astype(bf16)
    first_sum = jnp.zeros((8, LANES), f32)
    second_sum = jnp.zeros((8, LANES), f32)
    copies = []
    for block in range(blocks):
        for s in range(NI):
            at = (block * (span + 2) + 2 * s) * deep
            result = lax.dot_general(
                z_ref[at : at + 4 * deep],
                w_ref[...],
                (((0,), (0,)), ((), ())),
                preferred_element_type=f32,
            )
            for j in range(NI):
                J = block * NI + j
                mask = mask_ref[0 if J < SHORT_J else 1, 0 if s == 0 else 1]
                tile = result[:rows, j * LANES : (j + 1) * LANES] * twice(mask)
                out_ref[s, J] = tile.astype(bf16)
                first_sum += by_eight(tile)
                second_sum += by_eight(tile * tile)
        at = pl.ds(block * NI, NI)
        copies.append(pltpu.make_async_copy(out_ref.at[:, at], save_ref.at[:, at], sems.at[block]))
        copies[-1].start()
    row = message(
        jnp.sum(first_sum, 0, keepdims=True), jnp.sum(second_sum, 0, keepdims=True)
    )
    counts = jnp.sum(info_ref[...], 0, keepdims=True) * (1.0 / QUARTERS)
    send(stat_ref, row, counts)
    for copy in copies:
        copy.wait()


def forward_kernel(*refs, index, keep, residual, streamed, devices):
    refs = list(refs)
    c_ref = refs.pop(0)
    if streamed:
        load_sems, held = refs.pop(), refs.pop()
        loads = Streams([c_ref], [held], load_sems, 0)
        for i in range(CHUNKS):
            loads.start_load(i)
        c_ref = held
    res_ref = refs.pop(0) if residual else None
    gath_ref, first_ref, norm_ref, mask_ref, q_ref, w_ref, out_ref, save_ref = refs[:8]
    refs = refs[8:]
    keep_ref = refs.pop(0) if keep else None
    keep_save_ref = refs.pop(0) if keep else None
    stat_ref, sums, sems = refs[:3]
    sets = refs[3:6], refs[6:9]
    rows = c_ref.shape[2]
    counted = pixels_of(first_ref)
    _, _, slope, start = norm_constants(gath_ref, counted, norm_ref, index)
    half_slope, half_start = slope * 0.5, start * 0.5
    lanes = half_lanes(rows)
    sums[...] = jnp.zeros_like(sums)

    def activate(J, ring, slot):
        Jc = jnp.minimum(J, NJ - 1)
        jm = mask_row(J)
        for s in range(NI):
            half = c_ref[s, Jc].astype(f32) * half_slope + half_start
            if residual:
                half = half + 0.5 * res_ref[s, Jc].astype(f32)
            mask = mask_ref[jm, 0 if s == 0 else 1]
            value = (half + half * jnp.tanh(half)) * twice(mask)
            low = value.astype(bf16)
            put_column(ring, slot, s, value, low, q_ref)

    def finish(J, own, u):
        Jc = jnp.maximum(J, 0)
        jm = mask_row(J)
        tiles = []
        for s in range(NI):
            tile = own[2][(u * NI + s) * rows : (u * NI + s + 1) * rows]
            low = (tile * twice(mask_ref[jm, 0 if s == 0 else 1])).astype(bf16)
            out_ref[s, Jc] = low
            if keep:
                keep_ref[s, Jc] = own[0][u + 1, s + 1]
            tiles.append(low)
        sums[0, u] += summed(tiles)
        sums[1, u] += summed([tile * tile for tile in tiles])

    def before(block):
        if streamed:
            loads.when(block + 2 < CHUNKS, loads.wait_loads, block + 2)

    def after(block):
        saves.when(block > 0, saves.start_save, block - 1)

    saves = Streams([save_ref, keep_save_ref][: 1 + keep], [out_ref, keep_ref][: 1 + keep], sems, 0)
    if keep:
        sets[1][0][...] = jnp.zeros(sets[1][0].shape, bf16)
    if streamed:
        loads.wait_load(0)
        loads.wait_load(1)
    step, tail = pipeline(sets, activate, finish, w_ref, lanes, before, after)
    lax.fori_loop(0, CHUNKS // 2, step, 0)
    tail()
    saves.start_save(CHUNKS - 1)
    row = message(total_of(sums, 0), total_of(sums, 1))
    send(stat_ref, row)
    for i in range(CHUNKS):
        saves.wait_save(i)


def head_kernel(
    c_ref, res_ref, gath_ref, first_ref, norm_ref, mask_ref, hot_ref, info_ref, into_ref, back_ref,
    bias_ref, dy_save_ref, stat_ref, head_ref, grads, pool, dy_ref, sems, *, classes, devices
):
    rows = c_ref.shape[2]
    counted = pixels_of(first_ref)
    weight_total = jnp.sum(first_ref[:, 1, 1:2], 0, keepdims=True)
    mean, scale, slope, start = norm_constants(gath_ref, counted, norm_ref, 6)
    half_slope, half_start = slope * 0.5, start * 0.5
    pool[...] = jnp.zeros_like(pool)

    def gather(J, carry):
        jm = mask_row(J)
        total = pool[...]
        for s in range(NI):
            half = c_ref[s, J].astype(f32) * half_slope + half_start
            half = half + 0.5 * res_ref[s, J].astype(f32)
            mask = twice(mask_ref[jm, 0 if s == 0 else 1])
            t = jnp.tanh(half)
            total += (half + half * t) * mask
            grads[s, J] = (0.5 + 0.5 * t) * (1.0 + half * (1.0 - t)) * mask
        pool[...] = total
        return carry

    lax.fori_loop(0, NJ, gather, 0)
    pooled = pool[...]
    row_index = lax.broadcasted_iota(jnp.int32, (rows, LANES), 0)
    pooled = pooled + jnp.where(
        row_index % 2 == 0, pltpu.roll(pooled, rows - 1, 0), pltpu.roll(pooled, 1, 0)
    )
    pooled = pooled + jnp.where(
        row_index % 4 < 2, pltpu.roll(pooled, rows - 2, 0), pltpu.roll(pooled, 2, 0)
    )
    half_pool = pooled[:, :128] + pooled[:, 128:]
    half_pool = half_pool + pltpu.roll(half_pool, 64, 1)
    count = info_ref[:, 0:1]
    weight = info_ref[:, 1:2]
    pooled_low = (half_pool / count).astype(bf16)
    logits = jnp.dot(pooled_low, into_ref[...], preferred_element_type=f32) + bias_ref[...]
    lane = lax.broadcasted_iota(jnp.int32, logits.shape, 1)
    inside = lane < classes
    top = jnp.max(jnp.where(inside, logits, -jnp.inf), 1, keepdims=True)
    shifted = jnp.where(inside, logits - top, 0.0)
    powers = jnp.where(inside, jnp.exp(shifted), 0.0)
    sum_powers = jnp.sum(powers, 1, keepdims=True)
    hot = hot_ref[...]
    losses = jnp.log(sum_powers) - jnp.sum(hot * shifted, 1, keepdims=True)
    single = (lax.broadcasted_iota(jnp.int32, (rows, 1), 0) % QUARTERS == 0).astype(f32)
    loss = jnp.sum(losses * weight * single, 0, keepdims=True)
    grad_low = ((weight / weight_total) * (powers / sum_powers - hot)).astype(bf16)
    grad_once = grad_low * single.astype(bf16)
    bias_grad = jnp.sum(grad_once.astype(f32), 0, keepdims=True)
    head_ref[...] = lax.dot_general(
        grad_once, pooled_low, (((0,), (0,)), ((), ())), preferred_element_type=f32
    )
    extra = jnp.where(lax.broadcasted_iota(jnp.int32, (1, 128), 1) == 127, loss, bias_grad)
    spread = jnp.dot(grad_low, back_ref[...], preferred_element_type=f32) / count

    out = Streams([dy_save_ref], [dy_ref], sems, 0)

    def scatter(i, carry):
        first_sum, second_sum = carry
        for u in range(UNROLL):
            J = i * UNROLL + u
            for s in range(NI):
                dy = spread * grads[s, J]
                dy_ref[s, J] = dy.astype(bf16)
                first_sum += by_eight(dy)
                second_sum += by_eight(dy * c_ref[s, J].astype(f32))
        out.start_save(2 * i)
        out.start_save(2 * i + 1)
        return first_sum, second_sum

    zero = jnp.zeros((8, LANES), f32)
    first_sum, second_sum = lax.fori_loop(0, GROUPS, scatter, (zero, zero))
    first_sum = jnp.sum(first_sum, 0, keepdims=True)
    second_sum = (jnp.sum(second_sum, 0, keepdims=True) - mean * first_sum) * scale
    send(stat_ref, message(first_sum, second_sum), extra)
    for i in range(CHUNKS):
        out.wait_save(i)


def grad_constants(sums_ref, gath_ref, counted, norm4, index):
    first_total, second_total = totals(sums_ref)
    mean, scale, slope, _ = norm_constants(gath_ref, counted, norm4, index)
    along = -slope * scale * second_total / counted
    return slope, along, -slope * first_total / counted - along * mean


def backward_kernel(*refs, index, residual, adding, ordered, devices):
    inputs = 3 + residual + adding
    far_in, refs = refs[:inputs], refs[inputs:]
    refs = refs[:8] + refs[8 + ordered :]
    (
        sums_ref, gath_ref, gath_prev_ref, first_ref, norm_ref, mask_ref, q_ref, w_ref,
        out_far, grad_far, value_far, stat_ref, ring, side, offsets, sums, sems, matrix,
        matrix_sem, out_ref, grad_ref, value_ref,
    ) = refs[:22]
    held = list(refs[22:])
    loads = Streams(far_in, held, sems, 0, UNROLL)
    saves = Streams([out_far, grad_far, value_far], [out_ref, grad_ref, value_ref], sems, inputs, UNROLL)
    loads.start_load(0)
    fetch = pltpu.make_async_copy(w_ref, matrix, matrix_sem)
    fetch.start()
    for i in range(1, GROUPS):
        loads.start_load(i)
    dy_ref = held.pop(0)
    c_ref, prev_ref = held[:2]
    res_ref = held[2] if residual else None
    add_ref = held[-1] if adding else None
    rows = c_ref.shape[2]
    counted = pixels_of(first_ref)
    grad_slope, grad_along, grad_start = grad_constants(
        sums_ref, gath_ref, counted, norm_ref, index
    )
    mean, scale, slope, start = norm_constants(gath_prev_ref, counted, norm_ref, index - 1)
    half_slope, half_start = slope * 0.5, start * 0.5
    lanes = half_lanes(rows)
    sums[...] = jnp.zeros_like(sums)
    for a in range(3):
        for b in range(2):
            offsets[a, b] = grad_start * twice(mask_ref[a, b])

    def activate(J, slot):
        Jc = jnp.minimum(J, NJ - 1)
        jm = mask_row(J)
        slope_now, along_now = grad_slope, grad_along
        if slot > UNROLL:
            present = jnp.where(J < NJ, 1.0, 0.0)
            slope_now, along_now = grad_slope * present, grad_along * present
        for s in range(NI):
            grad = dy_ref[s, Jc].astype(f32) * slope_now + (
                c_ref[s, Jc].astype(f32) * along_now + offsets[jm, 0 if s == 0 else 1]
            )
            put_column(ring, slot, s, grad, grad.astype(bf16), q_ref)

    def multiply():
        for u in range(UNROLL):
            side_columns(ring, side, u, lanes)
        parts = [operands(ring, side, u) for u in range(UNROLL)]
        return product(
            [jnp.concatenate([part[k] for part in parts], 0) for k in range(4)], matrix
        )

    def convolve(J, u, everything):
        total = everything[u * NI * rows : (u + 1) * NI * rows]
        jm = mask_row(J)
        tiles, others = [], []
        for s in range(NI):
            grad_ref[s, J] = ring[u + 1, s + 1]
            half = prev_ref[s, J].astype(f32) * half_slope + half_start
            if residual:
                half = half + 0.5 * res_ref[s, J].astype(f32)
            sigma = (0.5 + 0.5 * jnp.tanh(half)) * twice(mask_ref[jm, 0 if s == 0 else 1])
            value = (half + half) * sigma
            value_ref[s, J] = value.astype(bf16)
            tile = total[s * rows : (s + 1) * rows]
            if adding:
                tile = tile + add_ref[s, J].astype(f32)
            tile = tile * (sigma + value - value * sigma)
            low = tile.astype(bf16)
            out_ref[s, J] = low
            tiles.append(low)
            others.append(low * prev_ref[s, J])
        sums[0, u] += summed(tiles)
        sums[1, u] += summed(others)

    ring[UNROLL] = jnp.zeros(ring.shape[1:], bf16)
    loads.wait_load(0)
    activate(0, UNROLL + 1)
    fetch.wait()

    def step(i, carry):
        @pl.when(i + 1 < GROUPS)
        def _():
            loads.wait_load(i + 1)

        for k in range(2):
            ring[k] = ring[UNROLL + k]
        for u in range(UNROLL):
            activate(i * UNROLL + u + 1, u + 2)
        everything = multiply()
        for u in range(UNROLL):
            convolve(i * UNROLL + u, u, everything)
        saves.start_save(i)
        return carry

    lax.fori_loop(0, GROUPS, step, 0)
    first_sum = total_of(sums, 0)
    second_sum = (total_of(sums, 1) - mean * first_sum) * scale
    send(stat_ref, message(first_sum, second_sum))
    for i in range(GROUPS):
        saves.wait_save(i)


def weight_grad_kernel(*refs, slot_out):
    grad_far, value_far, q_ref = refs[:3]
    refs = refs[3 + (slot_out is not None) :]
    out_ref, token_ref, refs = refs[0], refs[1], refs[2:]
    token_ref[...] = jnp.zeros_like(token_ref)
    ring, side, acc, grad_in_ref, value_ref, sems, piece_ref, piece_sem = refs
    loads = Streams([grad_far, value_far], [grad_in_ref, value_ref], sems, 0)
    for i in range(CHUNKS):
        loads.start_load(i)
    rows = value_ref.shape[2]
    lanes = half_lanes(rows)

    def load(J, slot):
        Jc = jnp.minimum(J, NJ - 1)
        some = jnp.where(J < NJ, 1.0, 0.0)
        for s in range(NI):
            low = value_ref[s, Jc]
            if slot == UNROLL + 1:
                low = low * some.astype(bf16)
            put_column(ring, slot, s, low.astype(f32), low, q_ref)

    ring[UNROLL] = jnp.zeros(ring.shape[1:], bf16)
    loads.wait_load(0)
    load(0, UNROLL + 1)

    def step(i, carry):
        loads.wait_load(2 * i + 1)
        loads.when(2 * i + 2 < CHUNKS, loads.wait_load, 2 * i + 2)
        for k in range(2):
            ring[k] = ring[UNROLL + k]
        for u in range(UNROLL):
            load(i * UNROLL + u + 1, u + 2)
        for u in range(UNROLL):
            side_columns(ring, side, u, lanes)
        grad = jnp.concatenate(
            [grad_in_ref[:, i * UNROLL + u] for u in range(UNROLL)], 0
        ).reshape(UNROLL * NI * rows, LANES)
        parts = [operands(ring, side, u) for u in range(UNROLL)]
        for k in range(4):
            value = jnp.concatenate([parts[u][k] for u in range(UNROLL)], 0)
            piece = lax.dot_general(
                grad, value, (((0,), (0,)), ((), ())), preferred_element_type=f32
            )
            at = slice(k * LANES, (k + 1) * LANES)
            acc[:, at] = jnp.where(i == 0, piece, acc[:, at] + piece)
        return carry

    lax.fori_loop(0, GROUPS, step, 0)
    taps = [None] * 9
    for slot in range(16):
        for out in range(4):
            tap = tap_of(slot, out)
            if tap is not None:
                piece = acc[out * 64 : (out + 1) * 64, slot * 64 : (slot + 1) * 64]
                taps[tap] = piece if taps[tap] is None else taps[tap] + piece
    result = jnp.concatenate(taps, 1)
    if slot_out is None:
        out_ref[...] = result.astype(bf16)
    else:
        width = piece_ref.shape[1]
        for j in range(piece_ref.shape[0]):
            piece_ref[j] = result[j * width : (j + 1) * width].astype(bf16)
        copy = pltpu.make_async_copy(piece_ref, out_ref.at[:, slot_out], piece_sem)
        copy.start()
        copy.wait()


def stem_back_kernel(
    dy_far, c_far, z_ref, sums_ref, gath_ref, norm_ref, mask_ref, table_ref, conv_ref, head_ref,
    *refs
):
    stat_refs, (out_ref, dy_ref, held, raw, sems) = refs[:7], refs[7:]
    loads = Streams([dy_far, c_far], [dy_ref, held], sems, 0, NI)
    for k in range(NJ // NI):
        loads.start_load(k)
    rows = held.shape[2]
    counted = pixels_of(gath_ref)
    slope, along, start = grad_constants(sums_ref, gath_ref, counted, norm_ref, 0)
    span = 2 * NI
    deep = (span + 2) * 4
    for block in range(NJ // NI):
        loads.wait_load(block)
        for s in range(NI):
            at = (block * (span + 2) + 2 * s) * deep
            pieces = []
            for j in range(NI):
                J = block * NI + j
                mask = twice(mask_ref[0 if J < SHORT_J else 1, 0 if s == 0 else 1])
                grad = dy_ref[s, J].astype(f32) * slope + held[s, J].astype(f32) * along
                pieces.append(((grad + start) * mask).astype(bf16))
            piece = jnp.dot(
                z_ref[at : at + 4 * deep][:, :rows],
                jnp.concatenate(pieces, 1),
                preferred_element_type=f32,
            )
            if block == 0 and s == 0:
                raw[...] = piece
            else:
                raw[...] += piece
    parts = [raw[:, k * 64 : (k + 1) * 64].astype(bf16) for k in range(NI * 4)]
    total = lax.dot_general(
        jnp.concatenate(parts, 0),
        table_ref[...].reshape(NI * 4 * 4 * deep, 32),
        (((0,), (0,)), ((), ())),
        preferred_element_type=f32,
    )
    stats = jnp.concatenate([ref[0:1] if len(ref.shape) == 2 else ref[0, 0:1] for ref in stat_refs], 0)
    shifts, gains = stats[:, :64], stats[:, 64:]
    norms = jnp.concatenate([gains, shifts, jnp.zeros((2, 64), f32)], 0).T
    head = head_ref[:, :64].T
    extra = jnp.concatenate([total[:, :27], norms[:, :14], head[:, :23]], 1)
    out_ref[...] = jnp.concatenate([conv_ref[...].astype(f32), extra], 1).astype(bf16)


def chain_kernel(
    early_ref, last_ref, noise_ref, conv_ref, stem_ref, head_ref, conv_out, extra_out,
    square_ref, *, devices
):
    count, width = early_ref.shape[0], early_ref.shape[2]
    narrow = devices // count
    member = lax.axis_index("wide")

    def partial(w):
        last = tree(last_ref[w * narrow + n].astype(f32) for n in range(narrow))
        return [last[:, :576]] + [early_ref[w, k].astype(f32) for k in range(5)], last[:, 576:]

    def place(k):
        return lax.rem(member + k, count)

    def hop(k, carried):
        conv, extra = carried
        top = jnp.max(jnp.abs(extra), keepdims=True)
        for piece in conv:
            top = jnp.maximum(top, jnp.max(jnp.abs(piece), keepdims=True))
        scale = top + 1e-06
        sender = place(k)
        more, more_extra = partial(place(k + 1))

        def passed(value, dither, added):
            level = (value / scale * levels + dither.astype(f32)).astype(bf16)
            return level.astype(f32) * scale / levels + added

        conv = [passed(conv[m], noise_ref[sender, m], more[m]) for m in range(6)]
        dither = noise_ref[sender, 6][:, :64]
        known = lax.broadcasted_iota(jnp.int32, extra.shape, 1) < 41 + head_ref.shape[1]
        return conv, jnp.where(known, passed(extra, dither, more_extra), 0.0)

    conv, extra = lax.fori_loop(1, count, hop, partial(place(1)))
    head = head_ref[...]
    masters = jnp.concatenate(
        [
            stem_ref[...], jnp.zeros((width, 14), f32), head,
            jnp.zeros((width, 64 - 41 - head.shape[1]), f32),
        ],
        1,
    )
    extra = extra + weight_decay * masters
    total = jnp.sum(extra * extra, keepdims=True)
    for m in range(6):
        value = conv[m] + weight_decay * conv_ref[m]
        conv_out[m] = value
        total = total + jnp.sum(value * value, keepdims=True)
    extra_out[...] = jnp.concatenate([extra, extra], 1)
    square_ref[...] = jnp.broadcast_to(total, square_ref.shape)


def adam_kernel(square_ref, heads_ref, first_ref, conv_ref, extra_ref, *refs, classes):
    news, held, sems = refs[15:33], refs[33:48], refs[48]
    copies = [pltpu.make_async_copy(refs[k], held[k], sems.at[k]) for k in range(15)]
    for copy in copies:
        copy.start()
    olds = held
    bias = jnp.sum(heads_ref[:, 1, :], 0, keepdims=True)
    loss = bias[:, 127:128]
    bias = bias[:, :classes]
    total = jnp.sum(square_ref[...][:, 0:1], 0, keepdims=True)
    total = total + jnp.sum(bias * bias, keepdims=True)
    norm = jnp.sqrt(total)
    factor = clip_limit / jnp.maximum(norm, clip_limit)
    extra = extra_ref[...]
    turned = extra.T
    parts = (
        (extra[:, :27],), tuple(conv_ref[m] for m in range(6)),
        (turned[27:34], turned[34:41]), (extra[:, 41 : 41 + classes],), (bias,),
    )
    for copy in copies:
        copy.wait()
    for k, pieces in enumerate(parts):
        master, first, second = olds[3 * k : 3 * k + 3]
        for m, gradient in enumerate(pieces):
            at = {6: (m,), 2: (slice(None), m)}.get(len(pieces), ())
            results = adam_update(gradient, first[at], second[at], master[at], factor)
            for ref, value in zip(news[3 * k : 3 * k + 3], results):
                ref[at] = value
    news[15][...] = norm
    news[16][...] = loss
    news[17][...] = jnp.sum(first_ref[:, 1, 1:2], 0, keepdims=True)


def stem_table():
    span = 2 * NI + 2
    table = np.zeros((NI * 4, 4, span, 4, 27), np.float32)
    for j in range(NI):
        for out in range(4):
            for ky in range(3):
                for kx in range(3):
                    for i in range(3):
                        table[
                            j * 4 + out, out // 2 + ky, 2 * j + out % 2 + kx, i,
                            (ky * 3 + kx) * 3 + i,
                        ] = 1.0
    return np.pad(table.reshape(NI * 4, 4 * span * 4, 27), ((0, 0), (0, 0), (0, 5)))


def adam_update(gradient, first, second, master, factor):
    clipped = gradient * factor
    new_first = first_decay * first + (1.0 - first_decay) * clipped
    new_second = second_decay * second + (1.0 - second_decay) * clipped * clipped
    corrected = (
        new_first
        / (1.0 - first_decay**STEP)
        / (jnp.sqrt(new_second / (1.0 - second_decay**STEP)) + adam_epsilon)
    )
    return (master - learn_rate * (corrected + decoupled * master), new_first, new_second)


def shared(rows):
    return lax.all_to_all(rows, BOTH, 0, 0, tiled=True)


def body(
    images,
    large_flag,
    labels,
    example_weights,
    cycle_noise,
    stem_weight,
    conv_weight,
    norm_params,
    head_weight,
    head_bias,
    stem_first,
    stem_second,
    conv_first,
    conv_second,
    norm_first,
    norm_second,
    head_first,
    head_second,
    bias_first,
    bias_second,
):
    wide_count = lax.axis_size("wide")
    devices = wide_count * lax.axis_size("narrow")
    count = large_flag.shape[0]
    rows = QUARTERS * count
    width = stem_weight.shape[0]
    channels = width * wide_count
    classes = head_weight.shape[0]
    assert channels == 64 and rows % 16 == 0 and rows <= 128

    member = lax.axis_index("wide")

    def to_wide(value):
        return lax.all_to_all(value, "wide", 0, 0, tiled=True)

    owned = (stem_weight, conv_weight, norm_params.transpose(1, 0, 2), head_weight.T)
    packed = call(
        pack_kernel,
        (jax.ShapeDtypeStruct((wide_count, 7, width, 576), bf16),),
        [pltpu.VMEM(value.shape, f32) for value in owned] + [pltpu.SemaphoreType.DMA((4,))],
        owned,
        "pack",
        stored=(0, 1, 2, 3),
        limit=8,
    )[0]
    packed = to_wide(packed)
    bias_row = jnp.pad(head_bias[None, :], ((0, 0), (0, 128 - classes)))

    dither = ((cycle_noise[0].astype(f32) + 0.5) / 65536.0 - 0.5).astype(bf16)
    hop_row = (member - 1 - jnp.arange(wide_count, dtype=jnp.int32)) % wide_count
    dither = jnp.take(dither, jnp.minimum(hop_row, wide_count - 2), axis=0)
    one, two, three = width * 27, width * 27 + 6 * width * 576, width * 41 + 6 * width * 576
    extra = jnp.concatenate(
        [
            dither[:, :one].reshape(wide_count, width, 27),
            dither[:, two:three].reshape(wide_count, 14, width).transpose(0, 2, 1),
            dither[:, three:].reshape(wide_count, classes, width).transpose(0, 2, 1),
        ],
        2,
    )
    extra = jnp.pad(extra, ((0, 0), (0, 0), (0, 576 - extra.shape[2])))
    dither = jnp.concatenate(
        [dither[:, one:two].reshape(wide_count, 6, width, 576), extra[:, None]], 1
    )

    large = large_flag == 1
    row_large = jnp.repeat(large, QUARTERS)
    quarter = jnp.arange(rows, dtype=jnp.int32) % QUARTERS
    upper = row_large | (quarter < SHORT_J // NI)
    ones = jnp.ones((rows,), bool)
    none = jnp.zeros((rows,), bool)
    mask_table = jnp.stack(
        [jnp.stack([ones, upper]), jnp.stack([row_large, row_large]), jnp.stack([none, none])]
    )
    mask_table = jnp.broadcast_to(mask_table[..., None], (3, 2, rows, 128)).astype(f32)
    q_table = jnp.broadcast_to(
        jnp.stack([quarter != QUARTERS - 1, quarter != 0])[..., None], (2, rows, 128)
    ).astype(f32)
    sides = jnp.where(large, SIDE, SHORT).astype(jnp.int32)
    weights_f = example_weights.astype(f32)
    lane = jnp.arange(128, dtype=jnp.int32)[None, :]
    info = jnp.where(
        lane == 0,
        jnp.repeat((sides * sides).astype(f32), QUARTERS)[:, None],
        jnp.where(lane == 1, jnp.repeat(weights_f, QUARTERS)[:, None], 0.0),
    )
    hot = (jnp.repeat(labels, QUARTERS)[:, None] == lane).astype(f32)

    span = 2 * NI
    position = jnp.arange(span * SIDE, dtype=jnp.int32)
    inside = row_large[:, None] | (
        (quarter[:, None] * span + (position // SIDE)[None, :] < SHORT)
        & ((position % SIDE)[None, :] < SHORT)
    )
    planes = images.reshape(3, rows, span * SIDE) * inside.astype(bf16)[None]

    (planes, mask_table, info, hot, bias_row, dither, packed) = lax.optimization_barrier(
        (planes, mask_table, info, hot, bias_row, dither, packed)
    )
    dither = to_wide(dither)
    table = jnp.asarray(stem_table(), bf16)
    norm4, into_head, from_head, stem_wide = call(
        small_kernel,
        (
            jax.ShapeDtypeStruct((16, LANES), f32),
            jax.ShapeDtypeStruct((128, 128), bf16),
            jax.ShapeDtypeStruct((128, LANES), bf16),
            jax.ShapeDtypeStruct((table.shape[1], NI * LANES), bf16),
        ),
        [],
        (packed, table),
        "small",
        limit=12,
    )
    matrices = call(
        weights_kernel,
        (Stored((1024, LANES)),) * 12,
        [pltpu.VMEM((12, 1024, LANES), bf16), pltpu.SemaphoreType.DMA((12,))],
        (packed,),
        "weights",
        limit=16,
    )

    z_rows = (SIDE // span) * (span + 2) * (span + 2) * 4
    full = pltpu.VMEM((NI, NJ, rows, LANES), bf16)
    side_shape = (UNROLL, NI + 2, rows, LANES)
    sets = [
        pltpu.VMEM((BLOCK + 2, NI + 2, rows, LANES), bf16),
        pltpu.VMEM((BLOCK, NI + 2, rows, LANES), bf16),
        pltpu.VMEM((BLOCK * NI * rows, LANES), f32),
    ] * 2
    stat = jax.ShapeDtypeStruct((devices, 128), f32)

    c0_saved, z, stat0 = call(
        functools.partial(stem_kernel, devices=devices),
        (
            stored_field(rows),
            jax.ShapeDtypeStruct((z_rows, 128), bf16),
            jax.ShapeDtypeStruct((devices, 2, 128), f32),
        ),
        [pltpu.VMEM((z_rows, 128), f32), full, pltpu.SemaphoreType.DMA((SIDE // span,))],
        (planes, stem_wide, mask_table, info),
        "stem",
    )
    current, saved = c0_saved, [c0_saved]
    early = jnp.zeros((wide_count, 4, width, 576), bf16)
    stat0, norm4, into_head, from_head, dither, early, *matrices = lax.optimization_barrier(
        (stat0, norm4, into_head, from_head, dither, early, *matrices)
    )
    gathered = [shared(stat0)]
    stream, streams = None, []
    ahead, back = matrices[:6], matrices[6:]
    for layer in range(1, 7):
        keep = layer % 2 == 1
        residual = keep and layer > 1
        args = (current,) + ((stream,) if residual else ())
        args += (gathered[layer - 1], gathered[0], norm4, mask_table, q_table, ahead[layer - 1])
        outs = call(
            functools.partial(
                forward_kernel, index=layer - 1, keep=keep, residual=residual,
                streamed=layer == 1, devices=devices,
            ),
            (field(rows), stored_field(rows)) * (2 if keep else 1) + (stat,),
            [
                pltpu.VMEM((2, BLOCK, 8, LANES), f32),
                pltpu.SemaphoreType.DMA((2, CHUNKS)),
            ]
            + sets
            + ([full, pltpu.SemaphoreType.DMA((1, CHUNKS))] if layer == 1 else []),
            args,
            "forward",
            cost=int(7e9),
            limit=24,
            stored=(0,) if layer == 1 else (),
        )
        current = outs[0]
        saved.append(outs[1])
        if keep:
            stream = outs[2]
            streams.append(outs[3])
        gathered.append(shared(outs[-1]))

    dys = [None] * 7
    stats = [None] * 7
    dys[6], stats[6], head_grad = call(
        functools.partial(head_kernel, classes=classes, devices=devices),
        (
            stored_field(rows),
            jax.ShapeDtypeStruct((devices, 2, 128), f32),
            jax.ShapeDtypeStruct((128, 128), f32),
        ),
        [
            pltpu.VMEM((NI, NJ, rows, LANES), f32),
            pltpu.VMEM((rows, LANES), f32),
            pltpu.VMEM((NI, NJ, rows, LANES), bf16),
            pltpu.SemaphoreType.DMA((1, CHUNKS)),
        ],
        (
            current, stream, gathered[6], gathered[0], norm4, mask_table, hot, info,
            into_head, from_head, bias_row,
        ),
        "head",
        cost=int(8e9),
        limit=28,
    )
    tokens = ()
    for layer in range(6, 0, -1):
        residual = layer in (5, 3)
        adding = layer % 2 == 1
        sums = shared(stats[layer])
        if layer == 6:
            heads = sums
        args = (dys[layer], saved[layer], saved[layer - 1])
        args += (streams[layer // 2 - 1],) if residual else ()
        args += (dys[layer + 1],) if adding else ()
        inputs = len(args)
        args += (
            sums, gathered[layer], gathered[layer - 1], gathered[0], norm4, mask_table, q_table,
            back[layer - 1], *tokens,
        )
        dys[layer - 1], grad, value, stats[layer - 1] = call(
            functools.partial(
                backward_kernel, index=layer, residual=residual, adding=adding,
                ordered=len(tokens), devices=devices,
            ),
            (stored_field(rows),) * 3 + (stat,),
            [
                pltpu.VMEM((UNROLL + 2, NI + 2, rows, LANES), bf16),
                pltpu.VMEM(side_shape, bf16),
                pltpu.VMEM((3, 2, rows, LANES), f32),
                pltpu.VMEM((2, UNROLL, 8, LANES), f32),
                pltpu.SemaphoreType.DMA((8, GROUPS)),
                pltpu.VMEM((1024, LANES), bf16),
                pltpu.SemaphoreType.DMA,
            ]
            + [full] * (3 + inputs),
            args,
            "backward",
            cost=int(8e9),
            limit=46,
            stored=tuple(range(inputs)) + (inputs + 7,),
        )
        slot_out = layer - 3 if layer > 2 else None
        args = (grad, value, q_table)
        outs = (jax.ShapeDtypeStruct((64, 576), bf16), jax.ShapeDtypeStruct((8, 128), f32))
        aliases = {}
        if layer > 2:
            aliases[len(args)] = 0
            args += (early,)
            outs = (Stored(early.shape), outs[1])
        result, token = call(
            functools.partial(weight_grad_kernel, slot_out=slot_out),
            outs,
            [
                pltpu.VMEM((UNROLL + 2, NI + 2, rows, LANES), bf16),
                pltpu.VMEM(side_shape, bf16),
                pltpu.VMEM((LANES, 1024), f32),
                full,
                full,
                pltpu.SemaphoreType.DMA((2, CHUNKS)),
                pltpu.VMEM((wide_count, width, 576), bf16),
                pltpu.SemaphoreType.DMA,
            ],
            args,
            "weight_grad",
            cost=int(7e9),
            limit=24,
            stored=(0, 1) + tuple(range(3, len(args))),
            aliases=aliases,
        )
        tokens = (token,)
        if layer > 2:
            early = result
        if layer == 3:
            early = lax.psum(early, "narrow")
        if layer == 2:
            late = lax.psum(result, "narrow").reshape(wide_count, 1, width, 576)
    early = to_wide(jnp.concatenate([late, early], 1))
    last = call(
        stem_back_kernel,
        (jax.ShapeDtypeStruct((64, 640), bf16),),
        [
            full,
            full,
            pltpu.VMEM((4 * (span + 2) * 4, NI * LANES), f32),
            pltpu.SemaphoreType.DMA((2, NJ // NI)),
        ],
        (
            dys[0], saved[0], z, shared(stats[0]), gathered[0], norm4, mask_table, table,
            result, head_grad, *stats,
        ),
        "stem_back",
        stored=(0, 1),
        cost=int(5e9),
    )[0]
    narrow_count = devices // wide_count
    last = jnp.broadcast_to(
        last.reshape(wide_count, 1, width, 640), (wide_count, narrow_count, width, 640)
    )
    last = shared(last.reshape(devices, width, 640))
    conv_total, extra_total, squares = call(
        functools.partial(chain_kernel, devices=devices),
        (
            jax.ShapeDtypeStruct((6, width, 576), f32),
            jax.ShapeDtypeStruct((width, 128), f32),
            jax.ShapeDtypeStruct((wide_count, 128), f32),
        ),
        [],
        (early, last, dither, conv_weight, stem_weight, head_weight.T),
        "chain",
    )
    olds = (
        stem_weight, stem_first, stem_second, conv_weight, conv_first, conv_second,
        *(value.transpose(1, 0, 2) for value in (norm_params, norm_first, norm_second)),
        head_weight.T, head_first.T, head_second.T,
        head_bias[None], bias_first[None], bias_second[None],
    )
    single = jax.ShapeDtypeStruct((1, 1), f32)
    news = call(
        functools.partial(adam_kernel, classes=classes),
        tuple(Result(old.shape, f32) for old in olds) + (single,) * 3,
        [pltpu.VMEM(old.shape, f32) for old in olds] + [pltpu.SemaphoreType.DMA((15,))],
        (to_wide(squares), heads, gathered[0], conv_total, extra_total, *olds),
        "adam",
        stored=tuple(range(5, 20)),
        limit=12,
    )
    return (
        *news[:6],
        *(new.transpose(1, 0, 2) for new in news[6:9]),
        *(new.T for new in news[9:12]),
        *(new[0] for new in news[12:15]),
        *(new[0, 0] for new in news[15:]),
    )


def solution(mesh):
    split = P(BOTH)
    ins = (
        P(None, BOTH), split, split, split, P("wide", None, None),
        P("wide", None), P(None, "wide", None), P(None, None, "wide"), P(None, "wide"), P(),
        P("wide", None), P("wide", None), P(None, "wide", None), P(None, "wide", None),
        P(None, None, "wide"), P(None, None, "wide"), P(None, "wide"), P(None, "wide"), P(), P(),
    )
    outs = (
        (P("wide", None),) * 3
        + (P(None, "wide", None),) * 3
        + (P(None, None, "wide"),) * 3
        + (P(None, "wide"),) * 3
        + (P(),) * 6
    )
    return jax.shard_map(body, mesh=mesh, in_specs=ins, out_specs=outs, check_vma=False)
```

```python
import functools

import jax
import jax.numpy as jnp
import numpy as np
from jax import lax
from jax.experimental import pallas as pl
from jax.experimental.pallas import tpu as pltpu
from jax.sharding import PartitionSpec as P

SIDE = 40
SHORT = 32
STEP = 10

norm_epsilon = 1e-05
clip_limit = 0.002
learn_rate = 0.4
first_decay = 0.9
second_decay = 0.999
adam_epsilon = 1e-08
weight_decay = 0.0005
decoupled = 0.01
levels = 15.0

QUARTERS = 4
PATCHES = SIDE // 2
NI = PATCHES // QUARTERS
NJ = PATCHES
SHORT_J = SHORT // 2
LANES = 256
UNROLL = 4
BLOCK = 2

f32 = jnp.float32
bf16 = jnp.bfloat16
BOTH = ("wide", "narrow")


def window_place(slot):
    group, sy, sx = slot // 4, (slot // 2) % 2, slot % 2
    wx = 1 + sx if group in (0, 2) else (3 if sx == 0 else 0)
    wy = 1 + sy if group in (0, 1) else (3 if sy == 0 else 0)
    return wy, wx


def tap_of(slot, out):
    wy, wx = window_place(slot)
    ky, kx = wy - out // 2, wx - out % 2
    if 0 <= ky < 3 and 0 <= kx < 3:
        return ky * 3 + kx
    return None


def whole():
    return pl.BlockSpec(memory_space=pltpu.VMEM)


def call(kernel, outs, scratch, args, name, cost=None, limit=24, stored=(), aliases=None):
    def place(out):
        return pl.BlockSpec(memory_space=pltpu.HBM) if type(out) is Stored else whole()

    def shape(out):
        kind = pltpu.HBM if isinstance(out, (Stored, Result)) else jax.ShapeDtypeStruct
        return kind(out.shape, out.dtype)

    args = [
        pltpu.with_memory_space_constraint(arg, pltpu.HBM) if k in stored else arg
        for k, arg in enumerate(args)
    ]

    return pl.pallas_call(
        kernel,
        out_shape=tuple(shape(out) for out in outs),
        in_specs=[
            pl.BlockSpec(memory_space=pltpu.HBM) if k in stored else whole()
            for k in range(len(args))
        ],
        out_specs=tuple(place(out) for out in outs),
        scratch_shapes=scratch,
        compiler_params=pltpu.CompilerParams(vmem_limit_bytes=limit * 2**20),
        name=name,
        input_output_aliases=aliases or {},
        cost_estimate=pl.CostEstimate(flops=cost, bytes_accessed=2**20, transcendentals=0)
        if cost
        else None,
    )(*args)


class Stored:
    def __init__(self, shape, dtype=bf16):
        self.shape, self.dtype = shape, dtype


class Result(Stored):
    pass


def stored_field(rows):
    return Stored((NI, NJ, rows, LANES))


class Streams:
    def __init__(self, outside, inside, sems, base, columns=None):
        self.outside, self.inside = tuple(outside), tuple(inside)
        self.sems, self.base, self.columns = sems, base, columns or BLOCK

    def pairs(self, i):
        for k, (far, near) in enumerate(zip(self.outside, self.inside)):
            at = pl.ds(i * self.columns, self.columns)
            yield far.at[:, at], near.at[:, at], self.sems.at[self.base + k, i]

    def when(self, condition, action, i):
        @pl.when(condition)
        def _():
            action(i)

    def start_load(self, i):
        for far, near, sem in self.pairs(i):
            pltpu.make_async_copy(far, near, sem).start()

    def wait_load(self, i):
        for far, near, sem in self.pairs(i):
            pltpu.make_async_copy(far, near, sem).wait()

    def wait_loads(self, i):
        self.wait_load(i)
        self.wait_load(i + 1)

    def start_save(self, i):
        for far, near, sem in self.pairs(i):
            pltpu.make_async_copy(near, far, sem).start()

    def wait_save(self, i):
        for far, near, sem in self.pairs(i):
            pltpu.make_async_copy(near, far, sem).wait()


CHUNKS = NJ // BLOCK
GROUPS = NJ // UNROLL


def field(rows):
    return jax.ShapeDtypeStruct((NI, NJ, rows, LANES), bf16)


def wide_pair(row):
    turned = pltpu.roll(row, 64, 1)
    lower = lax.broadcasted_iota(jnp.int32, row.shape, 1) < 64
    first = jnp.where(lower, row, turned)
    second = jnp.where(lower, turned, row)
    return jnp.concatenate([first, first], 1), jnp.concatenate([second, second], 1)


def folded(row):
    half = row[:, :128] + row[:, 128:]
    return half + pltpu.roll(half, 64, 1)


def message(first, second):
    lower = lax.broadcasted_iota(jnp.int32, (1, 128), 1) < 64
    return jnp.where(lower, folded(first), folded(second))


def totals(gathered):
    rows = gathered[:, 0, :] if len(gathered.shape) == 3 else gathered[...]
    return wide_pair(jnp.sum(rows, 0, keepdims=True))


def send(ref, first, second=None):
    if second is None:
        ref[...] = jnp.broadcast_to(first, ref.shape)
    else:
        both = jnp.concatenate([first, second], 0)[None]
        ref[...] = jnp.broadcast_to(both, ref.shape)


def norm_constants(gathered, counted, norm4, index):
    sums, squares = totals(gathered)
    mean = sums / counted
    scale = lax.rsqrt(squares / counted - mean * mean + norm_epsilon)
    gain = norm4[index : index + 1]
    slope = gain * scale
    return mean, scale, slope, norm4[7 + index : 8 + index] - mean * slope


def pixels_of(gathered_first):
    return jnp.sum(gathered_first[:, 1, 0:1], 0, keepdims=True)


def twice(tile):
    return jnp.concatenate([tile, tile], 1)


def mask_row(J):
    return jnp.where((J < 0) | (J >= NJ), 2, jnp.where(J < SHORT_J, 0, 1))


def put_column(ring, slot, s, value, low, q_ref):
    rows = value.shape[0]
    ring[slot, s + 1] = low
    if s == 0:
        ring[slot, NI + 1, :, :128] = (pltpu.roll(value[:, :128], rows - 1, 0) * q_ref[0]).astype(
            bf16
        )
    if s == NI - 1:
        ring[slot, 0, :, 128:] = (pltpu.roll(value[:, 128:], 1, 0) * q_ref[1]).astype(bf16)


def side_columns(ring, side, u, lanes):
    for s in range(NI + 2):
        if s == 0:
            side[u, s, :, 128:] = jnp.where(
                lanes[:, 128:], ring[u + 2, s, :, 128:], ring[u, s, :, 128:]
            )
        elif s == NI + 1:
            side[u, s, :, :128] = jnp.where(
                lanes[:, :128], ring[u + 2, s, :, :128], ring[u, s, :, :128]
            )
        else:
            side[u, s] = jnp.where(lanes, ring[u + 2, s], ring[u, s])


def operands(ring, side, u):
    rows = ring.shape[2]
    whole_rows = NI * rows
    last = NI + 2
    own = ring[u + 1, 1 : NI + 1].reshape(whole_rows, LANES)
    beside = side[u, 1 : NI + 1].reshape(whole_rows, LANES)
    above = jnp.concatenate(
        [ring[u + 1, 2:last, :, :128], ring[u + 1, 0:NI, :, 128:]], -1
    ).reshape(whole_rows, LANES)
    corner = jnp.concatenate([side[u, 2:last, :, :128], side[u, 0:NI, :, 128:]], -1).reshape(
        whole_rows, LANES
    )
    return own, beside, above, corner


def product(parts, w_ref):
    total = jnp.dot(parts[0], w_ref[0:LANES], preferred_element_type=f32)
    for k in range(1, 4):
        total += jnp.dot(
            parts[k], w_ref[k * LANES : (k + 1) * LANES], preferred_element_type=f32
        )
    return total


def tree(values):
    values = list(values)
    while len(values) > 1:
        paired = [a + b for a, b in zip(values[::2], values[1::2])]
        values = paired + values[len(values) - len(values) % 2 :]
    return values[0]


def by_eight(value):
    return tree(value[k : k + 8] for k in range(0, value.shape[0], 8))


def summed(tiles):
    low = tree(tiles)
    low = tree(low[k : k + 16] for k in range(0, low.shape[0], 16))
    return by_eight(low.astype(f32))


def total_of(sums, which):
    return jnp.sum(tree(sums[which, u] for u in range(sums.shape[1])), 0, keepdims=True)


def pipeline(sets, activate, finish, matrix, lanes, before, after):
    def ready(block, own, other):
        ring, side, _ = own
        if other is None:
            ring[0] = jnp.zeros(ring.shape[1:], bf16)
            activate(0, ring, 1)
        else:
            ring[0] = other[0][BLOCK]
            ring[1] = other[0][BLOCK + 1]
        for u in range(BLOCK):
            activate(block * BLOCK + u + 1, ring, u + 2)
        for u in range(BLOCK):
            side_columns(ring, side, u, lanes)

    def multiply(own):
        ring, side, result = own
        parts = [operands(ring, side, u) for u in range(BLOCK)]
        result[...] = product(
            [jnp.concatenate([part[k] for part in parts], 0) for k in range(4)], matrix
        )

    def step(j, carry):
        for half in range(2):
            own, other = sets[half], sets[1 - half]
            block = 2 * j + half
            if half == 0:
                before(block)
            multiply(own)
            for u in range(BLOCK):
                finish((block - 1) * BLOCK + u, other, u)
            ready(block + 1, other, own)
            after(block)
        return carry

    sets[1][2][...] = jnp.zeros(sets[1][2].shape, f32)
    ready(0, sets[0], None)

    def tail():
        for u in range(BLOCK):
            finish(NJ - BLOCK + u, sets[1], u)

    return step, tail


def half_lanes(rows):
    return lax.broadcasted_iota(jnp.int32, (rows, LANES), 1) % 128 < 64


def pack_kernel(*refs):
    out_ref, held, sems = refs[4], refs[5:9], refs[9]
    copies = [pltpu.make_async_copy(refs[k], held[k], sems.at[k]) for k in range(4)]
    for copy in copies:
        copy.start()
    for copy in copies:
        copy.wait()
    stem_ref, conv_ref, norm_ref, head_ref = held
    width = stem_ref.shape[0]
    gains = [norm_ref[:, k, :].T for k in range(2)]
    head = head_ref[...]
    used = 27 + 14 + head.shape[1]
    small = jnp.concatenate(
        [stem_ref[...], *gains, head, jnp.zeros((width, 128 - used), f32)], 1
    )
    high = small.astype(bf16)
    rest = small - high.astype(f32)
    middle = rest.astype(bf16)
    low = (rest - middle.astype(f32)).astype(bf16)
    tail = jnp.concatenate([high, middle, low, jnp.zeros((width, 192), bf16)], 1)
    for w in range(out_ref.shape[0]):
        for layer in range(6):
            out_ref[w, layer] = conv_ref[layer].astype(bf16)
        out_ref[w, 6] = tail


def weights_kernel(packed_ref, *refs):
    outs, (held, sems) = refs[:12], refs[12:]
    copies = []
    for layer in range(6):
        matrix = jnp.concatenate(
            [packed_ref[w, layer].astype(f32) for w in range(packed_ref.shape[0])], 0
        )
        turned = matrix.T
        empty = jnp.zeros((64, 64), f32)
        for slot in range(16):
            ahead, back = [], []
            for out in range(4):
                tap = tap_of(slot, out)
                if tap is None:
                    ahead.append(empty)
                    back.append(empty)
                else:
                    other = 8 - tap
                    ahead.append(turned[tap * 64 : (tap + 1) * 64])
                    back.append(matrix[:, other * 64 : (other + 1) * 64])
            at = slice(slot * 64, (slot + 1) * 64)
            held[layer, at] = jnp.concatenate(ahead, 1).astype(bf16)
            held[6 + layer, at] = jnp.concatenate(back, 1).astype(bf16)
        for k in (layer, 6 + layer):
            copies.append(pltpu.make_async_copy(held.at[k], outs[k], sems.at[k]))
            copies[-1].start()
    for copy in copies:
        copy.wait()


def small_kernel(packed_ref, table_ref, norm_ref, into_ref, back_ref, stem_ref):
    count, _, width, _ = packed_ref.shape
    parts = [
        jnp.concatenate(
            [packed_ref[w, 6, :, k * 128 : (k + 1) * 128].astype(f32) for w in range(count)], 0
        )
        for k in range(3)
    ]
    turned = ((parts[0] + parts[1]) + parts[2]).T
    norms = turned[27:43]
    norm_ref[...] = jnp.concatenate([norms] * 4, 1)
    head = jnp.concatenate([turned[41:], jnp.zeros((41, 64), f32)], 0)
    back_ref[...] = jnp.concatenate([head] * 4, 1).astype(bf16)
    into_ref[...] = jnp.concatenate([head.T, jnp.zeros((64, 128), f32)], 0).astype(bf16)
    stem = turned[:32].astype(bf16)
    for k in range(table_ref.shape[0] // 2):
        pair = [
            jnp.dot(table_ref[2 * k + e], stem, preferred_element_type=f32) for e in range(2)
        ]
        stem_ref[:, k * 128 : (k + 1) * 128] = jnp.concatenate(pair, 1).astype(bf16)


def stem_kernel(
    planes_ref, w_ref, mask_ref, info_ref, save_ref, z_ref, stat_ref, zf, out_ref, sems, *, devices
):
    rows = planes_ref.shape[1]
    zf[...] = jnp.zeros_like(zf)
    span = 2 * NI
    blocks = SIDE // span
    deep = (span + 2) * 4
    for i in range(3):
        turned = planes_ref[i].astype(f32).T
        for block in range(blocks):
            first = max(block * span - 1, 0)
            last = min(block * span + span + 1, SIDE)
            skip = first - (block * span - 1)
            for y in range(span):
                base = (block * (span + 2) + y + 1) * deep + skip * 4 + i
                zf[pl.ds(base, last - first, stride=4), :rows] = turned[
                    y * SIDE + first : y * SIDE + last
                ]
    lane = lax.broadcasted_iota(jnp.int32, (deep, 128), 1)
    for block in range(blocks):
        at = block * (span + 2) * deep
        low = zf[at + span * deep : at + (span + 1) * deep]
        zf[at : at + deep] = jnp.where(lane % 4 == 0, 0.0, pltpu.roll(low, 1, 1))
        high = zf[at + deep : at + 2 * deep]
        zf[at + (span + 1) * deep : at + (span + 2) * deep] = jnp.where(
            lane % 4 == 3, 0.0, pltpu.roll(high, 127, 1)
        )
    z_ref[...] = zf[...].astype(bf16)
    first_sum = jnp.zeros((8, LANES), f32)
    second_sum = jnp.zeros((8, LANES), f32)
    copies = []
    for block in range(blocks):
        for s in range(NI):
            at = (block * (span + 2) + 2 * s) * deep
            result = lax.dot_general(
                z_ref[at : at + 4 * deep],
                w_ref[...],
                (((0,), (0,)), ((), ())),
                preferred_element_type=f32,
            )
            for j in range(NI):
                J = block * NI + j
                mask = mask_ref[0 if J < SHORT_J else 1, 0 if s == 0 else 1]
                tile = result[:rows, j * LANES : (j + 1) * LANES] * twice(mask)
                out_ref[s, J] = tile.astype(bf16)
                first_sum += by_eight(tile)
                second_sum += by_eight(tile * tile)
        at = pl.ds(block * NI, NI)
        copies.append(pltpu.make_async_copy(out_ref.at[:, at], save_ref.at[:, at], sems.at[block]))
        copies[-1].start()
    row = message(
        jnp.sum(first_sum, 0, keepdims=True), jnp.sum(second_sum, 0, keepdims=True)
    )
    counts = jnp.sum(info_ref[...], 0, keepdims=True) * (1.0 / QUARTERS)
    send(stat_ref, row, counts)
    for copy in copies:
        copy.wait()


def forward_kernel(*refs, index, keep, residual, streamed, devices):
    refs = list(refs)
    c_ref = refs.pop(0)
    if streamed:
        matrix_sem, matrix, load_sems, held = (refs.pop() for _ in range(4))
        loads = Streams([c_ref], [held], load_sems, 0)
        for i in range(CHUNKS):
            loads.start_load(i)
        c_ref = held
    res_ref = refs.pop(0) if residual else None
    gath_ref, first_ref, norm_ref, mask_ref, q_ref, w_ref, out_ref, save_ref = refs[:8]
    refs = refs[8:]
    keep_ref = refs.pop(0) if keep else None
    keep_save_ref = refs.pop(0) if keep else None
    stat_ref, sums, sems = refs[:3]
    if streamed:
        fetch = pltpu.make_async_copy(w_ref, matrix, matrix_sem)
        fetch.start()
        w_ref = matrix
    sets = refs[3:6], refs[6:9]
    rows = c_ref.shape[2]
    counted = pixels_of(first_ref)
    _, _, slope, start = norm_constants(gath_ref, counted, norm_ref, index)
    half_slope, half_start = slope * 0.5, start * 0.5
    lanes = half_lanes(rows)
    sums[...] = jnp.zeros_like(sums)

    def activate(J, ring, slot):
        Jc = jnp.minimum(J, NJ - 1)
        jm = mask_row(J)
        for s in range(NI):
            half = c_ref[s, Jc].astype(f32) * half_slope + half_start
            if residual:
                half = half + 0.5 * res_ref[s, Jc].astype(f32)
            mask = mask_ref[jm, 0 if s == 0 else 1]
            value = (half + half * jnp.tanh(half)) * twice(mask)
            low = value.astype(bf16)
            put_column(ring, slot, s, value, low, q_ref)

    def finish(J, own, u):
        Jc = jnp.maximum(J, 0)
        jm = mask_row(J)
        tiles = []
        for s in range(NI):
            tile = own[2][(u * NI + s) * rows : (u * NI + s + 1) * rows]
            low = (tile * twice(mask_ref[jm, 0 if s == 0 else 1])).astype(bf16)
            out_ref[s, Jc] = low
            if keep:
                keep_ref[s, Jc] = own[0][u + 1, s + 1]
            tiles.append(low)
        sums[0, u] += summed(tiles)
        sums[1, u] += summed([tile * tile for tile in tiles])

    def before(block):
        if streamed:
            loads.when(block + 2 < CHUNKS, loads.wait_loads, block + 2)

    def after(block):
        saves.when(block > 0, saves.start_save, block - 1)

    saves = Streams([save_ref, keep_save_ref][: 1 + keep], [out_ref, keep_ref][: 1 + keep], sems, 0)
    if keep:
        sets[1][0][...] = jnp.zeros(sets[1][0].shape, bf16)
    if streamed:
        loads.wait_load(0)
        loads.wait_load(1)
    step, tail = pipeline(sets, activate, finish, w_ref, lanes, before, after)
    if streamed:
        fetch.wait()
    lax.fori_loop(0, CHUNKS // 2, step, 0)
    tail()
    saves.start_save(CHUNKS - 1)
    row = message(total_of(sums, 0), total_of(sums, 1))
    send(stat_ref, row)
    for i in range(CHUNKS):
        saves.wait_save(i)


def head_kernel(
    c_ref, res_ref, gath_ref, first_ref, norm_ref, mask_ref, hot_ref, info_ref, into_ref, back_ref,
    bias_ref, dy_save_ref, stat_ref, head_ref, grads, pool, dy_ref, sems, *, classes, devices
):
    rows = c_ref.shape[2]
    counted = pixels_of(first_ref)
    weight_total = jnp.sum(first_ref[:, 1, 1:2], 0, keepdims=True)
    mean, scale, slope, start = norm_constants(gath_ref, counted, norm_ref, 6)
    half_slope, half_start = slope * 0.5, start * 0.5
    pool[...] = jnp.zeros_like(pool)

    def gather(i, carry):
        values = []
        for u in range(UNROLL):
            J = i * UNROLL + u
            jm = mask_row(J)
            for s in range(NI):
                half = c_ref[s, J].astype(f32) * half_slope + half_start
                half = half + 0.5 * res_ref[s, J].astype(f32)
                sigma = (0.5 + 0.5 * jnp.tanh(half)) * twice(mask_ref[jm, 0 if s == 0 else 1])
                value = (half + half) * sigma
                values.append(value)
                grads[s, J] = sigma + value - value * sigma
        pool[...] += tree(values)
        return carry

    lax.fori_loop(0, GROUPS, gather, 0)
    pooled = pool[...]
    row_index = lax.broadcasted_iota(jnp.int32, (rows, LANES), 0)
    pooled = pooled + jnp.where(
        row_index % 2 == 0, pltpu.roll(pooled, rows - 1, 0), pltpu.roll(pooled, 1, 0)
    )
    pooled = pooled + jnp.where(
        row_index % 4 < 2, pltpu.roll(pooled, rows - 2, 0), pltpu.roll(pooled, 2, 0)
    )
    half_pool = pooled[:, :128] + pooled[:, 128:]
    half_pool = half_pool + pltpu.roll(half_pool, 64, 1)
    count = info_ref[:, 0:1]
    weight = info_ref[:, 1:2]
    pooled_low = (half_pool / count).astype(bf16)
    logits = jnp.dot(pooled_low, into_ref[...], preferred_element_type=f32) + bias_ref[...]
    lane = lax.broadcasted_iota(jnp.int32, logits.shape, 1)
    inside = lane < classes
    top = jnp.max(jnp.where(inside, logits, -jnp.inf), 1, keepdims=True)
    shifted = jnp.where(inside, logits - top, 0.0)
    powers = jnp.where(inside, jnp.exp(shifted), 0.0)
    sum_powers = jnp.sum(powers, 1, keepdims=True)
    hot = hot_ref[...]
    losses = jnp.log(sum_powers) - jnp.sum(hot * shifted, 1, keepdims=True)
    single = (lax.broadcasted_iota(jnp.int32, (rows, 1), 0) % QUARTERS == 0).astype(f32)
    loss = jnp.sum(losses * weight * single, 0, keepdims=True)
    grad_low = ((weight / weight_total) * (powers / sum_powers - hot)).astype(bf16)
    grad_once = grad_low * single.astype(bf16)
    bias_grad = jnp.sum(grad_once.astype(f32), 0, keepdims=True)
    head_ref[...] = lax.dot_general(
        grad_once, pooled_low, (((0,), (0,)), ((), ())), preferred_element_type=f32
    )
    extra = jnp.where(lax.broadcasted_iota(jnp.int32, (1, 128), 1) == 127, loss, bias_grad)
    spread = jnp.dot(grad_low, back_ref[...], preferred_element_type=f32) / count

    out = Streams([dy_save_ref], [dy_ref], sems, 0)

    def scatter(i, carry):
        first_sum, second_sum = carry
        for u in range(UNROLL):
            J = i * UNROLL + u
            for s in range(NI):
                dy = spread * grads[s, J]
                dy_ref[s, J] = dy.astype(bf16)
                first_sum += by_eight(dy)
                second_sum += by_eight(dy * c_ref[s, J].astype(f32))
        out.start_save(2 * i)
        out.start_save(2 * i + 1)
        return first_sum, second_sum

    zero = jnp.zeros((8, LANES), f32)
    first_sum, second_sum = lax.fori_loop(0, GROUPS, scatter, (zero, zero))
    first_sum = jnp.sum(first_sum, 0, keepdims=True)
    second_sum = (jnp.sum(second_sum, 0, keepdims=True) - mean * first_sum) * scale
    send(stat_ref, message(first_sum, second_sum), extra)
    for i in range(CHUNKS):
        out.wait_save(i)


def pieces_of(row):
    high = row.astype(bf16).astype(f32)
    middle = (row - high).astype(bf16).astype(f32)
    low = row - high - middle
    return [part[:, at : at + 64] for part in (high, middle, low) for at in (0, 64)]


def carried_lanes(width):
    return 576 + 64 * (-(-6 // width))


def carry(ref, weights, row, narrow):
    width = ref.shape[1]
    pieces = pieces_of(row)
    pieces += [jnp.zeros((1, 64), f32)] * (-len(pieces) % width)
    tail = [
        jnp.concatenate(pieces[at : at + width], 0) for at in range(0, len(pieces), width)
    ]
    for j in range(ref.shape[0] // narrow):
        rows = weights[j * width : (j + 1) * width]
        block = jnp.concatenate([rows, *tail], 1).astype(bf16)
        for n in range(narrow):
            ref[j * narrow + n] = block


def carried_totals(ref):
    width = ref.shape[1]
    total = tree(ref[d][:, 576:].astype(f32) for d in range(ref.shape[0]))
    found = [
        total[k % width : k % width + 1, 64 * (k // width) : 64 * (k // width) + 64]
        for k in range(6)
    ]
    halves = [found[k] + found[k + 2] + found[k + 4] for k in range(2)]
    return tuple(jnp.concatenate([half] * 4, 1) for half in halves)


def grad_constants(sums_ref, gath_ref, counted, norm4, index):
    first_total, second_total = sums_ref if isinstance(sums_ref, tuple) else totals(sums_ref)
    mean, scale, slope, _ = norm_constants(gath_ref, counted, norm4, index)
    along = -slope * scale * second_total / counted
    return slope, along, -slope * first_total / counted - along * mean


def backward_kernel(*refs, index, residual, adding, ordered, carrying, devices):
    inputs = 3 + residual + adding
    far_in, refs = refs[:inputs], refs[inputs:]
    refs = refs[:8] + refs[8 + ordered :]
    if carrying:
        weights_ref, carried_ref = refs[8], refs[13]
        refs = refs[:8] + refs[9:13] + refs[14:]
    (
        sums_ref, gath_ref, gath_prev_ref, first_ref, norm_ref, mask_ref, q_ref, w_ref,
        out_far, grad_far, value_far, stat_ref, ring, side, offsets, sums, sems, matrix,
        matrix_sem, out_ref, grad_ref, value_ref,
    ) = refs[:22]
    held = list(refs[22:])
    loads = Streams(far_in, held, sems, 0, UNROLL)
    saves = Streams([out_far, grad_far, value_far], [out_ref, grad_ref, value_ref], sems, inputs, UNROLL)
    loads.start_load(0)
    fetch = pltpu.make_async_copy(w_ref, matrix, matrix_sem)
    fetch.start()
    for i in range(1, GROUPS):
        loads.start_load(i)
    dy_ref = held.pop(0)
    c_ref, prev_ref = held[:2]
    res_ref = held[2] if residual else None
    add_ref = held[-1] if adding else None
    rows = c_ref.shape[2]
    counted = pixels_of(first_ref)
    grad_slope, grad_along, grad_start = grad_constants(
        sums_ref, gath_ref, counted, norm_ref, index
    )
    mean, scale, slope, start = norm_constants(gath_prev_ref, counted, norm_ref, index - 1)
    half_slope, half_start = slope * 0.5, start * 0.5
    lanes = half_lanes(rows)
    sums[...] = jnp.zeros_like(sums)
    for a in range(3):
        for b in range(2):
            offsets[a, b] = grad_start * twice(mask_ref[a, b])

    def activate(J, slot):
        Jc = jnp.minimum(J, NJ - 1)
        jm = mask_row(J)
        slope_now, along_now = grad_slope, grad_along
        if slot > UNROLL:
            present = jnp.where(J < NJ, 1.0, 0.0)
            slope_now, along_now = grad_slope * present, grad_along * present
        for s in range(NI):
            grad = dy_ref[s, Jc].astype(f32) * slope_now + (
                c_ref[s, Jc].astype(f32) * along_now + offsets[jm, 0 if s == 0 else 1]
            )
            put_column(ring, slot, s, grad, grad.astype(bf16), q_ref)

    def multiply():
        for u in range(UNROLL):
            side_columns(ring, side, u, lanes)
        parts = [operands(ring, side, u) for u in range(UNROLL)]
        return product(
            [jnp.concatenate([part[k] for part in parts], 0) for k in range(4)], matrix
        )

    def convolve(J, u, everything):
        total = everything[u * NI * rows : (u + 1) * NI * rows]
        jm = mask_row(J)
        tiles, others = [], []
        for s in range(NI):
            grad_ref[s, J] = ring[u + 1, s + 1]
            half = prev_ref[s, J].astype(f32) * half_slope + half_start
            if residual:
                half = half + 0.5 * res_ref[s, J].astype(f32)
            sigma = (0.5 + 0.5 * jnp.tanh(half)) * twice(mask_ref[jm, 0 if s == 0 else 1])
            value = (half + half) * sigma
            value_ref[s, J] = value.astype(bf16)
            tile = total[s * rows : (s + 1) * rows]
            if adding:
                tile = tile + add_ref[s, J].astype(f32)
            tile = tile * (sigma + value - value * sigma)
            low = tile.astype(bf16)
            out_ref[s, J] = low
            tiles.append(low)
            others.append(low * prev_ref[s, J])
        sums[0, u] += summed(tiles)
        sums[1, u] += summed(others)

    ring[UNROLL] = jnp.zeros(ring.shape[1:], bf16)
    loads.wait_load(0)
    activate(0, UNROLL + 1)
    fetch.wait()

    def step(i, carry):
        @pl.when(i + 1 < GROUPS)
        def _():
            loads.wait_load(i + 1)

        for k in range(2):
            ring[k] = ring[UNROLL + k]
        for u in range(UNROLL):
            activate(i * UNROLL + u + 1, u + 2)
        everything = multiply()
        for u in range(UNROLL):
            convolve(i * UNROLL + u, u, everything)
        saves.start_save(i)
        return carry

    lax.fori_loop(0, GROUPS, step, 0)
    first_sum = total_of(sums, 0)
    second_sum = (total_of(sums, 1) - mean * first_sum) * scale
    row = message(first_sum, second_sum)
    send(stat_ref, row)
    if carrying:
        carry(carried_ref, weights_ref[...].astype(f32), row, carrying)
    for i in range(GROUPS):
        saves.wait_save(i)


def weight_grad_kernel(*refs, slot_out, continued):
    grad_far, value_far, q_ref = refs[:3]
    refs = refs[3 + continued :]
    out_ref, token_ref, refs = refs[0], refs[1], refs[2:]
    token_ref[...] = jnp.zeros_like(token_ref)
    ring, side, acc, grad_in_ref, value_ref, sems, piece_ref, piece_sem = refs
    loads = Streams([grad_far, value_far], [grad_in_ref, value_ref], sems, 0)
    for i in range(CHUNKS):
        loads.start_load(i)
    rows = value_ref.shape[2]
    lanes = half_lanes(rows)

    def load(J, slot):
        Jc = jnp.minimum(J, NJ - 1)
        some = jnp.where(J < NJ, 1.0, 0.0)
        for s in range(NI):
            low = value_ref[s, Jc]
            if slot == UNROLL + 1:
                low = low * some.astype(bf16)
            put_column(ring, slot, s, low.astype(f32), low, q_ref)

    ring[UNROLL] = jnp.zeros(ring.shape[1:], bf16)
    loads.wait_load(0)
    load(0, UNROLL + 1)

    def step(i, carry):
        loads.wait_load(2 * i + 1)
        loads.when(2 * i + 2 < CHUNKS, loads.wait_load, 2 * i + 2)
        for k in range(2):
            ring[k] = ring[UNROLL + k]
        for u in range(UNROLL):
            load(i * UNROLL + u + 1, u + 2)
        for u in range(UNROLL):
            side_columns(ring, side, u, lanes)
        grad = jnp.concatenate(
            [grad_in_ref[:, i * UNROLL + u] for u in range(UNROLL)], 0
        ).reshape(UNROLL * NI * rows, LANES)
        parts = [operands(ring, side, u) for u in range(UNROLL)]
        for k in range(4):
            value = jnp.concatenate([parts[u][k] for u in range(UNROLL)], 0)
            piece = lax.dot_general(
                grad, value, (((0,), (0,)), ((), ())), preferred_element_type=f32
            )
            at = slice(k * LANES, (k + 1) * LANES)
            acc[:, at] = jnp.where(i == 0, piece, acc[:, at] + piece)
        return carry

    lax.fori_loop(0, GROUPS, step, 0)
    taps = [None] * 9
    for slot in range(16):
        for out in range(4):
            tap = tap_of(slot, out)
            if tap is not None:
                piece = acc[out * 64 : (out + 1) * 64, slot * 64 : (slot + 1) * 64]
                taps[tap] = piece if taps[tap] is None else taps[tap] + piece
    result = jnp.concatenate(taps, 1)
    if slot_out is None:
        out_ref[...] = result.astype(bf16)
    else:
        width = piece_ref.shape[1]
        for j in range(piece_ref.shape[0]):
            piece_ref[j] = result[j * width : (j + 1) * width].astype(bf16)
        copy = pltpu.make_async_copy(piece_ref, out_ref.at[:, slot_out], piece_sem)
        copy.start()
        copy.wait()


def stem_back_kernel(
    dy_far, c_far, z_ref, sums_ref, gath_ref, norm_ref, mask_ref, table_ref, conv_ref, head_ref,
    *refs
):
    stat_refs, (out_ref, dy_ref, held, raw, sems) = refs[:7], refs[7:]
    loads = Streams([dy_far, c_far], [dy_ref, held], sems, 0, NI)
    for k in range(NJ // NI):
        loads.start_load(k)
    rows = held.shape[2]
    counted = pixels_of(gath_ref)
    slope, along, start = grad_constants(
        carried_totals(sums_ref), gath_ref, counted, norm_ref, 0
    )
    span = 2 * NI
    deep = (span + 2) * 4
    for block in range(NJ // NI):
        loads.wait_load(block)
        for s in range(NI):
            at = (block * (span + 2) + 2 * s) * deep
            pieces = []
            for j in range(NI):
                J = block * NI + j
                mask = twice(mask_ref[0 if J < SHORT_J else 1, 0 if s == 0 else 1])
                grad = dy_ref[s, J].astype(f32) * slope + held[s, J].astype(f32) * along
                pieces.append(((grad + start) * mask).astype(bf16))
            piece = jnp.dot(
                z_ref[at : at + 4 * deep][:, :rows],
                jnp.concatenate(pieces, 1),
                preferred_element_type=f32,
            )
            if block == 0 and s == 0:
                raw[...] = piece
            else:
                raw[...] += piece
    parts = [raw[:, k * 64 : (k + 1) * 64].astype(bf16) for k in range(NI * 4)]
    total = lax.dot_general(
        jnp.concatenate(parts, 0),
        table_ref[...].reshape(NI * 4 * 4 * deep, 32),
        (((0,), (0,)), ((), ())),
        preferred_element_type=f32,
    )
    stats = jnp.concatenate([ref[0:1] if len(ref.shape) == 2 else ref[0, 0:1] for ref in stat_refs], 0)
    shifts, gains = stats[:, :64], stats[:, 64:]
    norms = jnp.concatenate([gains, shifts, jnp.zeros((2, 64), f32)], 0).T
    head = head_ref[:, :64].T
    extra = jnp.concatenate([total[:, :27], norms[:, :14], head[:, :23]], 1)
    out_ref[...] = jnp.concatenate([conv_ref[...].astype(f32), extra], 1).astype(bf16)


def chain_kernel(
    early_ref, late_ref, last_ref, noise_ref, conv_ref, stem_ref, head_ref, conv_out, extra_out,
    square_ref, *, devices
):
    count, width = early_ref.shape[0], early_ref.shape[2]
    narrow = devices // count
    member = lax.axis_index("wide")

    def partial(w):
        last = tree(last_ref[w * narrow + n].astype(f32) for n in range(narrow))
        late = tree(late_ref[w * narrow + n][:, :576].astype(f32) for n in range(narrow))
        return (
            [last[:, :576], late] + [early_ref[w, k].astype(f32) for k in range(4)],
            last[:, 576:],
        )

    def place(k):
        return lax.rem(member + k, count)

    def hop(k, carried):
        conv, extra = carried
        top = jnp.max(jnp.abs(extra), keepdims=True)
        for piece in conv:
            top = jnp.maximum(top, jnp.max(jnp.abs(piece), keepdims=True))
        scale = top + 1e-06
        sender = place(k)
        more, more_extra = partial(place(k + 1))

        def passed(value, dither, added):
            level = (value / scale * levels + dither.astype(f32)).astype(bf16)
            return level.astype(f32) * scale / levels + added

        conv = [passed(conv[m], noise_ref[sender, m], more[m]) for m in range(6)]
        dither = noise_ref[sender, 6][:, :64]
        known = lax.broadcasted_iota(jnp.int32, extra.shape, 1) < 41 + head_ref.shape[1]
        return conv, jnp.where(known, passed(extra, dither, more_extra), 0.0)

    conv, extra = lax.fori_loop(1, count, hop, partial(place(1)))
    head = head_ref[...]
    masters = jnp.concatenate(
        [
            stem_ref[...], jnp.zeros((width, 14), f32), head,
            jnp.zeros((width, 64 - 41 - head.shape[1]), f32),
        ],
        1,
    )
    extra = extra + weight_decay * masters
    total = jnp.sum(extra * extra, keepdims=True)
    for m in range(6):
        value = conv[m] + weight_decay * conv_ref[m]
        conv_out[m] = value
        total = total + jnp.sum(value * value, keepdims=True)
    extra_out[...] = jnp.concatenate([extra, extra], 1)
    square_ref[...] = jnp.broadcast_to(total, square_ref.shape)


def adam_kernel(square_ref, heads_ref, first_ref, conv_ref, extra_ref, *refs, classes):
    news, held, sems = refs[15:33], refs[33:48], refs[48]
    copies = [pltpu.make_async_copy(refs[k], held[k], sems.at[k]) for k in range(15)]
    for copy in copies:
        copy.start()
    olds = held
    bias = jnp.sum(heads_ref[:, 1, :], 0, keepdims=True)
    loss = bias[:, 127:128]
    bias = bias[:, :classes]
    total = jnp.sum(square_ref[...][:, 0:1], 0, keepdims=True)
    total = total + jnp.sum(bias * bias, keepdims=True)
    norm = jnp.sqrt(total)
    factor = clip_limit / jnp.maximum(norm, clip_limit)
    extra = extra_ref[...]
    turned = extra.T
    parts = (
        (extra[:, :27],), tuple(conv_ref[m] for m in range(6)),
        (turned[27:34], turned[34:41]), (extra[:, 41 : 41 + classes],), (bias,),
    )
    for copy in copies:
        copy.wait()
    for k, pieces in enumerate(parts):
        master, first, second = olds[3 * k : 3 * k + 3]
        for m, gradient in enumerate(pieces):
            at = {6: (m,), 2: (slice(None), m)}.get(len(pieces), ())
            results = adam_update(gradient, first[at], second[at], master[at], factor)
            for ref, value in zip(news[3 * k : 3 * k + 3], results):
                ref[at] = value
    news[15][...] = norm
    news[16][...] = loss
    news[17][...] = jnp.sum(first_ref[:, 1, 1:2], 0, keepdims=True)


def stem_table():
    span = 2 * NI + 2
    table = np.zeros((NI * 4, 4, span, 4, 27), np.float32)
    for j in range(NI):
        for out in range(4):
            for ky in range(3):
                for kx in range(3):
                    for i in range(3):
                        table[
                            j * 4 + out, out // 2 + ky, 2 * j + out % 2 + kx, i,
                            (ky * 3 + kx) * 3 + i,
                        ] = 1.0
    return np.pad(table.reshape(NI * 4, 4 * span * 4, 27), ((0, 0), (0, 0), (0, 5)))


def adam_update(gradient, first, second, master, factor):
    clipped = gradient * factor
    new_first = first_decay * first + (1.0 - first_decay) * clipped
    new_second = second_decay * second + (1.0 - second_decay) * clipped * clipped
    corrected = (
        new_first
        / (1.0 - first_decay**STEP)
        / (jnp.sqrt(new_second / (1.0 - second_decay**STEP)) + adam_epsilon)
    )
    return (master - learn_rate * (corrected + decoupled * master), new_first, new_second)


def shared(rows):
    return lax.all_to_all(rows, BOTH, 0, 0, tiled=True)


def body(
    images,
    large_flag,
    labels,
    example_weights,
    cycle_noise,
    stem_weight,
    conv_weight,
    norm_params,
    head_weight,
    head_bias,
    stem_first,
    stem_second,
    conv_first,
    conv_second,
    norm_first,
    norm_second,
    head_first,
    head_second,
    bias_first,
    bias_second,
):
    wide_count = lax.axis_size("wide")
    devices = wide_count * lax.axis_size("narrow")
    count = large_flag.shape[0]
    rows = QUARTERS * count
    width = stem_weight.shape[0]
    channels = width * wide_count
    classes = head_weight.shape[0]
    assert channels == 64 and rows % 16 == 0 and rows <= 128

    member = lax.axis_index("wide")

    def to_wide(value):
        return lax.all_to_all(value, "wide", 0, 0, tiled=True)

    owned = (stem_weight, conv_weight, norm_params.transpose(1, 0, 2), head_weight.T)
    packed = call(
        pack_kernel,
        (jax.ShapeDtypeStruct((wide_count, 7, width, 576), bf16),),
        [pltpu.VMEM(value.shape, f32) for value in owned] + [pltpu.SemaphoreType.DMA((4,))],
        owned,
        "pack",
        stored=(0, 1, 2, 3),
        limit=8,
    )[0]
    packed = to_wide(packed)
    bias_row = jnp.pad(head_bias[None, :], ((0, 0), (0, 128 - classes)))

    dither = ((cycle_noise[0].astype(f32) + 0.5) / 65536.0 - 0.5).astype(bf16)
    hop_row = (member - 1 - jnp.arange(wide_count, dtype=jnp.int32)) % wide_count
    dither = jnp.take(dither, jnp.minimum(hop_row, wide_count - 2), axis=0)
    one, two, three = width * 27, width * 27 + 6 * width * 576, width * 41 + 6 * width * 576
    extra = jnp.concatenate(
        [
            dither[:, :one].reshape(wide_count, width, 27),
            dither[:, two:three].reshape(wide_count, 14, width).transpose(0, 2, 1),
            dither[:, three:].reshape(wide_count, classes, width).transpose(0, 2, 1),
        ],
        2,
    )
    extra = jnp.pad(extra, ((0, 0), (0, 0), (0, 576 - extra.shape[2])))
    dither = jnp.concatenate(
        [dither[:, one:two].reshape(wide_count, 6, width, 576), extra[:, None]], 1
    )

    large = large_flag == 1
    row_large = jnp.repeat(large, QUARTERS)
    quarter = jnp.arange(rows, dtype=jnp.int32) % QUARTERS
    upper = row_large | (quarter < SHORT_J // NI)
    ones = jnp.ones((rows,), bool)
    none = jnp.zeros((rows,), bool)
    mask_table = jnp.stack(
        [jnp.stack([ones, upper]), jnp.stack([row_large, row_large]), jnp.stack([none, none])]
    )
    mask_table = jnp.broadcast_to(mask_table[..., None], (3, 2, rows, 128)).astype(f32)
    q_table = jnp.broadcast_to(
        jnp.stack([quarter != QUARTERS - 1, quarter != 0])[..., None], (2, rows, 128)
    ).astype(f32)
    sides = jnp.where(large, SIDE, SHORT).astype(jnp.int32)
    weights_f = example_weights.astype(f32)
    lane = jnp.arange(128, dtype=jnp.int32)[None, :]
    info = jnp.where(
        lane == 0,
        jnp.repeat((sides * sides).astype(f32), QUARTERS)[:, None],
        jnp.where(lane == 1, jnp.repeat(weights_f, QUARTERS)[:, None], 0.0),
    )
    hot = (jnp.repeat(labels, QUARTERS)[:, None] == lane).astype(f32)

    span = 2 * NI
    position = jnp.arange(span * SIDE, dtype=jnp.int32)
    inside = row_large[:, None] | (
        (quarter[:, None] * span + (position // SIDE)[None, :] < SHORT)
        & ((position % SIDE)[None, :] < SHORT)
    )
    planes = images.reshape(3, rows, span * SIDE) * inside.astype(bf16)[None]

    (planes, mask_table, q_table, info, hot, bias_row, dither, packed) = (
        lax.optimization_barrier(
            (planes, mask_table, q_table, info, hot, bias_row, dither, packed)
        )
    )
    dither = to_wide(dither)
    table = jnp.asarray(stem_table(), bf16)
    norm4, into_head, from_head, stem_wide = call(
        small_kernel,
        (
            jax.ShapeDtypeStruct((16, LANES), f32),
            jax.ShapeDtypeStruct((128, 128), bf16),
            jax.ShapeDtypeStruct((128, LANES), bf16),
            jax.ShapeDtypeStruct((table.shape[1], NI * LANES), bf16),
        ),
        [],
        (packed, table),
        "small",
        limit=12,
    )
    matrices = call(
        weights_kernel,
        (Stored((1024, LANES)),) * 12,
        [pltpu.VMEM((12, 1024, LANES), bf16), pltpu.SemaphoreType.DMA((12,))],
        (packed,),
        "weights",
        limit=16,
    )

    z_rows = (SIDE // span) * (span + 2) * (span + 2) * 4
    full = pltpu.VMEM((NI, NJ, rows, LANES), bf16)
    side_shape = (UNROLL, NI + 2, rows, LANES)
    sets = [
        pltpu.VMEM((BLOCK + 2, NI + 2, rows, LANES), bf16),
        pltpu.VMEM((BLOCK, NI + 2, rows, LANES), bf16),
        pltpu.VMEM((BLOCK * NI * rows, LANES), f32),
    ] * 2
    stat = jax.ShapeDtypeStruct((devices, 128), f32)

    c0_saved, z, stat0 = call(
        functools.partial(stem_kernel, devices=devices),
        (
            stored_field(rows),
            jax.ShapeDtypeStruct((z_rows, 128), bf16),
            jax.ShapeDtypeStruct((devices, 2, 128), f32),
        ),
        [pltpu.VMEM((z_rows, 128), f32), full, pltpu.SemaphoreType.DMA((SIDE // span,))],
        (planes, stem_wide, mask_table, info),
        "stem",
    )
    current, saved = c0_saved, [c0_saved]
    stat0, norm4, into_head, from_head, dither, *matrices = lax.optimization_barrier(
        (stat0, norm4, into_head, from_head, dither, *matrices)
    )
    gathered = [shared(stat0)]
    stream, streams = None, []
    ahead, back = matrices[:6], matrices[6:]
    for layer in range(1, 7):
        keep = layer % 2 == 1
        residual = keep and layer > 1
        args = (current,) + ((stream,) if residual else ())
        args += (gathered[layer - 1], gathered[0], norm4, mask_table, q_table, ahead[layer - 1])
        outs = call(
            functools.partial(
                forward_kernel, index=layer - 1, keep=keep, residual=residual,
                streamed=layer == 1, devices=devices,
            ),
            (field(rows), stored_field(rows)) * (2 if keep else 1) + (stat,),
            [
                pltpu.VMEM((2, BLOCK, 8, LANES), f32),
                pltpu.SemaphoreType.DMA((2, CHUNKS)),
            ]
            + sets
            + (
                [
                    full,
                    pltpu.SemaphoreType.DMA((1, CHUNKS)),
                    pltpu.VMEM((1024, LANES), bf16),
                    pltpu.SemaphoreType.DMA,
                ]
                if layer == 1
                else []
            ),
            args,
            "forward",
            cost=int(7e9),
            limit=24,
            stored=(0, len(args) - 1) if layer == 1 else (),
        )
        current = outs[0]
        saved.append(outs[1])
        if keep:
            stream = outs[2]
            streams.append(outs[3])
        gathered.append(shared(outs[-1]))

    dys = [None] * 7
    stats = [None] * 7
    dys[6], stats[6], head_grad = call(
        functools.partial(head_kernel, classes=classes, devices=devices),
        (
            stored_field(rows),
            jax.ShapeDtypeStruct((devices, 2, 128), f32),
            jax.ShapeDtypeStruct((128, 128), f32),
        ),
        [
            pltpu.VMEM((NI, NJ, rows, LANES), f32),
            pltpu.VMEM((rows, LANES), f32),
            pltpu.VMEM((NI, NJ, rows, LANES), bf16),
            pltpu.SemaphoreType.DMA((1, CHUNKS)),
        ],
        (
            current, stream, gathered[6], gathered[0], norm4, mask_table, hot, info,
            into_head, from_head, bias_row,
        ),
        "head",
        cost=int(8e9),
        limit=28,
    )
    tokens = ()
    narrow_count = devices // wide_count
    carried_shape = (devices, width, carried_lanes(width))
    for layer in range(6, 0, -1):
        residual = layer in (5, 3)
        adding = layer % 2 == 1
        sums = shared(stats[layer])
        if layer == 6:
            heads = sums
        args = (dys[layer], saved[layer], saved[layer - 1])
        args += (streams[layer // 2 - 1],) if residual else ()
        args += (dys[layer + 1],) if adding else ()
        inputs = len(args)
        args += (
            sums, gathered[layer], gathered[layer - 1], gathered[0], norm4, mask_table, q_table,
            back[layer - 1], *tokens, *((late,) if layer == 1 else ()),
        )
        dys[layer - 1], grad, value, stats[layer - 1], *carried = call(
            functools.partial(
                backward_kernel, index=layer, residual=residual, adding=adding,
                ordered=len(tokens), carrying=narrow_count if layer == 1 else 0, devices=devices,
            ),
            (stored_field(rows),) * 3
            + (stat,)
            + ((jax.ShapeDtypeStruct(carried_shape, bf16),) if layer == 1 else ()),
            [
                pltpu.VMEM((UNROLL + 2, NI + 2, rows, LANES), bf16),
                pltpu.VMEM(side_shape, bf16),
                pltpu.VMEM((3, 2, rows, LANES), f32),
                pltpu.VMEM((2, UNROLL, 8, LANES), f32),
                pltpu.SemaphoreType.DMA((8, GROUPS)),
                pltpu.VMEM((1024, LANES), bf16),
                pltpu.SemaphoreType.DMA,
            ]
            + [full] * (3 + inputs),
            args,
            "backward",
            cost=int(8e9),
            limit=46,
            stored=tuple(range(inputs)) + (inputs + 7,),
        )
        slot_out = layer - 3 if layer > 2 else None
        shape = (wide_count, 4, width, 576)
        args = (grad, value, q_table)
        outs = (jax.ShapeDtypeStruct((64, 576), bf16), jax.ShapeDtypeStruct((8, 128), f32))
        aliases = {}
        if 2 < layer < 6:
            aliases[len(args)] = 0
            args += (early,)
        if layer > 2:
            outs = (Stored(shape), outs[1])
        result, token = call(
            functools.partial(
                weight_grad_kernel, slot_out=slot_out, continued=len(args) == 4
            ),
            outs,
            [
                pltpu.VMEM((UNROLL + 2, NI + 2, rows, LANES), bf16),
                pltpu.VMEM(side_shape, bf16),
                pltpu.VMEM((LANES, 1024), f32),
                full,
                full,
                pltpu.SemaphoreType.DMA((2, CHUNKS)),
                pltpu.VMEM((wide_count, width, 576), bf16),
                pltpu.SemaphoreType.DMA,
            ],
            args,
            "weight_grad",
            cost=int(7e9),
            limit=24,
            stored=(0, 1) + tuple(range(3, len(args))),
            aliases=aliases,
        )
        tokens = (token,)
        if layer > 2:
            early = result
        if layer == 3:
            early = lax.psum(early, "narrow")
        if layer == 2:
            late = result
    carried = shared(carried[0])
    early = to_wide(early)
    last = call(
        stem_back_kernel,
        (jax.ShapeDtypeStruct((64, 640), bf16),),
        [
            full,
            full,
            pltpu.VMEM((4 * (span + 2) * 4, NI * LANES), f32),
            pltpu.SemaphoreType.DMA((2, NJ // NI)),
        ],
        (
            dys[0], saved[0], z, carried, gathered[0], norm4, mask_table, table,
            result, head_grad, *stats,
        ),
        "stem_back",
        stored=(0, 1),
        cost=int(5e9),
    )[0]
    last = jnp.broadcast_to(
        last.reshape(wide_count, 1, width, 640), (wide_count, narrow_count, width, 640)
    )
    last = shared(last.reshape(devices, width, 640))
    conv_total, extra_total, squares = call(
        functools.partial(chain_kernel, devices=devices),
        (
            jax.ShapeDtypeStruct((6, width, 576), f32),
            jax.ShapeDtypeStruct((width, 128), f32),
            jax.ShapeDtypeStruct((wide_count, 128), f32),
        ),
        [],
        (early, carried, last, dither, conv_weight, stem_weight, head_weight.T),
        "chain",
    )
    olds = (
        stem_weight, stem_first, stem_second, conv_weight, conv_first, conv_second,
        *(value.transpose(1, 0, 2) for value in (norm_params, norm_first, norm_second)),
        head_weight.T, head_first.T, head_second.T,
        head_bias[None], bias_first[None], bias_second[None],
    )
    single = jax.ShapeDtypeStruct((1, 1), f32)
    news = call(
        functools.partial(adam_kernel, classes=classes),
        tuple(Result(old.shape, f32) for old in olds) + (single,) * 3,
        [pltpu.VMEM(old.shape, f32) for old in olds] + [pltpu.SemaphoreType.DMA((15,))],
        (to_wide(squares), heads, gathered[0], conv_total, extra_total, *olds),
        "adam",
        stored=tuple(range(5, 20)),
        limit=12,
    )
    return (
        *news[:6],
        *(new.transpose(1, 0, 2) for new in news[6:9]),
        *(new.T for new in news[9:12]),
        *(new[0] for new in news[12:15]),
        *(new[0, 0] for new in news[15:]),
    )


def solution(mesh):
    split = P(BOTH)
    ins = (
        P(None, BOTH), split, split, split, P("wide", None, None),
        P("wide", None), P(None, "wide", None), P(None, None, "wide"), P(None, "wide"), P(),
        P("wide", None), P("wide", None), P(None, "wide", None), P(None, "wide", None),
        P(None, None, "wide"), P(None, None, "wide"), P(None, "wide"), P(None, "wide"), P(), P(),
    )
    outs = (
        (P("wide", None),) * 3
        + (P(None, "wide", None),) * 3
        + (P(None, None, "wide"),) * 3
        + (P(None, "wide"),) * 3
        + (P(),) * 6
    )
    return jax.shard_map(body, mesh=mesh, in_specs=ins, out_specs=outs, check_vma=False)
```

```python
import functools

import jax
import jax.numpy as jnp
import numpy as np
from jax import lax
from jax.experimental import pallas as pl
from jax.experimental.pallas import tpu as pltpu
from jax.sharding import PartitionSpec as P

SIDE = 40
SHORT = 32
STEP = 10

norm_epsilon = 1e-05
clip_limit = 0.002
learn_rate = 0.4
first_decay = 0.9
second_decay = 0.999
adam_epsilon = 1e-08
weight_decay = 0.0005
decoupled = 0.01
levels = 15.0

QUARTERS = 4
PATCHES = SIDE // 2
NI = PATCHES // QUARTERS
NJ = PATCHES
SHORT_J = SHORT // 2
LANES = 256
UNROLL = 4
BLOCK = 2

f32 = jnp.float32
bf16 = jnp.bfloat16
BOTH = ("wide", "narrow")


def window_place(slot):
    group, sy, sx = slot // 4, (slot // 2) % 2, slot % 2
    wx = 1 + sx if group in (0, 2) else (3 if sx == 0 else 0)
    wy = 1 + sy if group in (0, 1) else (3 if sy == 0 else 0)
    return wy, wx


def tap_of(slot, out):
    wy, wx = window_place(slot)
    ky, kx = wy - out // 2, wx - out % 2
    if 0 <= ky < 3 and 0 <= kx < 3:
        return ky * 3 + kx
    return None


def whole():
    return pl.BlockSpec(memory_space=pltpu.VMEM)


def call(kernel, outs, scratch, args, name, cost=None, limit=24, stored=(), aliases=None):
    def place(out):
        return pl.BlockSpec(memory_space=pltpu.HBM) if type(out) is Stored else whole()

    def shape(out):
        kind = pltpu.HBM if isinstance(out, (Stored, Result)) else jax.ShapeDtypeStruct
        return kind(out.shape, out.dtype)

    args = [
        pltpu.with_memory_space_constraint(arg, pltpu.HBM) if k in stored else arg
        for k, arg in enumerate(args)
    ]

    return pl.pallas_call(
        kernel,
        out_shape=tuple(shape(out) for out in outs),
        in_specs=[
            pl.BlockSpec(memory_space=pltpu.HBM) if k in stored else whole()
            for k in range(len(args))
        ],
        out_specs=tuple(place(out) for out in outs),
        scratch_shapes=scratch,
        compiler_params=pltpu.CompilerParams(vmem_limit_bytes=limit * 2**20),
        name=name,
        input_output_aliases=aliases or {},
        cost_estimate=pl.CostEstimate(flops=cost, bytes_accessed=2**20, transcendentals=0)
        if cost
        else None,
    )(*args)


class Stored:
    def __init__(self, shape, dtype=bf16):
        self.shape, self.dtype = shape, dtype


class Result(Stored):
    pass


def stored_field(rows):
    return Stored((NI, NJ, rows, LANES))


class Streams:
    def __init__(self, outside, inside, sems, base, columns=None):
        self.outside, self.inside = tuple(outside), tuple(inside)
        self.sems, self.base, self.columns = sems, base, columns or BLOCK

    def pairs(self, i):
        for k, (far, near) in enumerate(zip(self.outside, self.inside)):
            at = pl.ds(i * self.columns, self.columns)
            yield far.at[:, at], near.at[:, at], self.sems.at[self.base + k, i]

    def when(self, condition, action, i):
        @pl.when(condition)
        def _():
            action(i)

    def start_load(self, i):
        for far, near, sem in self.pairs(i):
            pltpu.make_async_copy(far, near, sem).start()

    def wait_load(self, i):
        for far, near, sem in self.pairs(i):
            pltpu.make_async_copy(far, near, sem).wait()

    def wait_loads(self, i):
        self.wait_load(i)
        self.wait_load(i + 1)

    def start_save(self, i):
        for far, near, sem in self.pairs(i):
            pltpu.make_async_copy(near, far, sem).start()

    def wait_save(self, i):
        for far, near, sem in self.pairs(i):
            pltpu.make_async_copy(near, far, sem).wait()


CHUNKS = NJ // BLOCK
GROUPS = NJ // UNROLL


def field(rows):
    return jax.ShapeDtypeStruct((NI, NJ, rows, LANES), bf16)


def wide_pair(row):
    turned = pltpu.roll(row, 64, 1)
    lower = lax.broadcasted_iota(jnp.int32, row.shape, 1) < 64
    first = jnp.where(lower, row, turned)
    second = jnp.where(lower, turned, row)
    return jnp.concatenate([first, first], 1), jnp.concatenate([second, second], 1)


def folded(row):
    half = row[:, :128] + row[:, 128:]
    return half + pltpu.roll(half, 64, 1)


def message(first, second):
    lower = lax.broadcasted_iota(jnp.int32, (1, 128), 1) < 64
    return jnp.where(lower, folded(first), folded(second))


def totals(gathered):
    rows = gathered[:, 0, :] if len(gathered.shape) == 3 else gathered[...]
    return wide_pair(jnp.sum(rows, 0, keepdims=True))


def send(ref, first, second=None):
    if second is None:
        ref[...] = jnp.broadcast_to(first, ref.shape)
    else:
        both = jnp.concatenate([first, second], 0)[None]
        ref[...] = jnp.broadcast_to(both, ref.shape)


def norm_constants(gathered, counted, norm4, index):
    sums, squares = totals(gathered)
    mean = sums / counted
    scale = lax.rsqrt(squares / counted - mean * mean + norm_epsilon)
    gain = norm4[index : index + 1]
    slope = gain * scale
    return mean, scale, slope, norm4[7 + index : 8 + index] - mean * slope


def pixels_of(gathered_first):
    return jnp.sum(gathered_first[:, 1, 0:1], 0, keepdims=True)


def twice(tile):
    return jnp.concatenate([tile, tile], 1)


def mask_row(J):
    return jnp.where((J < 0) | (J >= NJ), 2, jnp.where(J < SHORT_J, 0, 1))


def put_column(ring, slot, s, value, low, q_ref):
    rows = value.shape[0]
    ring[slot, s + 1] = low
    if s == 0:
        ring[slot, NI + 1, :, :128] = (pltpu.roll(value[:, :128], rows - 1, 0) * q_ref[0]).astype(
            bf16
        )
    if s == NI - 1:
        ring[slot, 0, :, 128:] = (pltpu.roll(value[:, 128:], 1, 0) * q_ref[1]).astype(bf16)


def side_columns(ring, side, u, lanes):
    for s in range(NI + 2):
        if s == 0:
            side[u, s, :, 128:] = jnp.where(
                lanes[:, 128:], ring[u + 2, s, :, 128:], ring[u, s, :, 128:]
            )
        elif s == NI + 1:
            side[u, s, :, :128] = jnp.where(
                lanes[:, :128], ring[u + 2, s, :, :128], ring[u, s, :, :128]
            )
        else:
            side[u, s] = jnp.where(lanes, ring[u + 2, s], ring[u, s])


def operands(ring, side, u):
    rows = ring.shape[2]
    whole_rows = NI * rows
    last = NI + 2
    own = ring[u + 1, 1 : NI + 1].reshape(whole_rows, LANES)
    beside = side[u, 1 : NI + 1].reshape(whole_rows, LANES)
    above = jnp.concatenate(
        [ring[u + 1, 2:last, :, :128], ring[u + 1, 0:NI, :, 128:]], -1
    ).reshape(whole_rows, LANES)
    corner = jnp.concatenate([side[u, 2:last, :, :128], side[u, 0:NI, :, 128:]], -1).reshape(
        whole_rows, LANES
    )
    return own, beside, above, corner


def product(parts, w_ref):
    total = jnp.dot(parts[0], w_ref[0:LANES], preferred_element_type=f32)
    for k in range(1, 4):
        total += jnp.dot(
            parts[k], w_ref[k * LANES : (k + 1) * LANES], preferred_element_type=f32
        )
    return total


def tree(values):
    values = list(values)
    while len(values) > 1:
        paired = [a + b for a, b in zip(values[::2], values[1::2])]
        values = paired + values[len(values) - len(values) % 2 :]
    return values[0]


def by_eight(value):
    return tree(value[k : k + 8] for k in range(0, value.shape[0], 8))


def summed(tiles):
    low = tree(tiles)
    low = tree(low[k : k + 16] for k in range(0, low.shape[0], 16))
    return by_eight(low.astype(f32))


def total_of(sums, which):
    return jnp.sum(tree(sums[which, u] for u in range(sums.shape[1])), 0, keepdims=True)


def pipeline(sets, activate, finish, matrix, lanes, before, after):
    def ready(block, own, other):
        ring, side, _ = own
        if other is None:
            ring[0] = jnp.zeros(ring.shape[1:], bf16)
            activate(0, ring, 1)
        else:
            ring[0] = other[0][BLOCK]
            ring[1] = other[0][BLOCK + 1]
        for u in range(BLOCK):
            activate(block * BLOCK + u + 1, ring, u + 2)
        for u in range(BLOCK):
            side_columns(ring, side, u, lanes)

    def multiply(own):
        ring, side, result = own
        parts = [operands(ring, side, u) for u in range(BLOCK)]
        result[...] = product(
            [jnp.concatenate([part[k] for part in parts], 0) for k in range(4)], matrix
        )

    def step(j, carry):
        for half in range(2):
            own, other = sets[half], sets[1 - half]
            block = 2 * j + half
            if half == 0:
                before(block)
            multiply(own)
            for u in range(BLOCK):
                finish((block - 1) * BLOCK + u, other, u)
            ready(block + 1, other, own)
            after(block)
        return carry

    sets[1][2][...] = jnp.zeros(sets[1][2].shape, f32)
    ready(0, sets[0], None)

    def tail():
        for u in range(BLOCK):
            finish(NJ - BLOCK + u, sets[1], u)

    return step, tail


def half_lanes(rows):
    return lax.broadcasted_iota(jnp.int32, (rows, LANES), 1) % 128 < 64


def pack_kernel(*refs):
    out_ref, held, sems = refs[4], refs[5:9], refs[9]
    copies = [pltpu.make_async_copy(refs[k], held[k], sems.at[k]) for k in range(4)]
    for copy in copies:
        copy.start()
    for copy in copies:
        copy.wait()
    stem_ref, conv_ref, norm_ref, head_ref = held
    width = stem_ref.shape[0]
    gains = [norm_ref[:, k, :].T for k in range(2)]
    head = head_ref[...]
    used = 27 + 14 + head.shape[1]
    small = jnp.concatenate(
        [stem_ref[...], *gains, head, jnp.zeros((width, 128 - used), f32)], 1
    )
    high = small.astype(bf16)
    rest = small - high.astype(f32)
    middle = rest.astype(bf16)
    low = (rest - middle.astype(f32)).astype(bf16)
    tail = jnp.concatenate([high, middle, low, jnp.zeros((width, 192), bf16)], 1)
    for w in range(out_ref.shape[0]):
        for layer in range(6):
            out_ref[w, layer] = conv_ref[layer].astype(bf16)
        out_ref[w, 6] = tail


def weights_kernel(packed_ref, *refs):
    outs, (held, sems) = refs[:12], refs[12:]
    copies = []
    for layer in range(6):
        matrix = jnp.concatenate(
            [packed_ref[w, layer].astype(f32) for w in range(packed_ref.shape[0])], 0
        )
        turned = matrix.T
        empty = jnp.zeros((64, 64), f32)
        for slot in range(16):
            ahead, back = [], []
            for out in range(4):
                tap = tap_of(slot, out)
                if tap is None:
                    ahead.append(empty)
                    back.append(empty)
                else:
                    other = 8 - tap
                    ahead.append(turned[tap * 64 : (tap + 1) * 64])
                    back.append(matrix[:, other * 64 : (other + 1) * 64])
            at = slice(slot * 64, (slot + 1) * 64)
            held[layer, at] = jnp.concatenate(ahead, 1).astype(bf16)
            held[6 + layer, at] = jnp.concatenate(back, 1).astype(bf16)
        for k in (layer, 6 + layer):
            copies.append(pltpu.make_async_copy(held.at[k], outs[k], sems.at[k]))
            copies[-1].start()
    for copy in copies:
        copy.wait()


def small_kernel(packed_ref, table_ref, norm_ref, into_ref, back_ref, stem_ref):
    count, _, width, _ = packed_ref.shape
    parts = [
        jnp.concatenate(
            [packed_ref[w, 6, :, k * 128 : (k + 1) * 128].astype(f32) for w in range(count)], 0
        )
        for k in range(3)
    ]
    turned = ((parts[0] + parts[1]) + parts[2]).T
    norms = turned[27:43]
    norm_ref[...] = jnp.concatenate([norms] * 4, 1)
    head = jnp.concatenate([turned[41:], jnp.zeros((41, 64), f32)], 0)
    back_ref[...] = jnp.concatenate([head] * 4, 1).astype(bf16)
    into_ref[...] = jnp.concatenate([head.T, jnp.zeros((64, 128), f32)], 0).astype(bf16)
    stem = turned[:32].astype(bf16)
    for k in range(table_ref.shape[0] // 2):
        pair = [
            jnp.dot(table_ref[2 * k + e], stem, preferred_element_type=f32) for e in range(2)
        ]
        stem_ref[:, k * 128 : (k + 1) * 128] = jnp.concatenate(pair, 1).astype(bf16)


def stem_kernel(
    planes_ref, w_ref, mask_ref, info_ref, save_ref, z_ref, stat_ref, zf, out_ref, sems, *, devices
):
    rows = planes_ref.shape[1]
    zf[...] = jnp.zeros_like(zf)
    span = 2 * NI
    blocks = SIDE // span
    deep = (span + 2) * 4
    for i in range(3):
        turned = planes_ref[i].astype(f32).T
        for block in range(blocks):
            first = max(block * span - 1, 0)
            last = min(block * span + span + 1, SIDE)
            skip = first - (block * span - 1)
            for y in range(span):
                base = (block * (span + 2) + y + 1) * deep + skip * 4 + i
                zf[pl.ds(base, last - first, stride=4), :rows] = turned[
                    y * SIDE + first : y * SIDE + last
                ]
    lane = lax.broadcasted_iota(jnp.int32, (deep, 128), 1)
    for block in range(blocks):
        at = block * (span + 2) * deep
        low = zf[at + span * deep : at + (span + 1) * deep]
        zf[at : at + deep] = jnp.where(lane % 4 == 0, 0.0, pltpu.roll(low, 1, 1))
        high = zf[at + deep : at + 2 * deep]
        zf[at + (span + 1) * deep : at + (span + 2) * deep] = jnp.where(
            lane % 4 == 3, 0.0, pltpu.roll(high, 127, 1)
        )
    z_ref[...] = zf[...].astype(bf16)
    first_sum = jnp.zeros((8, LANES), f32)
    second_sum = jnp.zeros((8, LANES), f32)
    copies = []
    for block in range(blocks):
        for s in range(NI):
            at = (block * (span + 2) + 2 * s) * deep
            result = lax.dot_general(
                z_ref[at : at + 4 * deep],
                w_ref[...],
                (((0,), (0,)), ((), ())),
                preferred_element_type=f32,
            )
            for j in range(NI):
                J = block * NI + j
                mask = mask_ref[0 if J < SHORT_J else 1, 0 if s == 0 else 1]
                tile = result[:rows, j * LANES : (j + 1) * LANES] * twice(mask)
                out_ref[s, J] = tile.astype(bf16)
                first_sum += by_eight(tile)
                second_sum += by_eight(tile * tile)
        at = pl.ds(block * NI, NI)
        copies.append(pltpu.make_async_copy(out_ref.at[:, at], save_ref.at[:, at], sems.at[block]))
        copies[-1].start()
    row = message(
        jnp.sum(first_sum, 0, keepdims=True), jnp.sum(second_sum, 0, keepdims=True)
    )
    counts = jnp.sum(info_ref[...], 0, keepdims=True) * (1.0 / QUARTERS)
    send(stat_ref, row, counts)
    for copy in copies:
        copy.wait()


def forward_kernel(*refs, index, keep, residual, streamed, devices):
    refs = list(refs)
    c_ref = refs.pop(0)
    if streamed:
        matrix_sem, matrix, load_sems, held = (refs.pop() for _ in range(4))
        loads = Streams([c_ref], [held], load_sems, 0)
        for i in range(CHUNKS):
            loads.start_load(i)
        c_ref = held
    res_ref = refs.pop(0) if residual else None
    gath_ref, first_ref, norm_ref, mask_ref, q_ref, w_ref, out_ref, save_ref = refs[:8]
    refs = refs[8:]
    keep_ref = refs.pop(0) if keep else None
    keep_save_ref = refs.pop(0) if keep else None
    stat_ref, sums, sems = refs[:3]
    if streamed:
        fetch = pltpu.make_async_copy(w_ref, matrix, matrix_sem)
        fetch.start()
        w_ref = matrix
    sets = refs[3:6], refs[6:9]
    rows = c_ref.shape[2]
    counted = pixels_of(first_ref)
    _, _, slope, start = norm_constants(gath_ref, counted, norm_ref, index)
    half_slope, half_start = slope * 0.5, start * 0.5
    lanes = half_lanes(rows)
    sums[...] = jnp.zeros_like(sums)

    def activate(J, ring, slot):
        Jc = jnp.minimum(J, NJ - 1)
        jm = mask_row(J)
        for s in range(NI):
            half = c_ref[s, Jc].astype(f32) * half_slope + half_start
            if residual:
                half = half + 0.5 * res_ref[s, Jc].astype(f32)
            mask = mask_ref[jm, 0 if s == 0 else 1]
            value = (half + half * jnp.tanh(half)) * twice(mask)
            low = value.astype(bf16)
            put_column(ring, slot, s, value, low, q_ref)

    def finish(J, own, u):
        Jc = jnp.maximum(J, 0)
        jm = mask_row(J)
        tiles = []
        for s in range(NI):
            tile = own[2][(u * NI + s) * rows : (u * NI + s + 1) * rows]
            low = (tile * twice(mask_ref[jm, 0 if s == 0 else 1])).astype(bf16)
            out_ref[s, Jc] = low
            if keep:
                keep_ref[s, Jc] = own[0][u + 1, s + 1]
            tiles.append(low)
        sums[0, u] += summed(tiles)
        sums[1, u] += summed([tile * tile for tile in tiles])

    def before(block):
        if streamed:
            loads.when(block + 2 < CHUNKS, loads.wait_loads, block + 2)

    def after(block):
        saves.when(block > 0, saves.start_save, block - 1)

    saves = Streams([save_ref, keep_save_ref][: 1 + keep], [out_ref, keep_ref][: 1 + keep], sems, 0)
    if keep:
        sets[1][0][...] = jnp.zeros(sets[1][0].shape, bf16)
    if streamed:
        loads.wait_load(0)
        loads.wait_load(1)
    step, tail = pipeline(sets, activate, finish, w_ref, lanes, before, after)
    if streamed:
        fetch.wait()
    lax.fori_loop(0, CHUNKS // 2, step, 0)
    tail()
    saves.start_save(CHUNKS - 1)
    row = message(total_of(sums, 0), total_of(sums, 1))
    send(stat_ref, row)
    for i in range(CHUNKS):
        saves.wait_save(i)


def head_kernel(
    c_ref, res_ref, gath_ref, first_ref, norm_ref, mask_ref, hot_ref, info_ref, into_ref, back_ref,
    bias_ref, dy_ref, stat_ref, head_ref, grads, pool, *, classes, devices
):
    rows = c_ref.shape[2]
    counted = pixels_of(first_ref)
    weight_total = jnp.sum(first_ref[:, 1, 1:2], 0, keepdims=True)
    mean, scale, slope, start = norm_constants(gath_ref, counted, norm_ref, 6)
    half_slope, half_start = slope * 0.5, start * 0.5
    pool[...] = jnp.zeros_like(pool)

    def gather(i, carry):
        values = []
        for u in range(UNROLL):
            J = i * UNROLL + u
            jm = mask_row(J)
            for s in range(NI):
                half = c_ref[s, J].astype(f32) * half_slope + half_start
                half = half + 0.5 * res_ref[s, J].astype(f32)
                sigma = (0.5 + 0.5 * jnp.tanh(half)) * twice(mask_ref[jm, 0 if s == 0 else 1])
                value = (half + half) * sigma
                values.append(value)
                grads[s, J] = (sigma + value - value * sigma).astype(bf16)
        pool[...] += tree(values)
        return carry

    lax.fori_loop(0, GROUPS, gather, 0)
    pooled = pool[...]
    row_index = lax.broadcasted_iota(jnp.int32, (rows, LANES), 0)
    pooled = pooled + jnp.where(
        row_index % 2 == 0, pltpu.roll(pooled, rows - 1, 0), pltpu.roll(pooled, 1, 0)
    )
    pooled = pooled + jnp.where(
        row_index % 4 < 2, pltpu.roll(pooled, rows - 2, 0), pltpu.roll(pooled, 2, 0)
    )
    half_pool = pooled[:, :128] + pooled[:, 128:]
    half_pool = half_pool + pltpu.roll(half_pool, 64, 1)
    count = info_ref[:, 0:1]
    weight = info_ref[:, 1:2]
    pooled_low = (half_pool / count).astype(bf16)
    logits = jnp.dot(pooled_low, into_ref[...], preferred_element_type=f32) + bias_ref[...]
    lane = lax.broadcasted_iota(jnp.int32, logits.shape, 1)
    inside = lane < classes
    top = jnp.max(jnp.where(inside, logits, -jnp.inf), 1, keepdims=True)
    shifted = jnp.where(inside, logits - top, 0.0)
    powers = jnp.where(inside, jnp.exp(shifted), 0.0)
    sum_powers = jnp.sum(powers, 1, keepdims=True)
    hot = hot_ref[...]
    losses = jnp.log(sum_powers) - jnp.sum(hot * shifted, 1, keepdims=True)
    single = (lax.broadcasted_iota(jnp.int32, (rows, 1), 0) % QUARTERS == 0).astype(f32)
    loss = jnp.sum(losses * weight * single, 0, keepdims=True)
    grad_low = ((weight / weight_total) * (powers / sum_powers - hot)).astype(bf16)
    grad_once = grad_low * single.astype(bf16)
    bias_grad = jnp.sum(grad_once.astype(f32), 0, keepdims=True)
    head_ref[...] = lax.dot_general(
        grad_once, pooled_low, (((0,), (0,)), ((), ())), preferred_element_type=f32
    )
    extra = jnp.where(lax.broadcasted_iota(jnp.int32, (1, 128), 1) == 127, loss, bias_grad)
    spread = jnp.dot(grad_low, back_ref[...], preferred_element_type=f32) / count

    def scatter(i, carry):
        first_sum, second_sum = carry
        tiles, others = [], []
        for u in range(UNROLL):
            J = i * UNROLL + u
            for s in range(NI):
                low = (spread * grads[s, J].astype(f32)).astype(bf16)
                dy_ref[s, J] = low
                tiles.append(low)
                others.append(low * c_ref[s, J])
        first_sum += tree(summed(tiles[k : k + NI]) for k in range(0, len(tiles), NI))
        second_sum += tree(summed(others[k : k + NI]) for k in range(0, len(others), NI))
        return first_sum, second_sum

    zero = jnp.zeros((8, LANES), f32)
    first_sum, second_sum = lax.fori_loop(0, NJ // UNROLL, scatter, (zero, zero))
    first_sum = jnp.sum(first_sum, 0, keepdims=True)
    second_sum = (jnp.sum(second_sum, 0, keepdims=True) - mean * first_sum) * scale
    send(stat_ref, message(first_sum, second_sum), extra)


def pieces_of(row):
    high = row.astype(bf16).astype(f32)
    middle = (row - high).astype(bf16).astype(f32)
    low = row - high - middle
    return [part[:, at : at + 64] for part in (high, middle, low) for at in (0, 64)]


def carried_lanes(width):
    return 576 + 64 * (-(-6 // width))


def carry(ref, weights, row, narrow):
    width = ref.shape[1]
    pieces = pieces_of(row)
    pieces += [jnp.zeros((1, 64), f32)] * (-len(pieces) % width)
    tail = [
        jnp.concatenate(pieces[at : at + width], 0) for at in range(0, len(pieces), width)
    ]
    for j in range(ref.shape[0] // narrow):
        rows = weights[j * width : (j + 1) * width]
        block = jnp.concatenate([rows, *tail], 1).astype(bf16)
        for n in range(narrow):
            ref[j * narrow + n] = block


def carried_totals(ref):
    width = ref.shape[1]
    total = tree(ref[d][:, 576:].astype(f32) for d in range(ref.shape[0]))
    found = [
        total[k % width : k % width + 1, 64 * (k // width) : 64 * (k // width) + 64]
        for k in range(6)
    ]
    halves = [found[k] + found[k + 2] + found[k + 4] for k in range(2)]
    return tuple(jnp.concatenate([half] * 4, 1) for half in halves)


def grad_constants(sums_ref, gath_ref, counted, norm4, index):
    first_total, second_total = sums_ref if isinstance(sums_ref, tuple) else totals(sums_ref)
    mean, scale, slope, _ = norm_constants(gath_ref, counted, norm4, index)
    along = -slope * scale * second_total / counted
    return slope, along, -slope * first_total / counted - along * mean


def backward_kernel(*refs, index, residual, adding, ordered, carrying, valued, kept, devices):
    inputs = 3 + residual + adding
    far_in, refs = refs[:inputs], refs[inputs:]
    refs = refs[:8] + refs[8 + ordered :]
    if carrying:
        weights_ref, carried_ref = refs[8], refs[12]
        refs = refs[:8] + refs[9:12] + refs[13:]
    if not valued:
        refs = refs[:10] + (None,) + refs[10:]
    if kept:
        refs += refs[8:11]
    (
        sums_ref, gath_ref, gath_prev_ref, first_ref, norm_ref, mask_ref, q_ref, w_ref,
        out_far, grad_far, value_far, stat_ref, ring, side, offsets, sums, sems, matrix,
        matrix_sem, out_ref, grad_ref, value_ref,
    ) = refs[:22]
    held = list(far_in)
    results = [(out_far, out_ref), (grad_far, grad_ref), (value_far, value_ref)][: 2 + valued]
    saves = None if kept else Streams(*zip(*results), sems, 0, UNROLL)
    fetch = pltpu.make_async_copy(w_ref, matrix, matrix_sem)
    fetch.start()
    dy_ref = held.pop(0)
    c_ref, prev_ref = held[:2]
    res_ref = held[2] if residual else None
    add_ref = held[-1] if adding else None
    rows = c_ref.shape[2]
    counted = pixels_of(first_ref)
    grad_slope, grad_along, grad_start = grad_constants(
        sums_ref, gath_ref, counted, norm_ref, index
    )
    mean, scale, slope, start = norm_constants(gath_prev_ref, counted, norm_ref, index - 1)
    half_slope, half_start = slope * 0.5, start * 0.5
    lanes = half_lanes(rows)
    sums[...] = jnp.zeros_like(sums)
    for a in range(3):
        for b in range(2):
            offsets[a, b] = grad_start * twice(mask_ref[a, b])

    def activate(J, slot):
        Jc = jnp.minimum(J, NJ - 1)
        jm = mask_row(J)
        slope_now, along_now = grad_slope, grad_along
        if slot > UNROLL:
            present = jnp.where(J < NJ, 1.0, 0.0)
            slope_now, along_now = grad_slope * present, grad_along * present
        for s in range(NI):
            grad = dy_ref[s, Jc].astype(f32) * slope_now + (
                c_ref[s, Jc].astype(f32) * along_now + offsets[jm, 0 if s == 0 else 1]
            )
            put_column(ring, slot, s, grad, grad.astype(bf16), q_ref)

    def multiply():
        for u in range(UNROLL):
            side_columns(ring, side, u, lanes)
        parts = [operands(ring, side, u) for u in range(UNROLL)]
        return product(
            [jnp.concatenate([part[k] for part in parts], 0) for k in range(4)], matrix
        )

    def convolve(J, u, everything):
        total = everything[u * NI * rows : (u + 1) * NI * rows]
        jm = mask_row(J)
        tiles, others = [], []
        for s in range(NI):
            grad_ref[s, J] = ring[u + 1, s + 1]
            half = prev_ref[s, J].astype(f32) * half_slope + half_start
            if residual:
                half = half + 0.5 * res_ref[s, J].astype(f32)
            sigma = (0.5 + 0.5 * jnp.tanh(half)) * twice(mask_ref[jm, 0 if s == 0 else 1])
            value = (half + half) * sigma
            if valued:
                value_ref[s, J] = value.astype(bf16)
            tile = total[s * rows : (s + 1) * rows]
            if adding:
                tile = tile + add_ref[s, J].astype(f32)
            tile = tile * (sigma + value - value * sigma)
            low = tile.astype(bf16)
            out_ref[s, J] = low
            tiles.append(low)
            others.append(low * prev_ref[s, J])
        sums[0, u] += summed(tiles)
        sums[1, u] += summed(others)

    ring[UNROLL] = jnp.zeros(ring.shape[1:], bf16)
    activate(0, UNROLL + 1)
    fetch.wait()

    def step(i, carry):

        for k in range(2):
            ring[k] = ring[UNROLL + k]
        for u in range(UNROLL):
            activate(i * UNROLL + u + 1, u + 2)
        everything = multiply()
        for u in range(UNROLL):
            convolve(i * UNROLL + u, u, everything)
        if not kept:
            saves.start_save(i)
        return carry

    lax.fori_loop(0, GROUPS, step, 0)
    first_sum = total_of(sums, 0)
    second_sum = (total_of(sums, 1) - mean * first_sum) * scale
    row = message(first_sum, second_sum)
    send(stat_ref, row)
    if carrying:
        carry(carried_ref, weights_ref[...].astype(f32), row, carrying)
    for i in range(0 if kept else GROUPS):
        saves.wait_save(i)


def weight_grad_kernel(*refs, slot_out, continued, fetching, kept):
    grad_far, value_far, q_ref = refs[:3]
    refs = refs[3 + kept + continued :]
    far, refs = refs[:fetching], refs[fetching:]
    out_ref, token_ref, near, refs = refs[0], refs[1], refs[2 : 2 + fetching], refs[2 + fetching :]
    token_ref[...] = jnp.zeros_like(token_ref)
    ring, side, acc, sems, piece_ref, piece_sem, fetch_sems = refs[:7]
    grad_in_ref, value_ref = (grad_far, value_far) if kept else refs[7:]
    fetches = Streams(far, near, fetch_sems, 0, UNROLL)
    loads = Streams([grad_far, value_far], [grad_in_ref, value_ref], sems, 0)
    for i in range(0 if kept else CHUNKS):
        loads.start_load(i)
    rows = value_ref.shape[2]
    lanes = half_lanes(rows)

    def load(J, slot):
        Jc = jnp.minimum(J, NJ - 1)
        some = jnp.where(J < NJ, 1.0, 0.0)
        for s in range(NI):
            low = value_ref[s, Jc]
            if slot == UNROLL + 1:
                low = low * some.astype(bf16)
            put_column(ring, slot, s, low.astype(f32), low, q_ref)

    ring[UNROLL] = jnp.zeros(ring.shape[1:], bf16)
    if not kept:
        loads.wait_load(0)
    load(0, UNROLL + 1)

    def step(i, carry):
        fetches.start_load(i)
        if not kept:
            loads.wait_load(2 * i + 1)
            loads.when(2 * i + 2 < CHUNKS, loads.wait_load, 2 * i + 2)
        for k in range(2):
            ring[k] = ring[UNROLL + k]
        for u in range(UNROLL):
            load(i * UNROLL + u + 1, u + 2)
        for u in range(UNROLL):
            side_columns(ring, side, u, lanes)
        grad = jnp.concatenate(
            [grad_in_ref[:, i * UNROLL + u] for u in range(UNROLL)], 0
        ).reshape(UNROLL * NI * rows, LANES)
        parts = [operands(ring, side, u) for u in range(UNROLL)]
        for k in range(4):
            value = jnp.concatenate([parts[u][k] for u in range(UNROLL)], 0)
            piece = lax.dot_general(
                grad, value, (((0,), (0,)), ((), ())), preferred_element_type=f32
            )
            at = slice(k * LANES, (k + 1) * LANES)
            acc[:, at] = jnp.where(i == 0, piece, acc[:, at] + piece)
        return carry

    lax.fori_loop(0, GROUPS, step, 0)
    taps = [None] * 9
    for slot in range(16):
        for out in range(4):
            tap = tap_of(slot, out)
            if tap is not None:
                piece = acc[out * 64 : (out + 1) * 64, slot * 64 : (slot + 1) * 64]
                taps[tap] = piece if taps[tap] is None else taps[tap] + piece
    for i in range(GROUPS):
        fetches.wait_load(i)
    result = jnp.concatenate(taps, 1)
    if slot_out is None:
        out_ref[...] = result.astype(bf16)
    else:
        width = piece_ref.shape[1]
        for j in range(piece_ref.shape[0]):
            piece_ref[j] = result[j * width : (j + 1) * width].astype(bf16)
        copy = pltpu.make_async_copy(piece_ref, out_ref.at[:, slot_out], piece_sem)
        copy.start()
        copy.wait()


def stem_back_kernel(
    dy_far, c_far, z_ref, sums_ref, gath_ref, norm_ref, mask_ref, table_ref, conv_ref, head_ref,
    *refs
):
    stat_refs, (out_ref, dy_ref, held, raw, sems) = refs[:7], refs[7:]
    loads = Streams([dy_far, c_far], [dy_ref, held], sems, 0, NI)
    for k in range(NJ // NI):
        loads.start_load(k)
    rows = held.shape[2]
    counted = pixels_of(gath_ref)
    slope, along, start = grad_constants(
        carried_totals(sums_ref), gath_ref, counted, norm_ref, 0
    )
    span = 2 * NI
    deep = (span + 2) * 4
    for block in range(NJ // NI):
        loads.wait_load(block)
        for j in range(NI):
            J = block * NI + j
            total = None
            for s in range(NI):
                at = (block * (span + 2) + 2 * s) * deep
                mask = twice(mask_ref[0 if J < SHORT_J else 1, 0 if s == 0 else 1])
                grad = dy_ref[s, J].astype(f32) * slope + held[s, J].astype(f32) * along
                piece = jnp.dot(
                    z_ref[at : at + 4 * deep][:, :rows],
                    ((grad + start) * mask).astype(bf16),
                    preferred_element_type=f32,
                )
                total = piece if total is None else total + piece
            at = slice(j * LANES, (j + 1) * LANES)
            raw[:, at] = total if block == 0 else raw[:, at] + total
    parts = [raw[:, k * 64 : (k + 1) * 64].astype(bf16) for k in range(NI * 4)]
    total = lax.dot_general(
        jnp.concatenate(parts, 0),
        table_ref[...].reshape(NI * 4 * 4 * deep, 32),
        (((0,), (0,)), ((), ())),
        preferred_element_type=f32,
    )
    stats = jnp.concatenate([ref[0:1] if len(ref.shape) == 2 else ref[0, 0:1] for ref in stat_refs], 0)
    shifts, gains = stats[:, :64], stats[:, 64:]
    norms = jnp.concatenate([gains, shifts, jnp.zeros((2, 64), f32)], 0).T
    head = head_ref[:, :64].T
    extra = jnp.concatenate([total[:, :27], norms[:, :14], head[:, :23]], 1)
    out_ref[...] = jnp.concatenate([conv_ref[...].astype(f32), extra], 1).astype(bf16)


def chain_kernel(
    early_ref, late_ref, last_ref, noise_ref, conv_ref, stem_ref, head_ref, conv_out, extra_out,
    square_ref, *, devices
):
    count, width = early_ref.shape[0], early_ref.shape[2]
    narrow = devices // count
    member = lax.axis_index("wide")

    def partial(w):
        last = tree(last_ref[w * narrow + n].astype(f32) for n in range(narrow))
        late = tree(late_ref[w * narrow + n][:, :576].astype(f32) for n in range(narrow))
        return (
            [last[:, :576], late] + [early_ref[w, k].astype(f32) for k in range(4)],
            last[:, 576:],
        )

    def place(k):
        return lax.rem(member + k, count)

    def hop(k, carried):
        conv, extra = carried
        top = jnp.max(jnp.abs(extra), keepdims=True)
        for piece in conv:
            top = jnp.maximum(top, jnp.max(jnp.abs(piece), keepdims=True))
        scale = top + 1e-06
        sender = place(k)
        more, more_extra = partial(place(k + 1))

        def passed(value, dither, added):
            level = (value / scale * levels + dither.astype(f32)).astype(bf16)
            return level.astype(f32) * scale / levels + added

        conv = [passed(conv[m], noise_ref[sender, m], more[m]) for m in range(6)]
        dither = noise_ref[sender, 6][:, :64]
        known = lax.broadcasted_iota(jnp.int32, extra.shape, 1) < 41 + head_ref.shape[1]
        return conv, jnp.where(known, passed(extra, dither, more_extra), 0.0)

    conv, extra = lax.fori_loop(1, count, hop, partial(place(1)))
    head = head_ref[...]
    masters = jnp.concatenate(
        [
            stem_ref[...], jnp.zeros((width, 14), f32), head,
            jnp.zeros((width, 64 - 41 - head.shape[1]), f32),
        ],
        1,
    )
    extra = extra + weight_decay * masters
    total = jnp.sum(extra * extra, keepdims=True)
    for m in range(6):
        value = conv[m] + weight_decay * conv_ref[m]
        conv_out[m] = value
        total = total + jnp.sum(value * value, keepdims=True)
    extra_out[...] = jnp.concatenate([extra, extra], 1)
    square_ref[...] = jnp.broadcast_to(total, square_ref.shape)


def adam_kernel(square_ref, heads_ref, first_ref, conv_ref, extra_ref, *refs, classes):
    news, held, sems = refs[15:33], refs[33:48], refs[48]
    copies = [pltpu.make_async_copy(refs[k], held[k], sems.at[k]) for k in range(15)]
    for copy in copies:
        copy.start()
    olds = held
    bias = jnp.sum(heads_ref[:, 1, :], 0, keepdims=True)
    loss = bias[:, 127:128]
    bias = bias[:, :classes]
    total = jnp.sum(square_ref[...][:, 0:1], 0, keepdims=True)
    total = total + jnp.sum(bias * bias, keepdims=True)
    norm = jnp.sqrt(total)
    factor = clip_limit / jnp.maximum(norm, clip_limit)
    extra = extra_ref[...]
    turned = extra.T
    parts = (
        (extra[:, :27],), tuple(conv_ref[m] for m in range(6)),
        (turned[27:34], turned[34:41]), (extra[:, 41 : 41 + classes],), (bias,),
    )
    for copy in copies:
        copy.wait()
    for k, pieces in enumerate(parts):
        master, first, second = olds[3 * k : 3 * k + 3]
        for m, gradient in enumerate(pieces):
            at = {6: (m,), 2: (slice(None), m)}.get(len(pieces), ())
            results = adam_update(gradient, first[at], second[at], master[at], factor)
            for ref, value in zip(news[3 * k : 3 * k + 3], results):
                ref[at] = value
    news[15][...] = norm
    news[16][...] = loss
    news[17][...] = jnp.sum(first_ref[:, 1, 1:2], 0, keepdims=True)


def stem_table():
    span = 2 * NI + 2
    table = np.zeros((NI * 4, 4, span, 4, 27), np.float32)
    for j in range(NI):
        for out in range(4):
            for ky in range(3):
                for kx in range(3):
                    for i in range(3):
                        table[
                            j * 4 + out, out // 2 + ky, 2 * j + out % 2 + kx, i,
                            (ky * 3 + kx) * 3 + i,
                        ] = 1.0
    return np.pad(table.reshape(NI * 4, 4 * span * 4, 27), ((0, 0), (0, 0), (0, 5)))


def adam_update(gradient, first, second, master, factor):
    clipped = gradient * factor
    new_first = first_decay * first + (1.0 - first_decay) * clipped
    new_second = second_decay * second + (1.0 - second_decay) * clipped * clipped
    corrected = (
        new_first
        / (1.0 - first_decay**STEP)
        / (jnp.sqrt(new_second / (1.0 - second_decay**STEP)) + adam_epsilon)
    )
    return (master - learn_rate * (corrected + decoupled * master), new_first, new_second)


def shared(rows):
    return lax.all_to_all(rows, BOTH, 0, 0, tiled=True)


def body(
    images,
    large_flag,
    labels,
    example_weights,
    cycle_noise,
    stem_weight,
    conv_weight,
    norm_params,
    head_weight,
    head_bias,
    stem_first,
    stem_second,
    conv_first,
    conv_second,
    norm_first,
    norm_second,
    head_first,
    head_second,
    bias_first,
    bias_second,
):
    wide_count = lax.axis_size("wide")
    devices = wide_count * lax.axis_size("narrow")
    count = large_flag.shape[0]
    rows = QUARTERS * count
    width = stem_weight.shape[0]
    channels = width * wide_count
    classes = head_weight.shape[0]
    assert channels == 64 and rows % 16 == 0 and rows <= 128

    member = lax.axis_index("wide")

    def to_wide(value):
        return lax.all_to_all(value, "wide", 0, 0, tiled=True)

    owned = (stem_weight, conv_weight, norm_params.transpose(1, 0, 2), head_weight.T)
    packed = call(
        pack_kernel,
        (jax.ShapeDtypeStruct((wide_count, 7, width, 576), bf16),),
        [pltpu.VMEM(value.shape, f32) for value in owned] + [pltpu.SemaphoreType.DMA((4,))],
        owned,
        "pack",
        stored=(0, 1, 2, 3),
        limit=8,
    )[0]
    packed = to_wide(packed)
    bias_row = jnp.pad(head_bias[None, :], ((0, 0), (0, 128 - classes)))

    dither = ((cycle_noise[0].astype(f32) + 0.5) / 65536.0 - 0.5).astype(bf16)
    hop_row = (member - 1 - jnp.arange(wide_count, dtype=jnp.int32)) % wide_count
    dither = jnp.take(dither, jnp.minimum(hop_row, wide_count - 2), axis=0)
    one, two, three = width * 27, width * 27 + 6 * width * 576, width * 41 + 6 * width * 576
    extra = jnp.concatenate(
        [
            dither[:, :one].reshape(wide_count, width, 27),
            dither[:, two:three].reshape(wide_count, 14, width).transpose(0, 2, 1),
            dither[:, three:].reshape(wide_count, classes, width).transpose(0, 2, 1),
        ],
        2,
    )
    extra = jnp.pad(extra, ((0, 0), (0, 0), (0, 576 - extra.shape[2])))
    dither = jnp.concatenate(
        [dither[:, one:two].reshape(wide_count, 6, width, 576), extra[:, None]], 1
    )

    large = large_flag == 1
    row_large = jnp.repeat(large, QUARTERS)
    quarter = jnp.arange(rows, dtype=jnp.int32) % QUARTERS
    upper = row_large | (quarter < SHORT_J // NI)
    ones = jnp.ones((rows,), bool)
    none = jnp.zeros((rows,), bool)
    mask_table = jnp.stack(
        [jnp.stack([ones, upper]), jnp.stack([row_large, row_large]), jnp.stack([none, none])]
    )
    mask_table = jnp.broadcast_to(mask_table[..., None], (3, 2, rows, 128)).astype(f32)
    q_table = jnp.broadcast_to(
        jnp.stack([quarter != QUARTERS - 1, quarter != 0])[..., None], (2, rows, 128)
    ).astype(f32)
    sides = jnp.where(large, SIDE, SHORT).astype(jnp.int32)
    weights_f = example_weights.astype(f32)
    lane = jnp.arange(128, dtype=jnp.int32)[None, :]
    info = jnp.where(
        lane == 0,
        jnp.repeat((sides * sides).astype(f32), QUARTERS)[:, None],
        jnp.where(lane == 1, jnp.repeat(weights_f, QUARTERS)[:, None], 0.0),
    )
    hot = (jnp.repeat(labels, QUARTERS)[:, None] == lane).astype(f32)

    span = 2 * NI
    position = jnp.arange(span * SIDE, dtype=jnp.int32)
    inside = row_large[:, None] | (
        (quarter[:, None] * span + (position // SIDE)[None, :] < SHORT)
        & ((position % SIDE)[None, :] < SHORT)
    )
    planes = images.reshape(3, rows, span * SIDE) * inside.astype(bf16)[None]

    (planes, mask_table, q_table, info, hot, bias_row, dither, packed) = (
        lax.optimization_barrier(
            (planes, mask_table, q_table, info, hot, bias_row, dither, packed)
        )
    )
    dither = to_wide(dither)
    table = jnp.asarray(stem_table(), bf16)
    norm4, into_head, from_head, stem_wide = call(
        small_kernel,
        (
            jax.ShapeDtypeStruct((16, LANES), f32),
            jax.ShapeDtypeStruct((128, 128), bf16),
            jax.ShapeDtypeStruct((128, LANES), bf16),
            jax.ShapeDtypeStruct((table.shape[1], NI * LANES), bf16),
        ),
        [],
        (packed, table),
        "small",
        limit=12,
    )
    matrices = call(
        weights_kernel,
        (Stored((1024, LANES)),) * 12,
        [pltpu.VMEM((12, 1024, LANES), bf16), pltpu.SemaphoreType.DMA((12,))],
        (packed,),
        "weights",
        limit=16,
    )

    z_rows = (SIDE // span) * (span + 2) * (span + 2) * 4
    full = pltpu.VMEM((NI, NJ, rows, LANES), bf16)
    side_shape = (UNROLL, NI + 2, rows, LANES)
    sets = [
        pltpu.VMEM((BLOCK + 2, NI + 2, rows, LANES), bf16),
        pltpu.VMEM((BLOCK, NI + 2, rows, LANES), bf16),
        pltpu.VMEM((BLOCK * NI * rows, LANES), f32),
    ] * 2
    stat = jax.ShapeDtypeStruct((devices, 128), f32)

    c0_saved, z, stat0 = call(
        functools.partial(stem_kernel, devices=devices),
        (
            stored_field(rows),
            jax.ShapeDtypeStruct((z_rows, 128), bf16),
            jax.ShapeDtypeStruct((devices, 2, 128), f32),
        ),
        [pltpu.VMEM((z_rows, 128), f32), full, pltpu.SemaphoreType.DMA((SIDE // span,))],
        (planes, stem_wide, mask_table, info),
        "stem",
    )
    current, saved = c0_saved, [c0_saved]
    stat0, norm4, into_head, from_head, dither, *matrices = lax.optimization_barrier(
        (stat0, norm4, into_head, from_head, dither, *matrices)
    )
    gathered = [shared(stat0)]
    stream, streams = None, []
    ahead, back = matrices[:6], matrices[6:]
    for layer in range(1, 7):
        keep = layer % 2 == 1
        residual = keep and layer > 1
        args = (current,) + ((stream,) if residual else ())
        args += (gathered[layer - 1], gathered[0], norm4, mask_table, q_table, ahead[layer - 1])
        outs = call(
            functools.partial(
                forward_kernel, index=layer - 1, keep=keep, residual=residual,
                streamed=layer == 1, devices=devices,
            ),
            (field(rows), stored_field(rows)) * (2 if keep else 1) + (stat,),
            [
                pltpu.VMEM((2, BLOCK, 8, LANES), f32),
                pltpu.SemaphoreType.DMA((2, CHUNKS)),
            ]
            + sets
            + (
                [
                    full,
                    pltpu.SemaphoreType.DMA((1, CHUNKS)),
                    pltpu.VMEM((1024, LANES), bf16),
                    pltpu.SemaphoreType.DMA,
                ]
                if layer == 1
                else []
            ),
            args,
            "forward",
            cost=int(7e9),
            limit=24,
            stored=(0, len(args) - 1) if layer == 1 else (),
        )
        before, current = current, outs[0]
        saved.append(outs[1])
        if keep:
            stream = outs[2]
            streams.append(outs[3])
        gathered.append(shared(outs[-1]))

    dys = [None] * 7
    stats = [None] * 7
    dys[6], stats[6], head_grad = call(
        functools.partial(head_kernel, classes=classes, devices=devices),
        (
            field(rows),
            jax.ShapeDtypeStruct((devices, 2, 128), f32),
            jax.ShapeDtypeStruct((128, 128), f32),
        ),
        [
            full,
            pltpu.VMEM((rows, LANES), f32),
        ],
        (
            current, stream, gathered[6], gathered[0], norm4, mask_table, hot, info,
            into_head, from_head, bias_row,
        ),
        "head",
        cost=int(8e9),
        limit=28,
    )
    def needed(layer):
        fields = (dys[layer], saved[layer], saved[layer - 1])
        fields += (streams[layer // 2 - 1],) if layer in (5, 3) else ()
        return fields + ((dys[layer + 1],) if layer % 2 == 1 else ())

    fetched = (dys[6], current, before)
    tokens = ()
    narrow_count = devices // wide_count
    carried_shape = (devices, width, carried_lanes(width))
    for layer in range(6, 0, -1):
        residual = layer in (5, 3)
        adding = layer % 2 == 1
        if layer == 6:
            heads = sums = shared(stats[6])
        args = fetched
        inputs = len(args)
        args += (
            sums, gathered[layer], gathered[layer - 1], gathered[0], norm4, mask_table, q_table,
            back[layer - 1], *tokens, *((late,) if layer == 1 else ()),
        )
        kept = int(layer > 1)
        valued = kept
        outs = call(
            functools.partial(
                backward_kernel, index=layer, residual=residual, adding=adding,
                ordered=len(tokens), carrying=narrow_count if layer == 1 else 0,
                valued=valued, kept=kept, devices=devices,
            ),
            ((field(rows) if kept else stored_field(rows)),) * (2 + valued)
            + (stat,)
            + ((jax.ShapeDtypeStruct(carried_shape, bf16),) if layer == 1 else ()),
            [
                pltpu.VMEM((UNROLL + 2, NI + 2, rows, LANES), bf16),
                pltpu.VMEM(side_shape, bf16),
                pltpu.VMEM((3, 2, rows, LANES), f32),
                pltpu.VMEM((2, UNROLL, 8, LANES), f32),
                pltpu.SemaphoreType.DMA((8, GROUPS)),
                pltpu.VMEM((1024, LANES), bf16),
                pltpu.SemaphoreType.DMA,
            ]
            + ([] if kept else [full] * 3),
            args,
            "backward",
            cost=int(8e9),
            limit=14 if kept else 30,
            stored=(inputs + 7,),
        )
        dys[layer - 1], grad, stats[layer - 1] = outs[0], outs[1], outs[2 + valued]
        carried = outs[3:]
        value = outs[2] if valued else streams[(layer - 1) // 2]
        sums = shared(stats[layer - 1]) if kept else None
        slot_out = layer - 3 if layer > 2 else None
        shape = (wide_count, 4, width, 576)
        args = (grad, value, q_table) + ((sums,) if kept else ())
        outs = (jax.ShapeDtypeStruct((64, 576), bf16), jax.ShapeDtypeStruct((8, 128), f32))
        aliases = {}
        if 2 < layer < 6:
            aliases[len(args)] = 0
            args += (early,)
        if layer > 2:
            outs = (Stored(shape), outs[1])
        continued = len(args) - 3 - kept
        wanted = needed(layer - 1)[1 : 4 if layer in (6, 4) else 3] if layer > 1 else ()
        args += wanted
        outs += (field(rows),) * len(wanted)
        result, token, *fetched = call(
            functools.partial(
                weight_grad_kernel, slot_out=slot_out, continued=continued,
                fetching=len(wanted), kept=kept,
            ),
            outs,
            [
                pltpu.VMEM((UNROLL + 2, NI + 2, rows, LANES), bf16),
                pltpu.VMEM(side_shape, bf16),
                pltpu.VMEM((LANES, 1024), f32),
                pltpu.SemaphoreType.DMA((2, CHUNKS)),
                pltpu.VMEM((wide_count, width, 576), bf16),
                pltpu.SemaphoreType.DMA,
                pltpu.SemaphoreType.DMA((3, GROUPS)),
            ]
            + ([] if kept else [full, full]),
            args,
            "weight_grad",
            cost=int(7e9),
            limit=14 if kept else 24,
            stored=(() if kept else (0, 1)) + tuple(range(3 + kept, len(args))),
            aliases=aliases,
        )
        tokens = (token,)
        fetched = (dys[layer - 1],) + tuple(fetched) + ((dys[layer],) if layer in (6, 4, 2) else ())
        if layer > 2:
            early = result
        if layer == 3:
            early = lax.psum(early, "narrow")
        if layer == 2:
            late = result
    carried = shared(carried[0])
    early = to_wide(early)
    last = call(
        stem_back_kernel,
        (jax.ShapeDtypeStruct((64, 640), bf16),),
        [
            full,
            full,
            pltpu.VMEM((4 * (span + 2) * 4, NI * LANES), f32),
            pltpu.SemaphoreType.DMA((2, NJ // NI)),
        ],
        (
            dys[0], saved[0], z, carried, gathered[0], norm4, mask_table, table,
            result, head_grad, *stats,
        ),
        "stem_back",
        stored=(0, 1),
        cost=int(5e9),
    )[0]
    last = jnp.broadcast_to(
        last.reshape(wide_count, 1, width, 640), (wide_count, narrow_count, width, 640)
    )
    last = shared(last.reshape(devices, width, 640))
    conv_total, extra_total, squares = call(
        functools.partial(chain_kernel, devices=devices),
        (
            jax.ShapeDtypeStruct((6, width, 576), f32),
            jax.ShapeDtypeStruct((width, 128), f32),
            jax.ShapeDtypeStruct((wide_count, 128), f32),
        ),
        [],
        (early, carried, last, dither, conv_weight, stem_weight, head_weight.T),
        "chain",
    )
    olds = (
        stem_weight, stem_first, stem_second, conv_weight, conv_first, conv_second,
        *(value.transpose(1, 0, 2) for value in (norm_params, norm_first, norm_second)),
        head_weight.T, head_first.T, head_second.T,
        head_bias[None], bias_first[None], bias_second[None],
    )
    single = jax.ShapeDtypeStruct((1, 1), f32)
    news = call(
        functools.partial(adam_kernel, classes=classes),
        tuple(Result(old.shape, f32) for old in olds) + (single,) * 3,
        [pltpu.VMEM(old.shape, f32) for old in olds] + [pltpu.SemaphoreType.DMA((15,))],
        (to_wide(squares), heads, gathered[0], conv_total, extra_total, *olds),
        "adam",
        stored=tuple(range(5, 20)),
        limit=12,
    )
    return (
        *news[:6],
        *(new.transpose(1, 0, 2) for new in news[6:9]),
        *(new.T for new in news[9:12]),
        *(new[0] for new in news[12:15]),
        *(new[0, 0] for new in news[15:]),
    )


def solution(mesh):
    split = P(BOTH)
    ins = (
        P(None, BOTH), split, split, split, P("wide", None, None),
        P("wide", None), P(None, "wide", None), P(None, None, "wide"), P(None, "wide"), P(),
        P("wide", None), P("wide", None), P(None, "wide", None), P(None, "wide", None),
        P(None, None, "wide"), P(None, None, "wide"), P(None, "wide"), P(None, "wide"), P(), P(),
    )
    outs = (
        (P("wide", None),) * 3
        + (P(None, "wide", None),) * 3
        + (P(None, None, "wide"),) * 3
        + (P(None, "wide"),) * 3
        + (P(),) * 6
    )
    return jax.shard_map(body, mesh=mesh, in_specs=ins, out_specs=outs, check_vma=False)
```

```python
import functools

import jax
import jax.numpy as jnp
import numpy as np
from jax import lax
from jax.experimental import pallas as pl
from jax.experimental.pallas import tpu as pltpu
from jax.sharding import PartitionSpec as P

SIDE = 40
SHORT = 32
STEP = 10

norm_epsilon = 1e-05
clip_limit = 0.002
learn_rate = 0.4
first_decay = 0.9
second_decay = 0.999
adam_epsilon = 1e-08
weight_decay = 0.0005
decoupled = 0.01
levels = 15.0

QUARTERS = 4
PATCHES = SIDE // 2
NI = PATCHES // QUARTERS
NJ = PATCHES
SHORT_J = SHORT // 2
LANES = 256
UNROLL = 4
BLOCK = 2

f32 = jnp.float32
bf16 = jnp.bfloat16
BOTH = ("wide", "narrow")


def window_place(slot):
    group, sy, sx = slot // 4, (slot // 2) % 2, slot % 2
    wx = 1 + sx if group in (0, 2) else (3 if sx == 0 else 0)
    wy = 1 + sy if group in (0, 1) else (3 if sy == 0 else 0)
    return wy, wx


def tap_of(slot, out):
    wy, wx = window_place(slot)
    ky, kx = wy - out // 2, wx - out % 2
    if 0 <= ky < 3 and 0 <= kx < 3:
        return ky * 3 + kx
    return None


def whole():
    return pl.BlockSpec(memory_space=pltpu.VMEM)


def call(kernel, outs, scratch, args, name, cost=None, limit=24, stored=(), aliases=None):
    def place(out):
        return pl.BlockSpec(memory_space=pltpu.HBM) if type(out) is Stored else whole()

    def shape(out):
        kind = pltpu.HBM if isinstance(out, (Stored, Result)) else jax.ShapeDtypeStruct
        return kind(out.shape, out.dtype)

    args = [
        pltpu.with_memory_space_constraint(arg, pltpu.HBM) if k in stored else arg
        for k, arg in enumerate(args)
    ]

    return pl.pallas_call(
        kernel,
        out_shape=tuple(shape(out) for out in outs),
        in_specs=[
            pl.BlockSpec(memory_space=pltpu.HBM) if k in stored else whole()
            for k in range(len(args))
        ],
        out_specs=tuple(place(out) for out in outs),
        scratch_shapes=scratch,
        compiler_params=pltpu.CompilerParams(vmem_limit_bytes=limit * 2**20),
        name=name,
        input_output_aliases=aliases or {},
        cost_estimate=pl.CostEstimate(flops=cost, bytes_accessed=2**20, transcendentals=0)
        if cost
        else None,
    )(*args)


class Stored:
    def __init__(self, shape, dtype=bf16):
        self.shape, self.dtype = shape, dtype


class Result(Stored):
    pass


def stored_field(rows):
    return Stored((NI, NJ, rows, LANES))


class Streams:
    def __init__(self, outside, inside, sems, base, columns=None):
        self.outside, self.inside = tuple(outside), tuple(inside)
        self.sems, self.base, self.columns = sems, base, columns or BLOCK

    def pairs(self, i):
        for k, (far, near) in enumerate(zip(self.outside, self.inside)):
            at = pl.ds(i * self.columns, self.columns)
            yield far.at[:, at], near.at[:, at], self.sems.at[self.base + k, i]

    def when(self, condition, action, i):
        @pl.when(condition)
        def _():
            action(i)

    def start_load(self, i):
        for far, near, sem in self.pairs(i):
            pltpu.make_async_copy(far, near, sem).start()

    def wait_load(self, i):
        for far, near, sem in self.pairs(i):
            pltpu.make_async_copy(far, near, sem).wait()

    def wait_loads(self, i):
        self.wait_load(i)
        self.wait_load(i + 1)

    def start_save(self, i):
        for far, near, sem in self.pairs(i):
            pltpu.make_async_copy(near, far, sem).start()

    def wait_save(self, i):
        for far, near, sem in self.pairs(i):
            pltpu.make_async_copy(near, far, sem).wait()


CHUNKS = NJ // BLOCK
GROUPS = NJ // UNROLL


def field(rows):
    return jax.ShapeDtypeStruct((NI, NJ, rows, LANES), bf16)


def wide_pair(row):
    turned = pltpu.roll(row, 64, 1)
    lower = lax.broadcasted_iota(jnp.int32, row.shape, 1) < 64
    first = jnp.where(lower, row, turned)
    second = jnp.where(lower, turned, row)
    return jnp.concatenate([first, first], 1), jnp.concatenate([second, second], 1)


def folded(row):
    half = row[:, :128] + row[:, 128:]
    return half + pltpu.roll(half, 64, 1)


def message(first, second):
    lower = lax.broadcasted_iota(jnp.int32, (1, 128), 1) < 64
    return jnp.where(lower, folded(first), folded(second))


def totals(gathered):
    rows = gathered[:, 0, :] if len(gathered.shape) == 3 else gathered[...]
    return wide_pair(jnp.sum(rows, 0, keepdims=True))


def send(ref, first, second=None):
    if second is None:
        ref[...] = jnp.broadcast_to(first, ref.shape)
    else:
        both = jnp.concatenate([first, second], 0)[None]
        ref[...] = jnp.broadcast_to(both, ref.shape)


def norm_constants(gathered, counted, norm4, index):
    sums, squares = totals(gathered)
    mean = sums / counted
    scale = lax.rsqrt(squares / counted - mean * mean + norm_epsilon)
    gain = norm4[index : index + 1]
    slope = gain * scale
    return mean, scale, slope, norm4[7 + index : 8 + index] - mean * slope


def pixels_of(gathered_first):
    return jnp.sum(gathered_first[:, 1, 0:1], 0, keepdims=True)


def twice(tile):
    return jnp.concatenate([tile, tile], 1)


def mask_row(J):
    return jnp.where((J < 0) | (J >= NJ), 2, jnp.where(J < SHORT_J, 0, 1))


def put_column(ring, slot, s, value, low, q_ref):
    rows = value.shape[0]
    ring[slot, s + 1] = low
    if s == 0:
        ring[slot, NI + 1, :, :128] = (pltpu.roll(value[:, :128], rows - 1, 0) * q_ref[0]).astype(
            bf16
        )
    if s == NI - 1:
        ring[slot, 0, :, 128:] = (pltpu.roll(value[:, 128:], 1, 0) * q_ref[1]).astype(bf16)


def side_columns(ring, side, u, lanes):
    for s in range(NI + 2):
        if s == 0:
            side[u, s, :, 128:] = jnp.where(
                lanes[:, 128:], ring[u + 2, s, :, 128:], ring[u, s, :, 128:]
            )
        elif s == NI + 1:
            side[u, s, :, :128] = jnp.where(
                lanes[:, :128], ring[u + 2, s, :, :128], ring[u, s, :, :128]
            )
        else:
            side[u, s] = jnp.where(lanes, ring[u + 2, s], ring[u, s])


def operands(ring, side, u):
    rows = ring.shape[2]
    whole_rows = NI * rows
    last = NI + 2
    own = ring[u + 1, 1 : NI + 1].reshape(whole_rows, LANES)
    beside = side[u, 1 : NI + 1].reshape(whole_rows, LANES)
    above = jnp.concatenate(
        [ring[u + 1, 2:last, :, :128], ring[u + 1, 0:NI, :, 128:]], -1
    ).reshape(whole_rows, LANES)
    corner = jnp.concatenate([side[u, 2:last, :, :128], side[u, 0:NI, :, 128:]], -1).reshape(
        whole_rows, LANES
    )
    return own, beside, above, corner


def product(parts, w_ref):
    total = jnp.dot(parts[0], w_ref[0:LANES], preferred_element_type=f32)
    for k in range(1, 4):
        total += jnp.dot(
            parts[k], w_ref[k * LANES : (k + 1) * LANES], preferred_element_type=f32
        )
    return total


def tree(values):
    values = list(values)
    while len(values) > 1:
        paired = [a + b for a, b in zip(values[::2], values[1::2])]
        values = paired + values[len(values) - len(values) % 2 :]
    return values[0]


def by_eight(value):
    return tree(value[k : k + 8] for k in range(0, value.shape[0], 8))


def summed(tiles):
    low = tree(tiles)
    low = tree(low[k : k + 16] for k in range(0, low.shape[0], 16))
    return by_eight(low.astype(f32))


def total_of(sums, which):
    return jnp.sum(tree(sums[which, u] for u in range(sums.shape[1])), 0, keepdims=True)


def pipeline(sets, activate, finish, matrix, lanes, before, after):
    def ready(block, own, other):
        ring, side, _ = own
        if other is None:
            ring[0] = jnp.zeros(ring.shape[1:], bf16)
            activate(0, ring, 1)
        else:
            ring[0] = other[0][BLOCK]
            ring[1] = other[0][BLOCK + 1]
        for u in range(BLOCK):
            activate(block * BLOCK + u + 1, ring, u + 2)
        for u in range(BLOCK):
            side_columns(ring, side, u, lanes)

    def multiply(own):
        ring, side, result = own
        parts = [operands(ring, side, u) for u in range(BLOCK)]
        result[...] = product(
            [jnp.concatenate([part[k] for part in parts], 0) for k in range(4)], matrix
        )

    def step(j, carry):
        for half in range(2):
            own, other = sets[half], sets[1 - half]
            block = 2 * j + half
            if half == 0:
                before(block)
            multiply(own)
            for u in range(BLOCK):
                finish((block - 1) * BLOCK + u, other, u)
            ready(block + 1, other, own)
            after(block)
        return carry

    sets[1][2][...] = jnp.zeros(sets[1][2].shape, f32)
    ready(0, sets[0], None)

    def tail():
        for u in range(BLOCK):
            finish(NJ - BLOCK + u, sets[1], u)

    return step, tail


def half_lanes(rows):
    return lax.broadcasted_iota(jnp.int32, (rows, LANES), 1) % 128 < 64


def pack_kernel(*refs):
    out_ref, held, sems = refs[4], refs[5:9], refs[9]
    copies = [pltpu.make_async_copy(refs[k], held[k], sems.at[k]) for k in range(4)]
    for copy in copies:
        copy.start()
    for copy in copies:
        copy.wait()
    stem_ref, conv_ref, norm_ref, head_ref = held
    width = stem_ref.shape[0]
    gains = [norm_ref[:, k, :].T for k in range(2)]
    head = head_ref[...]
    used = 27 + 14 + head.shape[1]
    small = jnp.concatenate(
        [stem_ref[...], *gains, head, jnp.zeros((width, 128 - used), f32)], 1
    )
    high = small.astype(bf16)
    rest = small - high.astype(f32)
    middle = rest.astype(bf16)
    low = (rest - middle.astype(f32)).astype(bf16)
    tail = jnp.concatenate([high, middle, low, jnp.zeros((width, 192), bf16)], 1)
    for w in range(out_ref.shape[0]):
        for layer in range(6):
            out_ref[w, layer] = conv_ref[layer].astype(bf16)
        out_ref[w, 6] = tail


def weights_kernel(packed_ref, *refs):
    outs, (held, sems) = refs[:12], refs[12:]
    copies = []
    for layer in range(6):
        matrix = jnp.concatenate(
            [packed_ref[w, layer].astype(f32) for w in range(packed_ref.shape[0])], 0
        )
        turned = matrix.T
        empty = jnp.zeros((64, 64), f32)
        for slot in range(16):
            ahead, back = [], []
            for out in range(4):
                tap = tap_of(slot, out)
                if tap is None:
                    ahead.append(empty)
                    back.append(empty)
                else:
                    other = 8 - tap
                    ahead.append(turned[tap * 64 : (tap + 1) * 64])
                    back.append(matrix[:, other * 64 : (other + 1) * 64])
            at = slice(slot * 64, (slot + 1) * 64)
            held[layer, at] = jnp.concatenate(ahead, 1).astype(bf16)
            held[6 + layer, at] = jnp.concatenate(back, 1).astype(bf16)
        for k in (layer, 6 + layer):
            copies.append(pltpu.make_async_copy(held.at[k], outs[k], sems.at[k]))
            copies[-1].start()
    for copy in copies:
        copy.wait()


def small_kernel(packed_ref, table_ref, norm_ref, into_ref, back_ref, stem_ref):
    count, _, width, _ = packed_ref.shape
    parts = [
        jnp.concatenate(
            [packed_ref[w, 6, :, k * 128 : (k + 1) * 128].astype(f32) for w in range(count)], 0
        )
        for k in range(3)
    ]
    turned = ((parts[0] + parts[1]) + parts[2]).T
    norms = turned[27:43]
    norm_ref[...] = jnp.concatenate([norms] * 4, 1)
    head = jnp.concatenate([turned[41:], jnp.zeros((41, 64), f32)], 0)
    back_ref[...] = jnp.concatenate([head] * 4, 1).astype(bf16)
    into_ref[...] = jnp.concatenate([head.T, jnp.zeros((64, 128), f32)], 0).astype(bf16)
    stem = turned[:32].astype(bf16)
    for k in range(table_ref.shape[0] // 2):
        pair = [
            jnp.dot(table_ref[2 * k + e], stem, preferred_element_type=f32) for e in range(2)
        ]
        stem_ref[:, k * 128 : (k + 1) * 128] = jnp.concatenate(pair, 1).astype(bf16)


def stem_kernel(
    planes_ref, w_ref, mask_ref, info_ref, save_ref, z_ref, stat_ref, zf, out_ref, sems, *, devices
):
    rows = planes_ref.shape[1]
    zf[...] = jnp.zeros_like(zf)
    span = 2 * NI
    blocks = SIDE // span
    deep = (span + 2) * 4
    for i in range(3):
        turned = planes_ref[i].astype(f32).T
        for block in range(blocks):
            first = max(block * span - 1, 0)
            last = min(block * span + span + 1, SIDE)
            skip = first - (block * span - 1)
            for y in range(span):
                base = (block * (span + 2) + y + 1) * deep + skip * 4 + i
                zf[pl.ds(base, last - first, stride=4), :rows] = turned[
                    y * SIDE + first : y * SIDE + last
                ]
    lane = lax.broadcasted_iota(jnp.int32, (deep, 128), 1)
    for block in range(blocks):
        at = block * (span + 2) * deep
        low = zf[at + span * deep : at + (span + 1) * deep]
        zf[at : at + deep] = jnp.where(lane % 4 == 0, 0.0, pltpu.roll(low, 1, 1))
        high = zf[at + deep : at + 2 * deep]
        zf[at + (span + 1) * deep : at + (span + 2) * deep] = jnp.where(
            lane % 4 == 3, 0.0, pltpu.roll(high, 127, 1)
        )
    z_ref[...] = zf[...].astype(bf16)
    first_sum = jnp.zeros((8, LANES), f32)
    second_sum = jnp.zeros((8, LANES), f32)
    copies = []
    for block in range(blocks):
        for s in range(NI):
            at = (block * (span + 2) + 2 * s) * deep
            result = lax.dot_general(
                z_ref[at : at + 4 * deep],
                w_ref[...],
                (((0,), (0,)), ((), ())),
                preferred_element_type=f32,
            )
            for j in range(NI):
                J = block * NI + j
                mask = mask_ref[0 if J < SHORT_J else 1, 0 if s == 0 else 1]
                tile = result[:rows, j * LANES : (j + 1) * LANES] * twice(mask)
                out_ref[s, J] = tile.astype(bf16)
                first_sum += by_eight(tile)
                second_sum += by_eight(tile * tile)
        at = pl.ds(block * NI, NI)
        copies.append(pltpu.make_async_copy(out_ref.at[:, at], save_ref.at[:, at], sems.at[block]))
        copies[-1].start()
    row = message(
        jnp.sum(first_sum, 0, keepdims=True), jnp.sum(second_sum, 0, keepdims=True)
    )
    counts = jnp.sum(info_ref[...], 0, keepdims=True) * (1.0 / QUARTERS)
    send(stat_ref, row, counts)
    for copy in copies:
        copy.wait()


def forward_kernel(*refs, index, keep, residual, streamed, devices):
    refs = list(refs)
    c_ref = refs.pop(0)
    if streamed:
        matrix_sem, matrix, load_sems, held = (refs.pop() for _ in range(4))
        loads = Streams([c_ref], [held], load_sems, 0)
        for i in range(CHUNKS):
            loads.start_load(i)
        c_ref = held
    res_ref = refs.pop(0) if residual else None
    gath_ref, first_ref, norm_ref, mask_ref, q_ref, w_ref, out_ref, save_ref = refs[:8]
    refs = refs[8:]
    keep_ref = refs.pop(0) if keep else None
    keep_save_ref = refs.pop(0) if keep else None
    stat_ref, sums, sems = refs[:3]
    if streamed:
        fetch = pltpu.make_async_copy(w_ref, matrix, matrix_sem)
        fetch.start()
        w_ref = matrix
    sets = refs[3:6], refs[6:9]
    rows = c_ref.shape[2]
    counted = pixels_of(first_ref)
    _, _, slope, start = norm_constants(gath_ref, counted, norm_ref, index)
    half_slope, half_start = slope * 0.5, start * 0.5
    lanes = half_lanes(rows)
    sums[...] = jnp.zeros_like(sums)

    def activate(J, ring, slot):
        Jc = jnp.minimum(J, NJ - 1)
        jm = mask_row(J)
        for s in range(NI):
            half = c_ref[s, Jc].astype(f32) * half_slope + half_start
            if residual:
                half = half + 0.5 * res_ref[s, Jc].astype(f32)
            mask = mask_ref[jm, 0 if s == 0 else 1]
            value = (half + half * jnp.tanh(half)) * twice(mask)
            low = value.astype(bf16)
            put_column(ring, slot, s, value, low, q_ref)

    def finish(J, own, u):
        Jc = jnp.maximum(J, 0)
        jm = mask_row(J)
        tiles = []
        for s in range(NI):
            tile = own[2][(u * NI + s) * rows : (u * NI + s + 1) * rows]
            low = (tile * twice(mask_ref[jm, 0 if s == 0 else 1])).astype(bf16)
            out_ref[s, Jc] = low
            if keep:
                keep_ref[s, Jc] = own[0][u + 1, s + 1]
            tiles.append(low)
        sums[0, u] += summed(tiles)
        sums[1, u] += summed([tile * tile for tile in tiles])

    def before(block):
        if streamed:
            loads.when(block + 2 < CHUNKS, loads.wait_loads, block + 2)

    def after(block):
        saves.when(block > 0, saves.start_save, block - 1)

    saves = Streams([save_ref, keep_save_ref][: 1 + keep], [out_ref, keep_ref][: 1 + keep], sems, 0)
    if keep:
        sets[1][0][...] = jnp.zeros(sets[1][0].shape, bf16)
    if streamed:
        loads.wait_load(0)
        loads.wait_load(1)
    step, tail = pipeline(sets, activate, finish, w_ref, lanes, before, after)
    if streamed:
        fetch.wait()
    lax.fori_loop(0, CHUNKS // 2, step, 0)
    tail()
    saves.start_save(CHUNKS - 1)
    row = message(total_of(sums, 0), total_of(sums, 1))
    send(stat_ref, row)
    for i in range(CHUNKS):
        saves.wait_save(i)


def head_kernel(
    c_ref, res_ref, gath_ref, first_ref, norm_ref, mask_ref, hot_ref, info_ref, into_ref, back_ref,
    bias_ref, dy_ref, stat_ref, head_ref, grads, pool, *, classes, devices
):
    rows = c_ref.shape[2]
    counted = pixels_of(first_ref)
    weight_total = jnp.sum(first_ref[:, 1, 1:2], 0, keepdims=True)
    mean, scale, slope, start = norm_constants(gath_ref, counted, norm_ref, 6)
    half_slope, half_start = slope * 0.5, start * 0.5
    pool[...] = jnp.zeros_like(pool)

    def gather(i, carry):
        values = []
        for u in range(UNROLL):
            J = i * UNROLL + u
            jm = mask_row(J)
            for s in range(NI):
                half = c_ref[s, J].astype(f32) * half_slope + half_start
                half = half + 0.5 * res_ref[s, J].astype(f32)
                sigma = (0.5 + 0.5 * jnp.tanh(half)) * twice(mask_ref[jm, 0 if s == 0 else 1])
                value = (half + half) * sigma
                values.append(value)
                grads[s, J] = (sigma + value - value * sigma).astype(bf16)
        pool[...] += tree(values)
        return carry

    lax.fori_loop(0, GROUPS, gather, 0)
    pooled = pool[...]
    row_index = lax.broadcasted_iota(jnp.int32, (rows, LANES), 0)
    pooled = pooled + jnp.where(
        row_index % 2 == 0, pltpu.roll(pooled, rows - 1, 0), pltpu.roll(pooled, 1, 0)
    )
    pooled = pooled + jnp.where(
        row_index % 4 < 2, pltpu.roll(pooled, rows - 2, 0), pltpu.roll(pooled, 2, 0)
    )
    half_pool = pooled[:, :128] + pooled[:, 128:]
    half_pool = half_pool + pltpu.roll(half_pool, 64, 1)
    count = info_ref[:, 0:1]
    weight = info_ref[:, 1:2]
    pooled_low = (half_pool / count).astype(bf16)
    logits = jnp.dot(pooled_low, into_ref[...], preferred_element_type=f32) + bias_ref[...]
    lane = lax.broadcasted_iota(jnp.int32, logits.shape, 1)
    inside = lane < classes
    top = jnp.max(jnp.where(inside, logits, -jnp.inf), 1, keepdims=True)
    shifted = jnp.where(inside, logits - top, 0.0)
    powers = jnp.where(inside, jnp.exp(shifted), 0.0)
    sum_powers = jnp.sum(powers, 1, keepdims=True)
    hot = hot_ref[...]
    losses = jnp.log(sum_powers) - jnp.sum(hot * shifted, 1, keepdims=True)
    single = (lax.broadcasted_iota(jnp.int32, (rows, 1), 0) % QUARTERS == 0).astype(f32)
    loss = jnp.sum(losses * weight * single, 0, keepdims=True)
    grad_low = ((weight / weight_total) * (powers / sum_powers - hot)).astype(bf16)
    grad_once = grad_low * single.astype(bf16)
    bias_grad = jnp.sum(grad_once.astype(f32), 0, keepdims=True)
    head_ref[...] = lax.dot_general(
        grad_once, pooled_low, (((0,), (0,)), ((), ())), preferred_element_type=f32
    )
    extra = jnp.where(lax.broadcasted_iota(jnp.int32, (1, 128), 1) == 127, loss, bias_grad)
    spread = jnp.dot(grad_low, back_ref[...], preferred_element_type=f32) / count

    def scatter(i, carry):
        first_sum, second_sum = carry
        tiles, others = [], []
        for u in range(UNROLL):
            J = i * UNROLL + u
            for s in range(NI):
                low = (spread * grads[s, J].astype(f32)).astype(bf16)
                dy_ref[s, J] = low
                tiles.append(low)
                others.append(low * c_ref[s, J])
        first_sum += tree(summed(tiles[k : k + NI]) for k in range(0, len(tiles), NI))
        second_sum += tree(summed(others[k : k + NI]) for k in range(0, len(others), NI))
        return first_sum, second_sum

    zero = jnp.zeros((8, LANES), f32)
    first_sum, second_sum = lax.fori_loop(0, NJ // UNROLL, scatter, (zero, zero))
    first_sum = jnp.sum(first_sum, 0, keepdims=True)
    second_sum = (jnp.sum(second_sum, 0, keepdims=True) - mean * first_sum) * scale
    send(stat_ref, message(first_sum, second_sum), extra)


def pieces_of(row):
    high = row.astype(bf16).astype(f32)
    middle = (row - high).astype(bf16).astype(f32)
    low = row - high - middle
    return [part[:, at : at + 64] for part in (high, middle, low) for at in (0, 64)]


def carried_lanes(width):
    return 576 + 64 * (-(-6 // width))


def carry(ref, weights, row, narrow):
    width = ref.shape[1]
    pieces = pieces_of(row)
    pieces += [jnp.zeros((1, 64), f32)] * (-len(pieces) % width)
    tail = [
        jnp.concatenate(pieces[at : at + width], 0) for at in range(0, len(pieces), width)
    ]
    for j in range(ref.shape[0] // narrow):
        rows = weights[j * width : (j + 1) * width]
        block = jnp.concatenate([rows, *tail], 1).astype(bf16)
        for n in range(narrow):
            ref[j * narrow + n] = block


def carried_totals(ref):
    width = ref.shape[1]
    total = tree(ref[d][:, 576:].astype(f32) for d in range(ref.shape[0]))
    found = [
        total[k % width : k % width + 1, 64 * (k // width) : 64 * (k // width) + 64]
        for k in range(6)
    ]
    halves = [found[k] + found[k + 2] + found[k + 4] for k in range(2)]
    return tuple(jnp.concatenate([half] * 4, 1) for half in halves)


def grad_constants(sums_ref, gath_ref, counted, norm4, index):
    first_total, second_total = sums_ref if isinstance(sums_ref, tuple) else totals(sums_ref)
    mean, scale, slope, _ = norm_constants(gath_ref, counted, norm4, index)
    along = -slope * scale * second_total / counted
    return slope, along, -slope * first_total / counted - along * mean


def backward_kernel(*refs, index, residual, adding, ordered, carrying, valued, kept, streamed, devices):
    inputs = 3 + residual + adding
    far_in, refs = refs[:inputs], refs[inputs:]
    refs = refs[:8] + refs[8 + ordered :]
    if carrying:
        weights_ref, carried_ref = refs[8], refs[12]
        refs = refs[:8] + refs[9:12] + refs[13:]
    if not valued:
        refs = refs[:10] + (None,) + refs[10:]
    if kept:
        refs += refs[8:11]
    (
        sums_ref, gath_ref, gath_prev_ref, first_ref, norm_ref, mask_ref, q_ref, w_ref,
        out_far, grad_far, value_far, stat_ref, ring, side, offsets, sums, sems, matrix,
        matrix_sem, out_ref, grad_ref, value_ref,
    ) = refs[:22]
    held = list(refs[22:] if streamed else far_in)
    loads = Streams(far_in[:2], held[:2], sems, 3, UNROLL)
    later = Streams(far_in[2:], held[2:], sems, 5, UNROLL)
    results = [(out_far, out_ref), (grad_far, grad_ref), (value_far, value_ref)][: 2 + valued]
    saves = None if kept else Streams(*zip(*results), sems, 0, UNROLL)
    fetch = pltpu.make_async_copy(w_ref, matrix, matrix_sem)
    if streamed:
        loads.start_load(0)
    fetch.start()
    for i in range(GROUPS if streamed else 0):
        if i + 1 < GROUPS:
            loads.start_load(i + 1)
        later.start_load(i)
    dy_ref = held.pop(0)
    c_ref, prev_ref = held[:2]
    res_ref = held[2] if residual else None
    add_ref = held[-1] if adding else None
    rows = c_ref.shape[2]
    counted = pixels_of(first_ref)
    grad_slope, grad_along, grad_start = grad_constants(
        sums_ref, gath_ref, counted, norm_ref, index
    )
    mean, scale, slope, start = norm_constants(gath_prev_ref, counted, norm_ref, index - 1)
    half_slope, half_start = slope * 0.5, start * 0.5
    lanes = half_lanes(rows)
    sums[...] = jnp.zeros_like(sums)
    for a in range(3):
        for b in range(2):
            offsets[a, b] = grad_start * twice(mask_ref[a, b])

    def activate(J, slot):
        Jc = jnp.minimum(J, NJ - 1)
        jm = mask_row(J)
        slope_now, along_now = grad_slope, grad_along
        if slot > UNROLL:
            present = jnp.where(J < NJ, 1.0, 0.0)
            slope_now, along_now = grad_slope * present, grad_along * present
        for s in range(NI):
            grad = dy_ref[s, Jc].astype(f32) * slope_now + (
                c_ref[s, Jc].astype(f32) * along_now + offsets[jm, 0 if s == 0 else 1]
            )
            put_column(ring, slot, s, grad, grad.astype(bf16), q_ref)

    def multiply():
        for u in range(UNROLL):
            side_columns(ring, side, u, lanes)
        parts = [operands(ring, side, u) for u in range(UNROLL)]
        return product(
            [jnp.concatenate([part[k] for part in parts], 0) for k in range(4)], matrix
        )

    def convolve(J, u, everything):
        total = everything[u * NI * rows : (u + 1) * NI * rows]
        jm = mask_row(J)
        tiles, others = [], []
        for s in range(NI):
            grad_ref[s, J] = ring[u + 1, s + 1]
            half = prev_ref[s, J].astype(f32) * half_slope + half_start
            if residual:
                half = half + 0.5 * res_ref[s, J].astype(f32)
            sigma = (0.5 + 0.5 * jnp.tanh(half)) * twice(mask_ref[jm, 0 if s == 0 else 1])
            value = (half + half) * sigma
            if valued:
                value_ref[s, J] = value.astype(bf16)
            tile = total[s * rows : (s + 1) * rows]
            if adding:
                tile = tile + add_ref[s, J].astype(f32)
            tile = tile * (sigma + value - value * sigma)
            low = tile.astype(bf16)
            out_ref[s, J] = low
            tiles.append(low)
            others.append(low * prev_ref[s, J])
        sums[0, u] += summed(tiles)
        sums[1, u] += summed(others)

    ring[UNROLL] = jnp.zeros(ring.shape[1:], bf16)
    if streamed:
        loads.wait_load(0)
    activate(0, UNROLL + 1)
    fetch.wait()

    def step(i, carry):
        if streamed:
            loads.when(i + 1 < GROUPS, loads.wait_load, i + 1)
            later.wait_load(i)

        for k in range(2):
            ring[k] = ring[UNROLL + k]
        for u in range(UNROLL):
            activate(i * UNROLL + u + 1, u + 2)
        everything = multiply()
        for u in range(UNROLL):
            convolve(i * UNROLL + u, u, everything)
        if not kept:
            saves.start_save(i)
        return carry

    lax.fori_loop(0, GROUPS, step, 0)
    first_sum = total_of(sums, 0)
    second_sum = (total_of(sums, 1) - mean * first_sum) * scale
    row = message(first_sum, second_sum)
    send(stat_ref, row)
    if carrying:
        carry(carried_ref, weights_ref[...].astype(f32), row, carrying)
    for i in range(0 if kept else GROUPS):
        saves.wait_save(i)


def weight_grad_kernel(*refs, slot_out, continued, fetching, kept, passing):
    grad_far, value_far, q_ref = refs[:3]
    refs = refs[3 + kept + continued :]
    far, refs = refs[:fetching], refs[fetching:]
    out_ref, token_ref, refs = refs[0], refs[1], refs[2 + passing :]
    near, refs = refs[:fetching], refs[fetching:]
    token_ref[...] = jnp.zeros_like(token_ref)
    ring, side, acc, sems, piece_ref, piece_sem, fetch_sems = refs[:7]
    grad_in_ref, value_ref = (grad_far, value_far) if kept else refs[7:]
    fetches = Streams(far, near, fetch_sems, 0, UNROLL)
    loads = Streams([grad_far, value_far], [grad_in_ref, value_ref], sems, 0)
    for i in range(0 if kept else CHUNKS):
        loads.start_load(i)
    rows = value_ref.shape[2]
    lanes = half_lanes(rows)

    def load(J, slot):
        Jc = jnp.minimum(J, NJ - 1)
        some = jnp.where(J < NJ, 1.0, 0.0)
        for s in range(NI):
            low = value_ref[s, Jc]
            if slot == UNROLL + 1:
                low = low * some.astype(bf16)
            put_column(ring, slot, s, low.astype(f32), low, q_ref)

    ring[UNROLL] = jnp.zeros(ring.shape[1:], bf16)
    if not kept:
        loads.wait_load(0)
    load(0, UNROLL + 1)

    def step(i, carry):
        fetches.start_load(i)
        if not kept:
            loads.wait_load(2 * i + 1)
            loads.when(2 * i + 2 < CHUNKS, loads.wait_load, 2 * i + 2)
        for k in range(2):
            ring[k] = ring[UNROLL + k]
        for u in range(UNROLL):
            load(i * UNROLL + u + 1, u + 2)
        for u in range(UNROLL):
            side_columns(ring, side, u, lanes)
        grad = jnp.concatenate(
            [grad_in_ref[:, i * UNROLL + u] for u in range(UNROLL)], 0
        ).reshape(UNROLL * NI * rows, LANES)
        parts = [operands(ring, side, u) for u in range(UNROLL)]
        for k in range(4):
            value = jnp.concatenate([parts[u][k] for u in range(UNROLL)], 0)
            piece = lax.dot_general(
                grad, value, (((0,), (0,)), ((), ())), preferred_element_type=f32
            )
            at = slice(k * LANES, (k + 1) * LANES)
            acc[:, at] = jnp.where(i == 0, piece, acc[:, at] + piece)
        return carry

    lax.fori_loop(0, GROUPS, step, 0)
    taps = [None] * 9
    for slot in range(16):
        for out in range(4):
            tap = tap_of(slot, out)
            if tap is not None:
                piece = acc[out * 64 : (out + 1) * 64, slot * 64 : (slot + 1) * 64]
                taps[tap] = piece if taps[tap] is None else taps[tap] + piece
    for i in range(GROUPS):
        fetches.wait_load(i)
    result = jnp.concatenate(taps, 1)
    if slot_out is None:
        out_ref[...] = result.astype(bf16)
    else:
        width = piece_ref.shape[1]
        for j in range(piece_ref.shape[0]):
            piece_ref[j] = result[j * width : (j + 1) * width].astype(bf16)
        copy = pltpu.make_async_copy(piece_ref, out_ref.at[:, slot_out], piece_sem)
        copy.start()
        copy.wait()


def stem_back_kernel(
    dy_far, c_far, z_ref, sums_ref, gath_ref, norm_ref, mask_ref, table_ref, conv_ref, head_ref,
    *refs
):
    stat_refs, (out_ref, dy_ref, held, raw, sems) = refs[:7], refs[7:]
    loads = Streams([dy_far, c_far], [dy_ref, held], sems, 0, NI)
    for k in range(NJ // NI):
        loads.start_load(k)
    rows = held.shape[2]
    counted = pixels_of(gath_ref)
    slope, along, start = grad_constants(
        carried_totals(sums_ref), gath_ref, counted, norm_ref, 0
    )
    span = 2 * NI
    deep = (span + 2) * 4
    for block in range(NJ // NI):
        loads.wait_load(block)
        for j in range(NI):
            J = block * NI + j
            total = None
            for s in range(NI):
                at = (block * (span + 2) + 2 * s) * deep
                mask = twice(mask_ref[0 if J < SHORT_J else 1, 0 if s == 0 else 1])
                grad = dy_ref[s, J].astype(f32) * slope + held[s, J].astype(f32) * along
                piece = jnp.dot(
                    z_ref[at : at + 4 * deep][:, :rows],
                    ((grad + start) * mask).astype(bf16),
                    preferred_element_type=f32,
                )
                total = piece if total is None else total + piece
            at = slice(j * LANES, (j + 1) * LANES)
            raw[:, at] = total if block == 0 else raw[:, at] + total
    parts = [raw[:, k * 64 : (k + 1) * 64].astype(bf16) for k in range(NI * 4)]
    total = lax.dot_general(
        jnp.concatenate(parts, 0),
        table_ref[...].reshape(NI * 4 * 4 * deep, 32),
        (((0,), (0,)), ((), ())),
        preferred_element_type=f32,
    )
    stats = jnp.concatenate([ref[0:1] if len(ref.shape) == 2 else ref[0, 0:1] for ref in stat_refs], 0)
    shifts, gains = stats[:, :64], stats[:, 64:]
    norms = jnp.concatenate([gains, shifts, jnp.zeros((2, 64), f32)], 0).T
    head = head_ref[:, :64].T
    extra = jnp.concatenate([total[:, :27], norms[:, :14], head[:, :23]], 1)
    out_ref[...] = jnp.concatenate([conv_ref[...].astype(f32), extra], 1).astype(bf16)


def chain_kernel(
    early_ref, late_ref, last_ref, noise_ref, conv_ref, stem_ref, head_ref, conv_out, extra_out,
    square_ref, *, devices
):
    count, width = early_ref.shape[0], early_ref.shape[2]
    narrow = devices // count
    member = lax.axis_index("wide")

    def partial(w):
        last = tree(last_ref[w * narrow + n].astype(f32) for n in range(narrow))
        late = tree(late_ref[w * narrow + n][:, :576].astype(f32) for n in range(narrow))
        return (
            [last[:, :576], late] + [early_ref[w, k].astype(f32) for k in range(4)],
            last[:, 576:],
        )

    def place(k):
        return lax.rem(member + k, count)

    def hop(k, carried):
        conv, extra = carried
        top = jnp.max(jnp.abs(extra), keepdims=True)
        for piece in conv:
            top = jnp.maximum(top, jnp.max(jnp.abs(piece), keepdims=True))
        scale = top + 1e-06
        sender = place(k)
        more, more_extra = partial(place(k + 1))

        def passed(value, dither, added):
            level = (value / scale * levels + dither.astype(f32)).astype(bf16)
            return level.astype(f32) * scale / levels + added

        conv = [passed(conv[m], noise_ref[sender, m], more[m]) for m in range(6)]
        dither = noise_ref[sender, 6][:, :64]
        known = lax.broadcasted_iota(jnp.int32, extra.shape, 1) < 41 + head_ref.shape[1]
        return conv, jnp.where(known, passed(extra, dither, more_extra), 0.0)

    conv, extra = lax.fori_loop(1, count, hop, partial(place(1)))
    head = head_ref[...]
    masters = jnp.concatenate(
        [
            stem_ref[...], jnp.zeros((width, 14), f32), head,
            jnp.zeros((width, 64 - 41 - head.shape[1]), f32),
        ],
        1,
    )
    extra = extra + weight_decay * masters
    total = jnp.sum(extra * extra, keepdims=True)
    for m in range(6):
        value = conv[m] + weight_decay * conv_ref[m]
        conv_out[m] = value
        total = total + jnp.sum(value * value, keepdims=True)
    extra_out[...] = jnp.concatenate([extra, extra], 1)
    square_ref[...] = jnp.broadcast_to(total, square_ref.shape)


def adam_kernel(square_ref, heads_ref, first_ref, conv_ref, extra_ref, *refs, classes):
    news, held, sems = refs[15:33], refs[33:48], refs[48]
    copies = [pltpu.make_async_copy(refs[k], held[k], sems.at[k]) for k in range(15)]
    for copy in copies:
        copy.start()
    olds = held
    bias = jnp.sum(heads_ref[:, 1, :], 0, keepdims=True)
    loss = bias[:, 127:128]
    bias = bias[:, :classes]
    total = jnp.sum(square_ref[...][:, 0:1], 0, keepdims=True)
    total = total + jnp.sum(bias * bias, keepdims=True)
    norm = jnp.sqrt(total)
    factor = clip_limit / jnp.maximum(norm, clip_limit)
    extra = extra_ref[...]
    turned = extra.T
    parts = (
        (extra[:, :27],), tuple(conv_ref[m] for m in range(6)),
        (turned[27:34], turned[34:41]), (extra[:, 41 : 41 + classes],), (bias,),
    )
    for copy in copies:
        copy.wait()
    for k, pieces in enumerate(parts):
        master, first, second = olds[3 * k : 3 * k + 3]
        for m, gradient in enumerate(pieces):
            at = {6: (m,), 2: (slice(None), m)}.get(len(pieces), ())
            results = adam_update(gradient, first[at], second[at], master[at], factor)
            for ref, value in zip(news[3 * k : 3 * k + 3], results):
                ref[at] = value
    news[15][...] = norm
    news[16][...] = loss
    news[17][...] = jnp.sum(first_ref[:, 1, 1:2], 0, keepdims=True)


def stem_table():
    span = 2 * NI + 2
    table = np.zeros((NI * 4, 4, span, 4, 27), np.float32)
    for j in range(NI):
        for out in range(4):
            for ky in range(3):
                for kx in range(3):
                    for i in range(3):
                        table[
                            j * 4 + out, out // 2 + ky, 2 * j + out % 2 + kx, i,
                            (ky * 3 + kx) * 3 + i,
                        ] = 1.0
    return np.pad(table.reshape(NI * 4, 4 * span * 4, 27), ((0, 0), (0, 0), (0, 5)))


def adam_update(gradient, first, second, master, factor):
    clipped = gradient * factor
    new_first = first_decay * first + (1.0 - first_decay) * clipped
    new_second = second_decay * second + (1.0 - second_decay) * clipped * clipped
    corrected = (
        new_first
        / (1.0 - first_decay**STEP)
        / (jnp.sqrt(new_second / (1.0 - second_decay**STEP)) + adam_epsilon)
    )
    return (master - learn_rate * (corrected + decoupled * master), new_first, new_second)


def shared(rows):
    return lax.all_to_all(rows, BOTH, 0, 0, tiled=True)


def body(
    images,
    large_flag,
    labels,
    example_weights,
    cycle_noise,
    stem_weight,
    conv_weight,
    norm_params,
    head_weight,
    head_bias,
    stem_first,
    stem_second,
    conv_first,
    conv_second,
    norm_first,
    norm_second,
    head_first,
    head_second,
    bias_first,
    bias_second,
):
    wide_count = lax.axis_size("wide")
    devices = wide_count * lax.axis_size("narrow")
    count = large_flag.shape[0]
    rows = QUARTERS * count
    width = stem_weight.shape[0]
    channels = width * wide_count
    classes = head_weight.shape[0]
    assert channels == 64 and rows % 16 == 0 and rows <= 128

    member = lax.axis_index("wide")

    def to_wide(value):
        return lax.all_to_all(value, "wide", 0, 0, tiled=True)

    owned = (stem_weight, conv_weight, norm_params.transpose(1, 0, 2), head_weight.T)
    packed = call(
        pack_kernel,
        (jax.ShapeDtypeStruct((wide_count, 7, width, 576), bf16),),
        [pltpu.VMEM(value.shape, f32) for value in owned] + [pltpu.SemaphoreType.DMA((4,))],
        owned,
        "pack",
        stored=(0, 1, 2, 3),
        limit=8,
    )[0]
    packed = to_wide(packed)
    bias_row = jnp.pad(head_bias[None, :], ((0, 0), (0, 128 - classes)))

    dither = ((cycle_noise[0].astype(f32) + 0.5) / 65536.0 - 0.5).astype(bf16)
    hop_row = (member - 1 - jnp.arange(wide_count, dtype=jnp.int32)) % wide_count
    dither = jnp.take(dither, jnp.minimum(hop_row, wide_count - 2), axis=0)
    one, two, three = width * 27, width * 27 + 6 * width * 576, width * 41 + 6 * width * 576
    extra = jnp.concatenate(
        [
            dither[:, :one].reshape(wide_count, width, 27),
            dither[:, two:three].reshape(wide_count, 14, width).transpose(0, 2, 1),
            dither[:, three:].reshape(wide_count, classes, width).transpose(0, 2, 1),
        ],
        2,
    )
    extra = jnp.pad(extra, ((0, 0), (0, 0), (0, 576 - extra.shape[2])))
    dither = jnp.concatenate(
        [dither[:, one:two].reshape(wide_count, 6, width, 576), extra[:, None]], 1
    )

    large = large_flag == 1
    row_large = jnp.repeat(large, QUARTERS)
    quarter = jnp.arange(rows, dtype=jnp.int32) % QUARTERS
    upper = row_large | (quarter < SHORT_J // NI)
    ones = jnp.ones((rows,), bool)
    none = jnp.zeros((rows,), bool)
    mask_table = jnp.stack(
        [jnp.stack([ones, upper]), jnp.stack([row_large, row_large]), jnp.stack([none, none])]
    )
    mask_table = jnp.broadcast_to(mask_table[..., None], (3, 2, rows, 128)).astype(f32)
    q_table = jnp.broadcast_to(
        jnp.stack([quarter != QUARTERS - 1, quarter != 0])[..., None], (2, rows, 128)
    ).astype(f32)
    sides = jnp.where(large, SIDE, SHORT).astype(jnp.int32)
    weights_f = example_weights.astype(f32)
    lane = jnp.arange(128, dtype=jnp.int32)[None, :]
    info = jnp.where(
        lane == 0,
        jnp.repeat((sides * sides).astype(f32), QUARTERS)[:, None],
        jnp.where(lane == 1, jnp.repeat(weights_f, QUARTERS)[:, None], 0.0),
    )
    hot = (jnp.repeat(labels, QUARTERS)[:, None] == lane).astype(f32)

    span = 2 * NI
    position = jnp.arange(span * SIDE, dtype=jnp.int32)
    inside = row_large[:, None] | (
        (quarter[:, None] * span + (position // SIDE)[None, :] < SHORT)
        & ((position % SIDE)[None, :] < SHORT)
    )
    planes = images.reshape(3, rows, span * SIDE) * inside.astype(bf16)[None]

    (planes, mask_table, q_table, info, hot, bias_row, dither, packed) = (
        lax.optimization_barrier(
            (planes, mask_table, q_table, info, hot, bias_row, dither, packed)
        )
    )
    dither = to_wide(dither)
    table = jnp.asarray(stem_table(), bf16)
    norm4, into_head, from_head, stem_wide = call(
        small_kernel,
        (
            jax.ShapeDtypeStruct((16, LANES), f32),
            jax.ShapeDtypeStruct((128, 128), bf16),
            jax.ShapeDtypeStruct((128, LANES), bf16),
            jax.ShapeDtypeStruct((table.shape[1], NI * LANES), bf16),
        ),
        [],
        (packed, table),
        "small",
        limit=12,
    )
    matrices = call(
        weights_kernel,
        (Stored((1024, LANES)),) * 12,
        [pltpu.VMEM((12, 1024, LANES), bf16), pltpu.SemaphoreType.DMA((12,))],
        (packed,),
        "weights",
        limit=16,
    )

    z_rows = (SIDE // span) * (span + 2) * (span + 2) * 4
    full = pltpu.VMEM((NI, NJ, rows, LANES), bf16)
    side_shape = (UNROLL, NI + 2, rows, LANES)
    sets = [
        pltpu.VMEM((BLOCK + 2, NI + 2, rows, LANES), bf16),
        pltpu.VMEM((BLOCK, NI + 2, rows, LANES), bf16),
        pltpu.VMEM((BLOCK * NI * rows, LANES), f32),
    ] * 2
    stat = jax.ShapeDtypeStruct((devices, 128), f32)

    c0_saved, z, stat0 = call(
        functools.partial(stem_kernel, devices=devices),
        (
            stored_field(rows),
            jax.ShapeDtypeStruct((z_rows, 128), bf16),
            jax.ShapeDtypeStruct((devices, 2, 128), f32),
        ),
        [pltpu.VMEM((z_rows, 128), f32), full, pltpu.SemaphoreType.DMA((SIDE // span,))],
        (planes, stem_wide, mask_table, info),
        "stem",
    )
    current, saved = c0_saved, [c0_saved]
    stat0, norm4, into_head, from_head, dither, *matrices = lax.optimization_barrier(
        (stat0, norm4, into_head, from_head, dither, *matrices)
    )
    gathered = [shared(stat0)]
    stream, streams = None, []
    ahead, back = matrices[:6], matrices[6:]
    for layer in range(1, 7):
        keep = layer % 2 == 1
        residual = keep and layer > 1
        args = (current,) + ((stream,) if residual else ())
        args += (gathered[layer - 1], gathered[0], norm4, mask_table, q_table, ahead[layer - 1])
        outs = call(
            functools.partial(
                forward_kernel, index=layer - 1, keep=keep, residual=residual,
                streamed=layer == 1, devices=devices,
            ),
            (field(rows), stored_field(rows)) * (2 if keep else 1) + (stat,),
            [
                pltpu.VMEM((2, BLOCK, 8, LANES), f32),
                pltpu.SemaphoreType.DMA((2, CHUNKS)),
            ]
            + sets
            + (
                [
                    full,
                    pltpu.SemaphoreType.DMA((1, CHUNKS)),
                    pltpu.VMEM((1024, LANES), bf16),
                    pltpu.SemaphoreType.DMA,
                ]
                if layer == 1
                else []
            ),
            args,
            "forward",
            cost=int(7e9),
            limit=24,
            stored=(0, len(args) - 1) if layer == 1 else (),
        )
        before, current = current, outs[0]
        saved.append(outs[1])
        if keep:
            stream = outs[2]
            streams.append(outs[3])
        gathered.append(shared(outs[-1]))

    dys = [None] * 7
    stats = [None] * 7
    dys[6], stats[6], head_grad = call(
        functools.partial(head_kernel, classes=classes, devices=devices),
        (
            field(rows),
            jax.ShapeDtypeStruct((devices, 2, 128), f32),
            jax.ShapeDtypeStruct((128, 128), f32),
        ),
        [
            full,
            pltpu.VMEM((rows, LANES), f32),
        ],
        (
            current, stream, gathered[6], gathered[0], norm4, mask_table, hot, info,
            into_head, from_head, bias_row,
        ),
        "head",
        cost=int(8e9),
        limit=28,
    )
    def needed(layer):
        fields = (dys[layer], saved[layer], saved[layer - 1])
        fields += (streams[layer // 2 - 1],) if layer in (5, 3) else ()
        return fields + ((dys[layer + 1],) if layer % 2 == 1 else ())

    fetched = (dys[6], current, before)
    tokens = ()
    narrow_count = devices // wide_count
    carried_shape = (devices, width, carried_lanes(width))
    for layer in range(6, 0, -1):
        residual = layer in (5, 3)
        adding = layer % 2 == 1
        if layer == 6:
            heads = sums = shared(stats[6])
        args = fetched
        inputs = len(args)
        args += (
            sums, gathered[layer], gathered[layer - 1], gathered[0], norm4, mask_table, q_table,
            back[layer - 1], *tokens, *((late,) if layer == 1 else ()),
        )
        kept, valued = int(layer > 2), int(layer > 1)
        outs = call(
            functools.partial(
                backward_kernel, index=layer, residual=residual, adding=adding,
                ordered=len(tokens), carrying=narrow_count if layer == 1 else 0,
                valued=valued, kept=kept, streamed=layer == 1,
                devices=devices,
            ),
            ((field(rows) if kept else stored_field(rows)),) * (2 + valued)
            + (stat,)
            + ((jax.ShapeDtypeStruct(carried_shape, bf16),) if layer == 1 else ()),
            [
                pltpu.VMEM((UNROLL + 2, NI + 2, rows, LANES), bf16),
                pltpu.VMEM(side_shape, bf16),
                pltpu.VMEM((3, 2, rows, LANES), f32),
                pltpu.VMEM((2, UNROLL, 8, LANES), f32),
                pltpu.SemaphoreType.DMA((8, GROUPS)),
                pltpu.VMEM((1024, LANES), bf16),
                pltpu.SemaphoreType.DMA,
            ]
            + ([] if kept else [full] * 3)
            + ([full] * inputs if layer == 1 else []),
            args,
            "backward",
            cost=int(8e9),
            limit=14 if kept else 46 if layer == 1 else 26,
            stored=(inputs + 7,) + (tuple(range(inputs)) if layer == 1 else ()),
        )
        dys[layer - 1], grad, stats[layer - 1] = outs[0], outs[1], outs[2 + valued]
        carried = outs[3:]
        value = outs[2] if valued else streams[(layer - 1) // 2]
        sums = shared(stats[layer - 1]) if layer > 1 else None
        slot_out = layer - 3 if layer > 2 else None
        shape = (wide_count, 4, width, 576)
        args = (grad, value, q_table) + ((sums,) if kept else ())
        outs = (jax.ShapeDtypeStruct((64, 576), bf16), jax.ShapeDtypeStruct((8, 128), f32))
        aliases = {}
        if 2 < layer < 6:
            aliases[len(args)] = 0
            args += (early,)
        if layer > 2:
            outs = (Stored(shape), outs[1])
        if layer == 2:
            aliases[len(args)] = 2
            args += (early,)
            outs += (Stored(shape),)
        continued = len(args) - 3 - kept
        wanted = needed(layer - 1)[1 : 4 if layer in (6, 4) else 3] if kept else ()
        args += wanted
        outs += (field(rows),) * len(wanted)
        result, token, *fetched = call(
            functools.partial(
                weight_grad_kernel, slot_out=slot_out, continued=continued,
                fetching=len(wanted), kept=kept, passing=int(layer == 2),
            ),
            outs,
            [
                pltpu.VMEM((UNROLL + 2, NI + 2, rows, LANES), bf16),
                pltpu.VMEM(side_shape, bf16),
                pltpu.VMEM((LANES, 1024), f32),
                pltpu.SemaphoreType.DMA((2, CHUNKS)),
                pltpu.VMEM((wide_count, width, 576), bf16),
                pltpu.SemaphoreType.DMA,
                pltpu.SemaphoreType.DMA((3, GROUPS)),
            ]
            + ([] if kept else [full, full]),
            args,
            "weight_grad",
            cost=int(7e9),
            limit=14 if kept else 24,
            stored=(() if kept else (0, 1)) + tuple(range(3 + kept, len(args))),
            aliases=aliases,
        )
        passed = fetched
        tokens = (token,)
        fetched = (dys[layer - 1],) + tuple(fetched) + ((dys[layer],) if layer in (6, 4, 2) else ())
        if layer == 2:
            fetched = needed(1)
        if layer > 2:
            early = result
        if layer == 2:
            early = lax.psum(passed[0], "narrow")
            late = result
    carried = shared(carried[0])
    early = to_wide(early)
    last = call(
        stem_back_kernel,
        (jax.ShapeDtypeStruct((64, 640), bf16),),
        [
            full,
            full,
            pltpu.VMEM((4 * (span + 2) * 4, NI * LANES), f32),
            pltpu.SemaphoreType.DMA((2, NJ // NI)),
        ],
        (
            dys[0], saved[0], z, carried, gathered[0], norm4, mask_table, table,
            result, head_grad, *stats,
        ),
        "stem_back",
        stored=(0, 1),
        cost=int(5e9),
    )[0]
    last = jnp.broadcast_to(
        last.reshape(wide_count, 1, width, 640), (wide_count, narrow_count, width, 640)
    )
    last = shared(last.reshape(devices, width, 640))
    conv_total, extra_total, squares = call(
        functools.partial(chain_kernel, devices=devices),
        (
            jax.ShapeDtypeStruct((6, width, 576), f32),
            jax.ShapeDtypeStruct((width, 128), f32),
            jax.ShapeDtypeStruct((wide_count, 128), f32),
        ),
        [],
        (early, carried, last, dither, conv_weight, stem_weight, head_weight.T),
        "chain",
    )
    olds = (
        stem_weight, stem_first, stem_second, conv_weight, conv_first, conv_second,
        *(value.transpose(1, 0, 2) for value in (norm_params, norm_first, norm_second)),
        head_weight.T, head_first.T, head_second.T,
        head_bias[None], bias_first[None], bias_second[None],
    )
    single = jax.ShapeDtypeStruct((1, 1), f32)
    news = call(
        functools.partial(adam_kernel, classes=classes),
        tuple(Result(old.shape, f32) for old in olds) + (single,) * 3,
        [pltpu.VMEM(old.shape, f32) for old in olds] + [pltpu.SemaphoreType.DMA((15,))],
        (to_wide(squares), heads, gathered[0], conv_total, extra_total, *olds),
        "adam",
        stored=tuple(range(5, 20)),
        limit=12,
    )
    return (
        *news[:6],
        *(new.transpose(1, 0, 2) for new in news[6:9]),
        *(new.T for new in news[9:12]),
        *(new[0] for new in news[12:15]),
        *(new[0, 0] for new in news[15:]),
    )


def solution(mesh):
    split = P(BOTH)
    ins = (
        P(None, BOTH), split, split, split, P("wide", None, None),
        P("wide", None), P(None, "wide", None), P(None, None, "wide"), P(None, "wide"), P(),
        P("wide", None), P("wide", None), P(None, "wide", None), P(None, "wide", None),
        P(None, None, "wide"), P(None, None, "wide"), P(None, "wide"), P(None, "wide"), P(), P(),
    )
    outs = (
        (P("wide", None),) * 3
        + (P(None, "wide", None),) * 3
        + (P(None, None, "wide"),) * 3
        + (P(None, "wide"),) * 3
        + (P(),) * 6
    )
    return jax.shard_map(body, mesh=mesh, in_specs=ins, out_specs=outs, check_vma=False)
```
